256 devices in a mesh: blk: 64 (over z, y_hi, x), mp: 4 (over y_lo, core).
Axes of the slice: x: 4, y: 4 (y_hi: 2, y_lo: 2; y = y_hi * 2 + y_lo), z: 8, core: 2. Of those that a mesh axis runs over, the one named last changes fastest.
Arguments:
- struct_feats: bfloat16 [32768, 1024], P('blk', 'mp'), may hold values from -10 to 10
- seq_feats: bfloat16 [32768, 1280], P('blk', 'mp'), may hold values from -10 to 10
- struct_proj: bfloat16 [1024, 512], P('mp'), may hold values from -6 to 6
- seq_proj: bfloat16 [1280, 512], P('mp'), may hold values from -6 to 6
- cluster_ids: int32 [32768], P('blk'), may hold values from 0 to 8191
- hard_owner: int32 [32768, 16, 1], P('blk'), may hold values from 0 to 63; in each aligned block of 2048 rows (0 to 2047, 2048 to 4095, ..., all dimensions but the last counted through in order) at most 64 rows name the same one
- hard_local: int32 [32768, 16], P('blk'), may hold values from 0 to 511
- hard_valid: int32 [32768, 16], P(('blk', 'mp')), may hold values 0 or 1
Outputs:
- seq_loss: float32 [32768], P('blk')
- struct_loss: float32 [32768], P(('blk', 'mp'))
- hard_loss: float32 [32768], P(('blk', 'mp'))
The draws below stay inside these ranges and needn't reach their ends.
Inputs may be any that keep to these rules, and one draw needn't show every extreme that they name: `hard_owner`: among the 2048 entries of each aligned block of 128 rows, no group index is named more than 64 times, and in some block one is named exactly 64 times.
All inputs are finite; a program needn't handle non-finite values. No bound on the sum of `hard_valid` on one device may be relied on, other than what follows from the above.
Results may differ from the reference program's by a relative error of at most 0.0054.
Values may be sent and summed in bfloat16 or wider, within the bound.
No kernel may reach another device: no remote copies, remote signals or barrier semaphores. Data moves between devices by JAX's collectives and lax.ppermute only.
A program may use at most 64 MiB of HBM per device.

```python
import math
import jax
import jax.numpy as jnp
import numpy as np
from jax import lax

DS = 1024
DQ = 1280
E = 512
K = 16
TOK_DEV = 512
TOKENS = 32768
SHARE_ROWS = 128
CAP = 64
CLUSTERS = 8192
N_BLK = 64


def family_layout(key):
    members = 4
    layout_key = jax.random.fold_in(key, 101)
    local_order = jax.random.permutation(jax.random.fold_in(layout_key, 1), TOK_DEV).astype(jnp.int32)
    positions = jnp.arange(TOK_DEV, dtype=jnp.int32)
    inverse = jnp.zeros((TOK_DEV,), jnp.int32).at[local_order].set(positions)
    row_index = jnp.arange(TOKENS, dtype=jnp.int32)
    local_rank = local_order[row_index % TOK_DEV]
    family = local_rank // members
    group_index = row_index // TOK_DEV
    random_pick = jax.random.randint(jax.random.fold_in(layout_key, 2), (TOKENS,), 0, N_BLK, dtype=jnp.int32)
    within = jnp.where(local_rank % members == 0, group_index, random_pick)
    label_order = jax.random.permutation(jax.random.fold_in(layout_key, 3), CLUSTERS).astype(jnp.int32)
    labels = label_order[family * N_BLK + within]
    return (family, labels, inverse, members)


def shared_latent(key, family_share, label_share, row_share):
    family, labels, inverse, members = family_layout(key)
    latent_key = jax.random.fold_in(key, 202)
    family_table = jax.random.normal(jax.random.fold_in(latent_key, 1), (TOK_DEV // members, E), jnp.float32)
    label_table = jax.random.normal(jax.random.fold_in(latent_key, 2), (CLUSTERS, E), jnp.float32)
    row_part = jax.random.normal(jax.random.fold_in(latent_key, 3), (TOKENS, E), jnp.float32)
    return math.sqrt(family_share) * family_table[family] + math.sqrt(label_share) * label_table[labels] + math.sqrt(row_share) * row_part


def place_latent(latent, noise):
    front = latent + 0.5 * noise[:, :E]
    return jnp.clip(jnp.concatenate([front, noise[:, E:]], axis=1), -10.0, 10.0).astype(jnp.bfloat16)


def aligned_projection(own_key, rows):
    random_part = jax.random.normal(jax.random.fold_in(own_key, 1), (rows, E), jnp.float32) * rows ** (-0.5)
    diagonal = jax.random.uniform(jax.random.fold_in(own_key, 2), (E,), jnp.float32, 2.0, 4.0)
    on_diagonal = jnp.arange(rows, dtype=jnp.int32)[:, None] == jnp.arange(E, dtype=jnp.int32)[None, :]
    values = random_part + jnp.where(on_diagonal, diagonal[None, :], 0.0)
    return jnp.clip(values, -6.0, 6.0).astype(jnp.bfloat16)


def draw_struct_feats(key, part):
    own_key = jax.random.fold_in(key, 11)
    latent = shared_latent(key, 1.3, 0.45, 0.25)
    noise = jax.random.normal(own_key, (TOKENS, DS), jnp.float32)
    return place_latent(latent, noise)


def draw_seq_feats(key, part):
    own_key = jax.random.fold_in(key, 12)
    latent = shared_latent(key, 1.3, 0.45, 0.25)
    noise = jax.random.normal(own_key, (TOKENS, DQ), jnp.float32)
    return place_latent(latent, noise)


def draw_struct_proj(key, part):
    own_key = jax.random.fold_in(key, 13)
    return aligned_projection(own_key, DS)


def draw_seq_proj(key, part):
    own_key = jax.random.fold_in(key, 14)
    return aligned_projection(own_key, DQ)


def draw_cluster_ids(key, part):
    family, labels, inverse, members = family_layout(key)
    return labels.astype(jnp.int32)


def draw_hard_local(key, part):
    own_key = jax.random.fold_in(key, 16)
    family, labels, inverse, members = family_layout(key)
    offset = jax.random.randint(own_key, (TOKENS, 1), 0, members, dtype=jnp.int32)
    member_pick = (jnp.arange(K, dtype=jnp.int32)[None, :] + offset) % members
    return inverse[family[:, None] * members + member_pick].astype(jnp.int32)


def place_ends(entries, stream_key, smallest, high):
    dims = entries.shape
    spot = [jax.random.randint(jax.random.fold_in(stream_key, axis), (), 0, dims[axis]) for axis in range(len(dims))]
    entries = entries.at[tuple(spot)].set(smallest)
    longest = dims.index(max(dims))
    spot[longest] = (spot[longest] + 1) % dims[longest]
    return entries.at[tuple(spot)].set(high)


def shared_out(key, own, number, rows, count, top, bound, lean):
    ranking = jax.random.permutation(key, count)
    heavy_load, ordinary = shares(count, rows * top, bound, lean, True), shares(count, rows * top, bound, lean, False)
    places = jnp.arange(count)

    def named(sizes, offset_by):
        used = int((sizes > 0).sum())
        fixed = max(1, used // 4)
        shifted = fixed + (places - fixed + offset_by * (used - fixed)) % max(1, count - fixed)
        return jnp.zeros((count,), jnp.int32).at[ranking[jnp.where(places < fixed, places, shifted)]].set(jnp.asarray(sizes, jnp.int32))

    sizes = jnp.where(number % 4 == 0, named(heavy_load, number // 4), named(ordinary, number - number // 4 - 1))
    mixed = jax.random.permutation(jax.random.fold_in(own, 3), count)
    donor, receiver = mixed[0:count // 2 * 2:2], mixed[1:count // 2 * 2:2]
    room = jnp.minimum(sizes[donor] - 1, bound - sizes[receiver]) // 2
    room = jnp.where((donor == ranking[0]) | (receiver == ranking[0]) | (sizes[receiver] == 0), 0, jnp.maximum(room, 0))
    shifted = jax.random.randint(jax.random.fold_in(own, 4), (count // 2,), 0, 1 << 20) % (room + 1)
    sizes = sizes.at[donor].add(-shifted).at[receiver].add(shifted)
    items = jnp.searchsorted(jnp.cumsum(sizes), jnp.arange(rows * top), side="right").astype(jnp.int32)
    table = items.reshape(top, rows).T
    table = table[jax.random.permutation(jax.random.fold_in(own, 1), rows)]
    offset_by = jax.random.randint(jax.random.fold_in(own, 2), (rows, 1), 0, top)
    return jnp.take_along_axis(table, (jnp.arange(top)[None, :] + offset_by) % top, axis=1)


def shares(number_of, total, bound, lean, full):
    loads = [(1 << 20) // math.isqrt(grade ** lean) + 1 for grade in range(1, number_of + 1)]
    largest = bound if full else min(bound, max(-(-total // number_of), total * loads[0] // sum(loads)))
    least = 1 if total - largest >= number_of - 1 else 0
    holding, spare = [largest] + [least] * (number_of - 1), total - largest - least * (number_of - 1)
    while spare > 0:
        free = [i for i in range(1, number_of) if holding[i] < largest] or [i for i in range(1, number_of) if holding[i] < bound]
        pool, left = sum([loads[i] for i in free]), spare
        for i in free:
            more = min(bound - holding[i], max(1, left * loads[i] // pool), spare)
            holding[i] = holding[i] + more
            spare = spare - more
    return np.array(holding)


def setup_inputs(seed: int = 0) -> dict:
    streams_of = jax.random.split(jax.random.key(seed), 9)
    struct_feats = draw_struct_feats(jax.random.fold_in(streams_of[8], 71), 0)
    seq_feats = draw_seq_feats(jax.random.fold_in(streams_of[8], 71), 0)
    struct_proj = draw_struct_proj(jax.random.fold_in(streams_of[8], 71), 0)
    seq_proj = draw_seq_proj(jax.random.fold_in(streams_of[8], 71), 0)
    cluster_ids = draw_cluster_ids(jax.random.fold_in(streams_of[8], 71), 0)
    hard_owner_keys = jax.random.split(jax.random.fold_in(streams_of[5], 1), TOKENS * K // (SHARE_ROWS * K))
    hard_owner_turns = jax.random.permutation(jax.random.fold_in(streams_of[5], 3), TOKENS * K // (SHARE_ROWS * K))
    hard_owner = jax.vmap(lambda own, number: shared_out(jax.random.fold_in(streams_of[5], 2), own, number, SHARE_ROWS * K, N_BLK, 1, CAP, 2))(hard_owner_keys, hard_owner_turns).reshape((TOKENS, K, 1))
    hard_local = draw_hard_local(jax.random.fold_in(streams_of[8], 71), 0)
    hard_valid = place_ends((jax.random.randint(streams_of[7], (TOKENS, K), 0, 4) < 3).astype(jnp.int32), jax.random.fold_in(streams_of[7], 1), 0, 1)
    return {"struct_feats": struct_feats, "seq_feats": seq_feats, "struct_proj": struct_proj, "seq_proj": seq_proj, "cluster_ids": cluster_ids, "hard_owner": hard_owner, "hard_local": hard_local, "hard_valid": hard_valid}


LOGIT_SCALE = 14.285714285714286
EPSILON = 1e-06

def normalize(raw_values):
    total = lax.optimization_barrier(jnp.sum(raw_values * raw_values, axis=1, keepdims=True))
    return (raw_values * lax.rsqrt(total + EPSILON)).astype(jnp.bfloat16)

def reference(struct_feats, seq_feats, struct_proj, seq_proj, cluster_ids, hard_owner, hard_local, hard_valid):
    structs = normalize(jnp.dot(struct_feats, struct_proj, preferred_element_type=jnp.float32))
    queries = normalize(jnp.dot(seq_feats, seq_proj, preferred_element_type=jnp.float32))
    struct_full = structs.astype(jnp.float32)
    query_full = queries.astype(jnp.float32)
    query_blocks = query_full.reshape(N_BLK, TOK_DEV, E)
    cluster_blocks = cluster_ids.reshape(N_BLK, TOK_DEV)

    def cycle_step(carried, slices):
        col_total, col_matched = carried
        query_block, cluster_block = slices
        weights = jnp.exp(LOGIT_SCALE * jnp.dot(query_block, struct_full.T))
        matched = (cluster_block[:, None] == cluster_ids[None, :]).astype(jnp.float32)
        kept = weights * matched
        return ((col_total + lax.optimization_barrier(jnp.sum(weights, axis=0)), col_matched + lax.optimization_barrier(jnp.sum(kept, axis=0))), (lax.optimization_barrier(jnp.sum(weights, axis=1)), lax.optimization_barrier(jnp.sum(kept, axis=1))))
    zeros_cols = jnp.zeros((TOKENS,), jnp.float32)
    (col_total, col_matched), (row_total, row_matched) = lax.scan(cycle_step, (zeros_cols, zeros_cols), (query_blocks, cluster_blocks))
    seq_loss = jnp.log(row_total.reshape(-1)) - jnp.log(row_matched.reshape(-1))
    struct_loss = jnp.log(col_total) - jnp.log(col_matched)
    hard_rows = hard_owner[:, :, 0] * TOK_DEV + hard_local
    self_logits = LOGIT_SCALE * lax.optimization_barrier(jnp.sum(query_full * struct_full, axis=1))

    def hard_block(slices):
        query_block, rows_block, valid_block, self_block = slices
        fetched_rows = struct_full[rows_block]
        hard_logits = LOGIT_SCALE * jnp.einsum('ske,se->sk', fetched_rows, query_block)
        extra = lax.optimization_barrier(jnp.sum(valid_block.astype(jnp.float32) * jnp.exp(hard_logits), axis=1))
        return jnp.log(jnp.exp(self_block) + extra) - self_block
    hard_loss = lax.map(hard_block, (query_blocks, hard_rows.reshape(N_BLK, TOK_DEV, K), hard_valid.reshape(N_BLK, TOK_DEV, K), self_logits.reshape(N_BLK, TOK_DEV)))
    return (seq_loss, struct_loss, hard_loss.reshape(-1))
```

```python
import math

import jax
import jax.numpy as jnp
from jax import lax
from jax.experimental import pallas as pl
from jax.experimental.pallas import tpu as pltpu
from jax.sharding import Mesh, PartitionSpec as P

LOGIT_SCALE = 14.285714285714286
EPSILON = 1e-06
LOG2E = math.log2(math.e)

SHARE = 128
SIDE = 16
EDGE = SHARE * SIDE
WIDTH = 512
SLOTS = 16
EXT = 16
TILE = 512
STRIP = 256
SUB = 32

COL_AXES = ("yh", "x", "yl")
MP_AXES = ("yl", "core")
SIZES = {"z": 8, "yh": 2, "x": 4, "yl": 2, "core": 2}

VMEM = pl.BlockSpec(memory_space=pltpu.VMEM)
SMEM = pl.BlockSpec(memory_space=pltpu.SMEM)
ANY = pl.BlockSpec(memory_space=pl.ANY)


def shifted(value, axes, steps):
    names = (axes,) if isinstance(axes, str) else axes
    count = math.prod(SIZES[name] for name in names)
    return lax.ppermute(value, axes, [((place + steps) % count, place) for place in range(count)])


def project_kernel(core_ref, seq_hbm, struct_hbm, wq_hbm, ws_hbm, keep_ref, send_ref, seq_ref, struct_ref, wq_ref, ws_ref, sems):
    core = core_ref[0]
    copies = [
        pltpu.make_async_copy(source, target, sems.at[place])
        for place, (source, target) in enumerate(
            ((seq_hbm, seq_ref), (wq_hbm, wq_ref), (struct_hbm, struct_ref), (ws_hbm, ws_ref))
        )
    ]
    for copy in copies:
        copy.start()
    copies[0].wait()
    copies[1].wait()
    for half in range(2):
        for out, which in ((keep_ref, core), (send_ref, 1 - core)):
            rows = pl.ds(pl.multiple_of((half * 2 + which) * SHARE, SHARE), SHARE)
            out[half, :, 0:WIDTH] = lax.dot_general(
                seq_ref[:, rows], wq_ref[...], (((0,), (0,)), ((), ())), preferred_element_type=jnp.float32
            )
    copies[2].wait()
    copies[3].wait()
    for half in range(2):
        for out, which in ((keep_ref, core), (send_ref, 1 - core)):
            rows = pl.ds(pl.multiple_of((half * 2 + which) * SHARE, SHARE), SHARE)
            out[half, :, WIDTH:] = jnp.dot(struct_ref[rows, :], ws_ref[...], preferred_element_type=jnp.float32)


def project(core, seq_feats, struct_feats, seq_proj, struct_proj):
    shape = jax.ShapeDtypeStruct((2, SHARE, 2 * WIDTH), jnp.float32)
    held = (seq_feats, struct_feats, seq_proj, struct_proj)
    return pl.pallas_call(
        project_kernel,
        out_shape=(shape, shape),
        in_specs=[SMEM, ANY, ANY, ANY, ANY],
        out_specs=(VMEM, VMEM),
        scratch_shapes=[pltpu.VMEM(each.shape, each.dtype) for each in held] + [pltpu.SemaphoreType.DMA((4,))],
        compiler_params=pltpu.CompilerParams(vmem_limit_bytes=56 * 1024 * 1024),
        name="project",
    )(core, *held)


def merge_kernel(yl_ref, keep_ref, got_ref, keep2_ref, send2_ref):
    yl = yl_ref[0]
    keep2_ref[...] = keep_ref[yl] + got_ref[yl]
    send2_ref[...] = (keep_ref[1 - yl] + got_ref[1 - yl]).astype(jnp.bfloat16)


def merge(yl, keep, got):
    return pl.pallas_call(
        merge_kernel,
        out_shape=(
            jax.ShapeDtypeStruct((SHARE, 2 * WIDTH), jnp.float32),
            jax.ShapeDtypeStruct((SHARE, 2 * WIDTH), jnp.bfloat16),
        ),
        in_specs=[SMEM, VMEM, VMEM],
        out_specs=(VMEM, VMEM),
        compiler_params=pltpu.CompilerParams(vmem_limit_bytes=24 * 1024 * 1024),
        name="merge",
    )(yl, keep, got)


def lanes_summed(values):
    return lax.dot_general(
        jnp.ones((8, values.shape[1]), jnp.float32),
        values,
        (((1,), (1,)), ((), ())),
        precision=lax.Precision.HIGHEST,
        preferred_element_type=jnp.float32,
    )


def finish_kernel(keep2_ref, got2_ref, ext_ref, seq_ref, struct_ref, self_ref):
    def normalized(at):
        raw = keep2_ref[:, at] + got2_ref[:, at].astype(jnp.float32)
        total = jnp.sum(raw * raw, axis=1, keepdims=True)
        return (raw * lax.rsqrt(total + EPSILON)).astype(jnp.bfloat16)

    seq = normalized(slice(0, WIDTH))
    struct = normalized(slice(WIDTH, 2 * WIDTH))
    ext = ext_ref[...]
    seq_ref[0:SHARE, :] = seq
    seq_ref[SHARE:, :] = ext
    for peer in range(SIDE):
        struct_ref[peer, 0:SHARE, :] = struct
        struct_ref[peer, SHARE:, :] = ext
    self_ref[...] = lanes_summed(seq.astype(jnp.float32) * struct.astype(jnp.float32))


def finish(keep2, got2, ext):
    return pl.pallas_call(
        finish_kernel,
        out_shape=(
            jax.ShapeDtypeStruct((SHARE + EXT, WIDTH), jnp.bfloat16),
            jax.ShapeDtypeStruct((SIDE, SHARE + EXT, WIDTH), jnp.bfloat16),
            jax.ShapeDtypeStruct((8, SHARE), jnp.float32),
        ),
        in_specs=[VMEM] * 3,
        out_specs=(VMEM,) * 3,
        compiler_params=pltpu.CompilerParams(vmem_limit_bytes=24 * 1024 * 1024),
        name="finish",
    )(keep2, got2, ext)


def pair_kernel(place_ref, *refs):
    seq_refs, s, rows_ref, cols_ref = refs[0:SIDE], refs[SIDE], refs[SIDE + 1], refs[SIDE + 2]
    q, buf0, buf1, info, lab8, ct, cm, row_acc = refs[SIDE + 3 :]
    tiles = EDGE // TILE
    strips = EDGE // STRIP
    part = TILE // strips
    buffers = (buf0, buf1)
    my_z, my_core = place_ref[0], place_ref[1]
    my_block = my_z * 2 + my_core

    ct[...] = jnp.zeros_like(ct)
    cm[...] = jnp.zeros_like(cm)
    row_acc[...] = jnp.zeros_like(row_acc)
    lane_less_row = lax.broadcasted_iota(jnp.int32, (8, 128), 1) - lax.broadcasted_iota(jnp.int32, (8, 128), 0)

    def integers(values):
        return values.astype(jnp.float32).astype(jnp.int32)

    for chunk in range(SIDE):
        labels = integers(s[chunk, SHARE:, 2 * SHARE :])
        labels = labels[:, 0:SHARE] * 128 + labels[:, SHARE:]
        lab8[:, chunk * 128 : (chunk + 1) * 128] = labels[0:8]
    for block in range(SIDE):
        at = slice(block * SHARE, (block + 1) * SHARE)
        q[at, :] = seq_refs[block][0:SHARE, :]
        ext = integers(seq_refs[block][SHARE:, :])
        high, low = ext[:, 0:SHARE], ext[:, SHARE : 2 * SHARE]
        label = ext[:, 2 * SHARE : 3 * SHARE] * 128 + ext[:, 3 * SHARE :]
        code = jnp.where((high >> 4) == my_block, (high & 15) * 128 + low, -1)
        whole = jnp.concatenate(
            [code, -1 - label, jnp.full((128 - 2 * EXT, SHARE), -1, jnp.int32)], axis=0
        ).astype(jnp.float32)
        info[at, :] = whole.T.astype(jnp.int32)

    for tile in range(tiles + 1):

        def body(step, carry, tile=tile):
            if tile < tiles:
                cols = s[pl.ds(step * (STRIP // SHARE), STRIP // SHARE), 0:SHARE, :].reshape(STRIP, WIDTH)
                start = pl.multiple_of(step * STRIP, STRIP)
                buffers[tile % 2][:, pl.ds(start, STRIP)] = lax.dot_general(
                    q[tile * TILE : (tile + 1) * TILE, :],
                    cols,
                    (((1,), (1,)), ((), ())),
                    preferred_element_type=jnp.float32,
                )
            if tile > 0:
                logits = buffers[(tile - 1) % 2]
                block = (tile - 1) * (TILE // SHARE) + step // 2
                groups = range(SUB // 8)
                for sub in range(part // SUB):
                    local = [pl.multiple_of(step * part + sub * SUB + group * 8, 8) for group in groups]
                    code = [info[pl.ds(pl.multiple_of((tile - 1) * TILE + each, 8), 8), :] for each in local]
                    label = [jnp.broadcast_to(-1 - each[:, SLOTS : SLOTS + 1], (8, 128)) for each in code]
                    lane = [each & 127 for each in code]
                    chunk_of = [each >> 7 for each in code]
                    row_total = [jnp.zeros((8, 128), jnp.float32) for _ in groups]
                    row_matched = list(row_total)
                    picked = list(row_total)
                    for chunk in range(SIDE):
                        at = slice(chunk * 128, (chunk + 1) * 128)
                        col_label = lab8[:, at]
                        col_total, col_matched = ct[:, at], cm[:, at]
                        for group in groups:
                            expo = jnp.exp2(logits[pl.ds(local[group], 8), at] * (LOGIT_SCALE * LOG2E))
                            kept = jnp.where(label[group] == col_label, expo, 0.0)
                            row_total[group] += expo
                            row_matched[group] += kept
                            col_total += expo
                            col_matched += kept
                            found = jnp.take_along_axis(expo, lane[group], axis=1, mode="promise_in_bounds")
                            picked[group] = jnp.where(chunk_of[group] == chunk, found, picked[group])
                        ct[:, at] = col_total
                        cm[:, at] = col_matched
                    for which, each in enumerate((row_total, row_matched, picked)):
                        sums = row_acc[which, block]
                        for group in groups:
                            here = lane_less_row == (step % 2) * part + sub * SUB + group * 8
                            sums = jnp.where(here, jnp.sum(each[group], axis=1, keepdims=True), sums)
                        row_acc[which, block] = sums
            return carry

        lax.fori_loop(0, strips, body, 0)

    row_of = lax.broadcasted_iota(jnp.int32, (8, SHARE), 0)
    for far in range(8):
        out = jnp.zeros((8, SHARE), jnp.float32)
        for mate in range(2):
            for which in range(3):
                row = jnp.sum(row_acc[which, far * 2 + mate], axis=0, keepdims=True)
                out = jnp.where(row_of == (my_core ^ mate) * 3 + which, row, out)
        z = (my_z + far) & 7
        for peer in range(4):
            rows_ref[z * 4 + peer] = out
    for chunk in range(SIDE):
        at = slice(chunk * 128, (chunk + 1) * 128)
        total = jnp.sum(ct[:, at], axis=0, keepdims=True)
        matched = jnp.sum(cm[:, at], axis=0, keepdims=True)
        cols_ref[chunk] = jnp.where(row_of == 0, total, matched)


def pair_sums(place, seq_blocks, struct_blocks):
    return pl.pallas_call(
        pair_kernel,
        out_shape=(
            jax.ShapeDtypeStruct((32, 8, SHARE), jnp.float32),
            jax.ShapeDtypeStruct((SIDE, 8, SHARE), jnp.float32),
        ),
        in_specs=[SMEM] + [VMEM] * 17,
        out_specs=(VMEM, VMEM),
        scratch_shapes=[
            pltpu.VMEM((EDGE, WIDTH), jnp.bfloat16),
            pltpu.VMEM((TILE, EDGE), jnp.float32),
            pltpu.VMEM((TILE, EDGE), jnp.float32),
            pltpu.VMEM((EDGE, 128), jnp.int32),
            pltpu.VMEM((8, EDGE), jnp.int32),
            pltpu.VMEM((8, EDGE), jnp.float32),
            pltpu.VMEM((8, EDGE), jnp.float32),
            pltpu.VMEM((3, SIDE, 8, 128), jnp.float32),
        ],
        compiler_params=pltpu.CompilerParams(vmem_limit_bytes=28 * 1024 * 1024),
        cost_estimate=pl.CostEstimate(
            flops=2 * EDGE * EDGE * WIDTH, bytes_accessed=4 * EDGE * WIDTH, transcendentals=EDGE * EDGE
        ),
        name="pair_sums",
    )(place, *seq_blocks, struct_blocks)


def over_z(block):
    found = {0: block, 1: shifted(block, "z", 1), 7: shifted(block, "z", -1)}
    found[2], found[6] = shifted(found[1], "z", 1), shifted(found[7], "z", -1)
    found[3], found[5] = shifted(found[2], "z", 1), shifted(found[6], "z", -1)
    found[4] = shifted(found[3], "z", 1)
    return [found[place] for place in range(8)]


def per_device(struct_feats, seq_feats, struct_proj, seq_proj, cluster_ids, hard_owner, hard_local, hard_valid):
    place = lambda axes: lax.axis_index(axes).astype(jnp.int32)
    core, yl = place("core"), place("yl")
    keep, send = project(core.reshape(1), seq_feats.T, struct_feats, seq_proj, struct_proj)
    got = shifted(send, "core", 1)

    own = lambda value: lax.dynamic_slice_in_dim(value, place(MP_AXES) * SHARE, SHARE, 0)
    labels = own(cluster_ids)
    owner = own(hard_owner[:, :, 0])
    local = own(hard_local)
    block = (owner >> 3) * 2 + ((local >> 7) & 1)
    chunk = (owner & 7) * 2 + (local >> 8)
    high = jnp.where(hard_valid > 0, block * 16 + chunk, -1).T
    low = (local & 127).T
    wide = lambda value: jnp.broadcast_to(value[None], (EXT, SHARE))
    ext = jnp.concatenate([high, low, wide(labels >> 7), wide(labels & 127)], axis=1).astype(jnp.bfloat16)

    keep2, send2 = merge(yl.reshape(1), keep, got)
    got2 = shifted(send2, "yl", 1)
    seq_block, struct_block, self_dot = finish(keep2, got2, ext)

    struct_blocks = lax.all_to_all(struct_block, COL_AXES, split_axis=0, concat_axis=0, tiled=True)
    seq_blocks = [each for held in over_z(seq_block) for each in (held, shifted(held, "core", 1))]

    rows, cols = pair_sums(jnp.stack([place("z"), core]), seq_blocks, struct_blocks)
    rows = lax.all_to_all(rows, ("z",) + MP_AXES, split_axis=0, concat_axis=0, tiled=True)
    cols = jnp.sum(lax.all_to_all(cols, COL_AXES, split_axis=0, concat_axis=0, tiled=True), axis=0)
    rows = jnp.sum(rows.reshape(8, 2, 2, 8, SHARE), axis=(0, 2))[:, 0:6].reshape(2, 2, 3, SHARE)

    seq_loss = (jnp.log(rows[:, :, 0]) - jnp.log(rows[:, :, 1])).reshape(4 * SHARE)
    struct_loss = jnp.log(cols[0]) - jnp.log(cols[1])
    self_logits = LOGIT_SCALE * self_dot[0]
    extra = rows[:, :, 2].reshape(4, SHARE)[place(MP_AXES)]
    hard_loss = jnp.log(jnp.exp(self_logits) + extra) - self_logits
    return (seq_loss, struct_loss, hard_loss)


def solution(mesh):
    fine = Mesh(mesh.devices.reshape(8, 2, 4, 2, 2), ("z", "yh", "x", "yl", "core"))
    blk = ("z", "yh", "x")
    both = blk + MP_AXES
    placed = (
        P(blk, MP_AXES),
        P(blk, MP_AXES),
        P(MP_AXES, None),
        P(MP_AXES, None),
        P(blk),
        P(blk, None, None),
        P(blk, None),
        P(both, None),
    )
    return jax.shard_map(
        per_device,
        mesh=fine,
        in_specs=placed,
        out_specs=(P(blk), P(both), P(both)),
        check_vma=False,
    )
```

```python
import functools
import math

import jax
import jax.numpy as jnp
from jax import lax
from jax.experimental import pallas as pl
from jax.experimental.pallas import tpu as pltpu
from jax.sharding import Mesh, PartitionSpec as P

LOGIT_SCALE = 14.285714285714286
EPSILON = 1e-06
LOG2E = math.log2(math.e)

SHARE = 128
SIDE = 16
EDGE = SHARE * SIDE
WIDTH = 512
SLOTS = 16
EXT = 16
TILE = 512
STRIP = 256
SUB = 32
PICKS = 3

COL_AXES = ("yh", "x", "yl")
MP_AXES = ("yl", "core")
SIZES = {"z": 8, "yh": 2, "x": 4, "yl": 2, "core": 2}

VMEM = pl.BlockSpec(memory_space=pltpu.VMEM)
SMEM = pl.BlockSpec(memory_space=pltpu.SMEM)
HBM = pl.BlockSpec(memory_space=pltpu.HBM)


def shifted(value, axes, steps):
    names = (axes,) if isinstance(axes, str) else axes
    count = math.prod(SIZES[name] for name in names)
    return lax.ppermute(value, axes, [((place + steps) % count, place) for place in range(count)])


def project_kernel(core_ref, feats_hbm, proj_hbm, keep_ref, send_ref, feats_ref, proj_ref, sems, *, turned):
    core = core_ref[0]
    copies = [
        pltpu.make_async_copy(feats_hbm, feats_ref, sems.at[0]),
        pltpu.make_async_copy(proj_hbm, proj_ref, sems.at[1]),
    ]
    for copy in copies:
        copy.start()
    for copy in copies:
        copy.wait()
    for out, which in ((send_ref, 1 - core), (keep_ref, core)):
        for half in range(2):
            rows = pl.ds(pl.multiple_of((half * 2 + which) * SHARE, SHARE), SHARE)
            feats, over = (feats_ref[:, rows], 0) if turned else (feats_ref[rows, :], 1)
            out[half] = lax.dot_general(
                feats, proj_ref[...], (((over,), (0,)), ((), ())), preferred_element_type=jnp.float32
            )


def project(core, feats, proj, turned, name):
    shape = jax.ShapeDtypeStruct((2, SHARE, WIDTH), jnp.float32)
    return pl.pallas_call(
        functools.partial(project_kernel, turned=turned),
        out_shape=(shape, shape),
        in_specs=[SMEM, HBM, HBM],
        out_specs=(VMEM, VMEM),
        scratch_shapes=[
            pltpu.VMEM(feats.shape, feats.dtype),
            pltpu.VMEM(proj.shape, proj.dtype),
            pltpu.SemaphoreType.DMA((2,)),
        ],
        compiler_params=pltpu.CompilerParams(vmem_limit_bytes=12 * 1024 * 1024),
        name=name,
    )(core, feats, proj)


def merge_kernel(yl_ref, keep_ref, got_ref, keep2_ref, send2_ref):
    yl = yl_ref[0]
    send2_ref[...] = (keep_ref[1 - yl] + got_ref[1 - yl]).astype(jnp.bfloat16)
    keep2_ref[...] = keep_ref[yl] + got_ref[yl]


def merge(yl, keep, got, name):
    return pl.pallas_call(
        merge_kernel,
        out_shape=(
            jax.ShapeDtypeStruct((SHARE, WIDTH), jnp.float32),
            jax.ShapeDtypeStruct((SHARE, WIDTH), jnp.bfloat16),
        ),
        in_specs=[SMEM, VMEM, VMEM],
        out_specs=(VMEM, VMEM),
        compiler_params=pltpu.CompilerParams(vmem_limit_bytes=12 * 1024 * 1024),
        name=name,
    )(yl, keep, got)


def lanes_summed(values):
    return lax.dot_general(
        jnp.ones((8, values.shape[1]), jnp.float32),
        values,
        (((1,), (1,)), ((), ())),
        precision=lax.Precision.HIGHEST,
        preferred_element_type=jnp.float32,
    )


def normalized(keep2_ref, got2_ref):
    raw = keep2_ref[...] + got2_ref[...].astype(jnp.float32)
    total = jnp.sum(raw * raw, axis=1, keepdims=True)
    return (raw * lax.rsqrt(total + EPSILON)).astype(jnp.bfloat16)


def finish_kernel(keep2_s, got2_s, keep2_q, got2_q, struct_ext_ref, seq_ext_ref, peers_ref, seq_ref, self_ref):
    struct = normalized(keep2_s, got2_s)
    turned = struct.astype(jnp.float32).T.astype(jnp.bfloat16)
    struct_ext = struct_ext_ref[...]
    for peer in range(SIDE):
        peers_ref[peer, 0:WIDTH, :] = turned
        peers_ref[peer, WIDTH:, :] = struct_ext
    seq = normalized(keep2_q, got2_q)
    seq_ref[0:SHARE, :] = seq
    seq_ref[SHARE:, :] = seq_ext_ref[...]
    self_ref[...] = lanes_summed(seq.astype(jnp.float32) * struct.astype(jnp.float32))


def finish(*held):
    return pl.pallas_call(
        finish_kernel,
        out_shape=(
            jax.ShapeDtypeStruct((SIDE, WIDTH + EXT, SHARE), jnp.bfloat16),
            jax.ShapeDtypeStruct((SHARE + EXT, WIDTH), jnp.bfloat16),
            jax.ShapeDtypeStruct((8, SHARE), jnp.float32),
        ),
        in_specs=[VMEM] * 6,
        out_specs=(VMEM,) * 3,
        compiler_params=pltpu.CompilerParams(vmem_limit_bytes=12 * 1024 * 1024),
        name="finish",
    )(*held)


def integers(values):
    return values.astype(jnp.float32).astype(jnp.int32)


def pair_kernel(place_ref, *refs):
    seq_refs, s, rows_ref, cols_ref = refs[0:SIDE], refs[SIDE], refs[SIDE + 1], refs[SIDE + 2]
    q, ext_all, slots, info, counts, counts_smem, buf0, buf1, lab8, ct, cm, rt, rm, ex, sem = refs[SIDE + 3 :]
    tiles = EDGE // TILE
    strips = EDGE // STRIP
    part = TILE // strips
    buffers = (buf0, buf1)
    my_z, my_core = place_ref[0], place_ref[1]
    my_block = my_z * 2 + my_core
    lane = lax.broadcasted_iota(jnp.int32, (8, 128), 1)

    for block in range(SIDE):
        ext_all[block] = seq_refs[block][SHARE:, :]

    def decode(block, carry):
        ext = integers(ext_all[block])
        high, low = ext[:, 0:SHARE], ext[:, SHARE : 2 * SHARE]
        label = ext[:, 2 * SHARE : 3 * SHARE] * 128 + ext[:, 3 * SHARE :]
        hit = (high >> 4) == my_block
        slots[0] = jnp.where(hit, 1, 0)
        slots[1] = jnp.where(hit, (high & 15) * 128 + low + 1, 0)
        order = lax.broadcasted_iota(jnp.int32, (SLOTS, SHARE), 0)
        packed = jnp.zeros((SLOTS, SHARE), jnp.int32)
        found = jnp.zeros((SLOTS, SHARE), jnp.int32)
        for slot in range(SLOTS):
            code = jnp.broadcast_to(slots[1, slot : slot + 1, :], (SLOTS, SHARE))
            packed = packed + jnp.where(order == found, code, 0)
            found = found + jnp.broadcast_to(slots[0, slot : slot + 1, :], (SLOTS, SHARE))
        counts[block] = found[0:8]
        whole = jnp.concatenate(
            [packed - 1, label, jnp.zeros((128 - 2 * EXT, SHARE), jnp.int32)], axis=0
        ).astype(jnp.float32)
        info[pl.ds(pl.multiple_of(block * SHARE, SHARE), SHARE), :] = whole.T.astype(jnp.int32)
        return carry

    lax.fori_loop(0, SIDE, decode, 0)
    most = counts[...].reshape(SIDE * 8, 128)
    for step in (1, 2, 4, 8, 16, 32):
        most = jnp.maximum(most, pltpu.roll(most, step, axis=1))
    counts[...] = most.reshape(SIDE, 8, 128)
    to_smem = pltpu.make_async_copy(counts, counts_smem, sem)
    to_smem.start()

    for block in range(SIDE):
        q[block * SHARE : (block + 1) * SHARE, :] = seq_refs[block][0:SHARE, :]
    for chunk in range(SIDE):
        labels = integers(s[chunk, WIDTH:, :])
        lab8[:, chunk * 128 : (chunk + 1) * 128] = labels[0:8] * 128 + labels[8:16]
    ct[...] = jnp.zeros_like(ct)
    cm[...] = jnp.zeros_like(cm)
    to_smem.wait()
    row_of = lax.broadcasted_iota(jnp.int32, (8, SHARE), 0)

    for tile in range(tiles + 1):

        def body(step, carry, tile=tile):
            if tile < tiles:
                cols = jnp.concatenate([s[step * 2, 0:WIDTH, :], s[step * 2 + 1, 0:WIDTH, :]], axis=1)
                start = pl.multiple_of(step * STRIP, STRIP)
                buffers[tile % 2][:, pl.ds(start, STRIP)] = lax.dot_general(
                    q[tile * TILE : (tile + 1) * TILE, :],
                    cols,
                    (((1,), (0,)), ((), ())),
                    preferred_element_type=jnp.float32,
                )
            if tile > 0:
                logits = buffers[(tile - 1) % 2]

                def rows_at(group):
                    local = pl.multiple_of(step * part + group * 8, 8)
                    return local, info[pl.ds(pl.multiple_of((tile - 1) * TILE + local, 8), 8), :]

                def weights(local, chunk):
                    at = slice(chunk * 128, (chunk + 1) * 128)
                    return jnp.exp2(logits[pl.ds(local, 8), at] * (LOGIT_SCALE * LOG2E))

                zero = jnp.zeros((8, 128), jnp.float32)
                for sub in range(part // SUB):
                    groups = range(SUB // 8)
                    held = [rows_at(sub * (SUB // 8) + group) for group in groups]
                    label = [jnp.broadcast_to(code[:, SLOTS : SLOTS + 1], (8, 128)) for _, code in held]
                    wanted = [
                        [jnp.broadcast_to(code[:, pick : pick + 1], (8, 128)) for pick in range(PICKS)] for _, code in held
                    ]
                    row_total = [zero for _ in groups]
                    row_matched = [zero for _ in groups]
                    picked = [[zero] * PICKS for _ in groups]
                    for chunk in range(SIDE):
                        at = slice(chunk * 128, (chunk + 1) * 128)
                        col_label, col = lab8[:, at], lane + chunk * 128
                        col_total, col_matched = ct[:, at], cm[:, at]
                        for group in groups:
                            expo = weights(held[group][0], chunk)
                            kept = jnp.where(label[group] == col_label, expo, 0.0)
                            row_total[group] += expo
                            row_matched[group] += kept
                            col_total += expo
                            col_matched += kept
                            for pick in range(PICKS):
                                picked[group][pick] = jnp.where(
                                    wanted[group][pick] == col, expo, picked[group][pick]
                                )
                        ct[:, at] = col_total
                        cm[:, at] = col_matched
                    for group in groups:
                        local = held[group][0]
                        rt[pl.ds(local, 8), :] = row_total[group]
                        rm[pl.ds(local, 8), :] = row_matched[group]
                        ex[pl.ds(local, 8), :] = sum(picked[group][1:], picked[group][0])

                def pick_more(pick, carry):
                    for group in range(part // 8):
                        local, code = rows_at(group)
                        want = jnp.sum(jnp.where(lane == pick, code.astype(jnp.float32), 0.0), axis=1, keepdims=True)
                        want = jnp.broadcast_to(want.astype(jnp.int32), (8, 128))
                        found = zero
                        for chunk in range(SIDE):
                            found = jnp.where(want == lane + chunk * 128, weights(local, chunk), found)
                        ex[pl.ds(local, 8), :] += found
                    return carry

                block = (tile - 1) * (TILE // SHARE) + step // 2
                lax.fori_loop(PICKS, counts_smem[block, 0, (step % 2) * part + part - 1], pick_more, 0)
            return carry

        lax.fori_loop(0, strips, body, 0)
        if tile > 0:
            sums = [lanes_summed(each[...]) for each in (rt, rm, ex)]
            for inner in range(TILE // SHARE):
                block = (tile - 1) * (TILE // SHARE) + inner
                at = slice(inner * SHARE, (inner + 1) * SHARE)
                z, first = (my_z + block // 2) & 7, (my_core ^ (block % 2)) * 3
                out = jnp.zeros((8, SHARE), jnp.float32) if block % 2 == 0 else rows_ref[z]
                for which in range(3):
                    out = jnp.where(row_of == first + which, sums[which][:, at], out)
                rows_ref[z] = out

    for chunk in range(SIDE):
        at = slice(chunk * 128, (chunk + 1) * 128)
        total = jnp.sum(ct[:, at], axis=0, keepdims=True)
        matched = jnp.sum(cm[:, at], axis=0, keepdims=True)
        cols_ref[chunk] = jnp.where(row_of == 0, total, matched)


def pair_sums(place, seq_blocks, struct_blocks):
    return pl.pallas_call(
        pair_kernel,
        out_shape=(
            jax.ShapeDtypeStruct((8, 8, SHARE), jnp.float32),
            jax.ShapeDtypeStruct((SIDE, 8, SHARE), jnp.float32),
        ),
        in_specs=[SMEM] + [VMEM] * (SIDE + 1),
        out_specs=(VMEM, VMEM),
        scratch_shapes=[
            pltpu.VMEM((EDGE, WIDTH), jnp.bfloat16),
            pltpu.VMEM((SIDE, EXT, WIDTH), jnp.bfloat16),
            pltpu.VMEM((2, SLOTS, SHARE), jnp.int32),
            pltpu.VMEM((EDGE, 128), jnp.int32),
            pltpu.VMEM((SIDE, 8, 128), jnp.int32),
            pltpu.SMEM((SIDE, 8, 128), jnp.int32),
            pltpu.VMEM((TILE, EDGE), jnp.float32),
            pltpu.VMEM((TILE, EDGE), jnp.float32),
            pltpu.VMEM((8, EDGE), jnp.int32),
            pltpu.VMEM((8, EDGE), jnp.float32),
            pltpu.VMEM((8, EDGE), jnp.float32),
            pltpu.VMEM((TILE, 128), jnp.float32),
            pltpu.VMEM((TILE, 128), jnp.float32),
            pltpu.VMEM((TILE, 128), jnp.float32),
            pltpu.SemaphoreType.DMA,
        ],
        compiler_params=pltpu.CompilerParams(vmem_limit_bytes=28 * 1024 * 1024),
        cost_estimate=pl.CostEstimate(
            flops=2 * EDGE * EDGE * WIDTH, bytes_accessed=4 * EDGE * WIDTH, transcendentals=EDGE * EDGE
        ),
        name="pair_sums",
    )(place, *seq_blocks, struct_blocks)


def over_z(block):
    found = {0: block, 1: shifted(block, "z", 1), 7: shifted(block, "z", -1)}
    found[2], found[6] = shifted(found[1], "z", 1), shifted(found[7], "z", -1)
    found[3], found[5] = shifted(found[2], "z", 1), shifted(found[6], "z", -1)
    found[4] = shifted(found[3], "z", 1)
    return [found[place] for place in range(8)]


def per_device(struct_feats, seq_feats, struct_proj, seq_proj, cluster_ids, hard_owner, hard_local, hard_valid):
    place = lambda axes: lax.axis_index(axes).astype(jnp.int32)
    core, yl = place("core"), place("yl")
    keep_s, send_s = project(core.reshape(1), struct_feats, struct_proj, False, "project_struct")
    got_s = shifted(send_s, "core", 1)
    keep_q, send_q = project(core.reshape(1), seq_feats.T, seq_proj, True, "project_seq")
    got_q = shifted(send_q, "core", 1)

    keep2_s, send2_s = merge(yl.reshape(1), keep_s, got_s, "merge_struct")
    got2_s = shifted(send2_s, "yl", 1)
    keep2_q, send2_q = merge(yl.reshape(1), keep_q, got_q, "merge_seq")
    got2_q = shifted(send2_q, "yl", 1)
    cluster_ids, hard_owner, hard_local, hard_valid, send2_q = lax.optimization_barrier(
        (cluster_ids, hard_owner, hard_local, hard_valid, send2_q)
    )
    own = lambda value: lax.dynamic_slice_in_dim(value, place(MP_AXES) * SHARE, SHARE, 0)
    labels = own(cluster_ids)
    owner = own(hard_owner[:, :, 0])
    local = own(hard_local)
    block = (owner >> 3) * 2 + ((local >> 7) & 1)
    chunk = (owner & 7) * 2 + (local >> 8)
    high = jnp.where(hard_valid > 0, block * 16 + chunk, -1).T
    low = (local & 127).T
    wide = lambda value: jnp.broadcast_to(value[None], (EXT, SHARE))
    seq_ext = jnp.concatenate([high, low, wide(labels >> 7), wide(labels & 127)], axis=1).astype(jnp.bfloat16)
    struct_ext = jnp.concatenate([wide(labels >> 7)[0:8], wide(labels & 127)[0:8]], axis=0).astype(jnp.bfloat16)

    struct_peers, seq_block, self_dot = finish(keep2_s, got2_s, keep2_q, got2_q, struct_ext, seq_ext)
    struct_blocks = lax.all_to_all(struct_peers, COL_AXES, split_axis=0, concat_axis=0, tiled=True)
    seq_blocks = [each for held in over_z(seq_block) for each in (held, shifted(held, "core", 1))]

    rows, cols = pair_sums(jnp.stack([place("z"), core]), seq_blocks, struct_blocks)
    rows = jnp.sum(lax.all_to_all(rows, "z", split_axis=0, concat_axis=0, tiled=True), axis=0)
    cols = jnp.sum(lax.all_to_all(cols, COL_AXES, split_axis=0, concat_axis=0, tiled=True), axis=0)
    rows = lax.all_gather(rows, MP_AXES, axis=0, tiled=False).reshape(2, 2, 8, SHARE)
    rows = jnp.sum(rows, axis=1)[:, 0:6].reshape(2, 2, 3, SHARE)

    seq_loss = (jnp.log(rows[:, :, 0]) - jnp.log(rows[:, :, 1])).reshape(4 * SHARE)
    struct_loss = jnp.log(cols[0]) - jnp.log(cols[1])
    self_logits = LOGIT_SCALE * self_dot[0]
    extra = rows[:, :, 2].reshape(4, SHARE)[place(MP_AXES)]
    hard_loss = jnp.log(jnp.exp(self_logits) + extra) - self_logits
    return (seq_loss, struct_loss, hard_loss)


def solution(mesh):
    fine = Mesh(mesh.devices.reshape(8, 2, 4, 2, 2), ("z", "yh", "x", "yl", "core"))
    blk = ("z", "yh", "x")
    both = blk + MP_AXES
    placed = (
        P(blk, MP_AXES),
        P(blk, MP_AXES),
        P(MP_AXES, None),
        P(MP_AXES, None),
        P(blk),
        P(blk, None, None),
        P(blk, None),
        P(both, None),
    )
    return jax.shard_map(
        per_device,
        mesh=fine,
        in_specs=placed,
        out_specs=(P(blk), P(both), P(both)),
        check_vma=False,
    )
```

```python
import functools
import math

import jax
import jax.numpy as jnp
from jax import lax
from jax.experimental import pallas as pl
from jax.experimental.pallas import tpu as pltpu
from jax.sharding import Mesh, PartitionSpec as P

LOGIT_SCALE = 14.285714285714286
EPSILON = 1e-06
LOG2E = math.log2(math.e)
POLYNOMIAL = (4.626287491105563e-06, 0.00010370556301479831, 0.001853591056490648, 0.024912203935707634, 0.22321428590727893, 1.0000000060541538)

SHARE = 128
SIDE = 16
EDGE = SHARE * SIDE
WIDTH = 512
SLOTS = 16
EXT = 16
TILE = 512
STRIP = 512
SUB = 32

COL_AXES = ("yh", "x", "yl")
MP_AXES = ("yl", "core")
SIZES = {"z": 8, "yh": 2, "x": 4, "yl": 2, "core": 2}

VMEM = pl.BlockSpec(memory_space=pltpu.VMEM)
SMEM = pl.BlockSpec(memory_space=pltpu.SMEM)
HBM = pl.BlockSpec(memory_space=pltpu.HBM)


def shifted(value, axes, steps):
    names = (axes,) if isinstance(axes, str) else axes
    count = math.prod(SIZES[name] for name in names)
    return lax.ppermute(value, axes, [((place + steps) % count, place) for place in range(count)])


def project_kernel(core_ref, feats_hbm, proj_hbm, keep_ref, send_ref, feats_ref, proj_ref, sems, *, turned):
    core = core_ref[0]
    copies = [
        pltpu.make_async_copy(feats_hbm, feats_ref, sems.at[0]),
        pltpu.make_async_copy(proj_hbm, proj_ref, sems.at[1]),
    ]
    for copy in copies:
        copy.start()
    for copy in copies:
        copy.wait()
    for out, which in ((send_ref, 1 - core), (keep_ref, core)):
        for half in range(2):
            rows = pl.ds(pl.multiple_of((half * 2 + which) * SHARE, SHARE), SHARE)
            feats, over = (feats_ref[:, rows], 0) if turned else (feats_ref[rows, :], 1)
            out[half] = lax.dot_general(
                feats, proj_ref[...], (((over,), (0,)), ((), ())), preferred_element_type=jnp.float32
            )


def project(core, feats, proj, turned, name):
    shape = jax.ShapeDtypeStruct((2, SHARE, WIDTH), jnp.float32)
    return pl.pallas_call(
        functools.partial(project_kernel, turned=turned),
        out_shape=(shape, shape),
        in_specs=[SMEM, HBM, HBM],
        out_specs=(VMEM, VMEM),
        scratch_shapes=[
            pltpu.VMEM(feats.shape, feats.dtype),
            pltpu.VMEM(proj.shape, proj.dtype),
            pltpu.SemaphoreType.DMA((2,)),
        ],
        compiler_params=pltpu.CompilerParams(vmem_limit_bytes=12 * 1024 * 1024),
        name=name,
    )(core, feats, proj)


def merge_kernel(yl_ref, keep_ref, got_ref, keep2_ref, send2_ref):
    yl = yl_ref[0]
    send2_ref[...] = (keep_ref[1 - yl] + got_ref[1 - yl]).astype(jnp.bfloat16)
    keep2_ref[...] = keep_ref[yl] + got_ref[yl]


def merge(yl, keep, got, name):
    return pl.pallas_call(
        merge_kernel,
        out_shape=(
            jax.ShapeDtypeStruct((SHARE, WIDTH), jnp.float32),
            jax.ShapeDtypeStruct((SHARE, WIDTH), jnp.bfloat16),
        ),
        in_specs=[SMEM, VMEM, VMEM],
        out_specs=(VMEM, VMEM),
        compiler_params=pltpu.CompilerParams(vmem_limit_bytes=12 * 1024 * 1024),
        name=name,
    )(yl, keep, got)


def lanes_summed(values):
    return lax.dot_general(
        jnp.ones((8, values.shape[1]), jnp.float32),
        values,
        (((1,), (1,)), ((), ())),
        precision=lax.Precision.HIGHEST,
        preferred_element_type=jnp.float32,
    )


def normalized(keep2_ref, got2_ref):
    raw = keep2_ref[...] + got2_ref[...].astype(jnp.float32)
    total = jnp.sum(raw * raw, axis=1, keepdims=True)
    return (raw * lax.rsqrt(total + EPSILON)).astype(jnp.bfloat16)


def finish_kernel(keep2_s, got2_s, keep2_q, got2_q, struct_ext_ref, seq_ext_ref, peers_ref, seq_ref, self_ref):
    struct = normalized(keep2_s, got2_s)
    turned = struct.astype(jnp.float32).T.astype(jnp.bfloat16)
    struct_ext = struct_ext_ref[...]
    for peer in range(SIDE):
        peers_ref[peer, 0:WIDTH, :] = turned
        peers_ref[peer, WIDTH:, :] = struct_ext
    seq = normalized(keep2_q, got2_q)
    seq_ref[0:SHARE, :] = seq
    seq_ref[SHARE:, :] = seq_ext_ref[...]
    self_ref[...] = lanes_summed(seq.astype(jnp.float32) * struct.astype(jnp.float32))


def finish(*held):
    return pl.pallas_call(
        finish_kernel,
        out_shape=(
            jax.ShapeDtypeStruct((SIDE, WIDTH + EXT, SHARE), jnp.bfloat16),
            jax.ShapeDtypeStruct((SHARE + EXT, WIDTH), jnp.bfloat16),
            jax.ShapeDtypeStruct((8, SHARE), jnp.float32),
        ),
        in_specs=[VMEM] * 6,
        out_specs=(VMEM,) * 3,
        compiler_params=pltpu.CompilerParams(vmem_limit_bytes=12 * 1024 * 1024),
        name="finish",
    )(*held)


def integers(values):
    return values.astype(jnp.float32).astype(jnp.int32)


def exponential(products):
    power = products * POLYNOMIAL[0] + POLYNOMIAL[1]
    for coefficient in POLYNOMIAL[2:]:
        power = power * products + coefficient
    for _ in range(6):
        power = power * power
    return power


def pair_kernel(place_ref, *refs):
    seq_refs, s, rows_ref, cols_ref = refs[0:SIDE], refs[SIDE], refs[SIDE + 1], refs[SIDE + 2]
    q, info, buf0, buf1, lab8, ct, cm, rt, rm, ex = refs[SIDE + 3 :]
    tiles = EDGE // TILE
    strips = EDGE // STRIP
    part = TILE // strips
    buffers = (buf0, buf1)
    my_z, my_core = place_ref[0], place_ref[1]
    my_block = my_z * 2 + my_core

    for block in range(SIDE):
        at = slice(block * SHARE, (block + 1) * SHARE)
        q[at, :] = seq_refs[block][0:SHARE, :]
        ext = integers(seq_refs[block][SHARE:, :])
        high, low = ext[:, 0:SHARE], ext[:, SHARE : 2 * SHARE]
        label = ext[:, 2 * SHARE : 3 * SHARE] * 128 + ext[:, 3 * SHARE :]
        code = jnp.where((high >> 4) == my_block, (high & 15) * 128 + low, -1)
        whole = jnp.concatenate(
            [code, -1 - label, jnp.full((128 - 2 * EXT, SHARE), -1, jnp.int32)], axis=0
        ).astype(jnp.float32)
        info[at, :] = whole.T.astype(jnp.int32)
    for chunk in range(SIDE):
        labels = integers(s[chunk, WIDTH:, :])
        lab8[:, chunk * 128 : (chunk + 1) * 128] = labels[0:8] * 128 + labels[8:16]
    ct[...] = jnp.zeros_like(ct)
    cm[...] = jnp.zeros_like(cm)
    row_of = lax.broadcasted_iota(jnp.int32, (8, SHARE), 0)

    for tile in range(tiles + 1):

        def body(step, carry, tile=tile):
            if tile < tiles:
                wide = STRIP // SHARE
                cols = jnp.concatenate([s[step * wide + each, 0:WIDTH, :] for each in range(wide)], axis=1)
                start = pl.multiple_of(step * STRIP, STRIP)
                buffers[tile % 2][:, pl.ds(start, STRIP)] = lax.dot_general(
                    q[tile * TILE : (tile + 1) * TILE, :],
                    cols,
                    (((1,), (0,)), ((), ())),
                    preferred_element_type=jnp.float32,
                )
            if tile > 0:
                products = buffers[(tile - 1) % 2]
                zero = jnp.zeros((8, 128), jnp.float32)
                groups = range(SUB // 8)
                for sub in range(part // SUB):
                    local = [pl.multiple_of(step * part + sub * SUB + group * 8, 8) for group in groups]
                    code = [info[pl.ds(pl.multiple_of((tile - 1) * TILE + each, 8), 8), :] for each in local]
                    label = [jnp.broadcast_to(-1 - each[:, SLOTS : SLOTS + 1], (8, 128)) for each in code]
                    lane = [each & 127 for each in code]
                    chunk_of = [each >> 7 for each in code]
                    row_total, row_matched, picked = [zero for _ in groups], [zero for _ in groups], [zero for _ in groups]
                    for chunk in range(SIDE):
                        at = slice(chunk * 128, (chunk + 1) * 128)
                        col_label = lab8[:, at]
                        col_total, col_matched = ct[:, at], cm[:, at]
                        for group in groups:
                            product = products[pl.ds(local[group], 8), at]
                            if chunk % 2:
                                expo = exponential(product)
                            else:
                                expo = jnp.exp2(product * (LOGIT_SCALE * LOG2E))
                            kept = jnp.where(label[group] == col_label, expo, 0.0)
                            row_total[group] += expo
                            row_matched[group] += kept
                            col_total += expo
                            col_matched += kept
                            found = jnp.take_along_axis(expo, lane[group], axis=1, mode="promise_in_bounds")
                            picked[group] = jnp.where(chunk_of[group] == chunk, found, picked[group])
                        ct[:, at] = col_total
                        cm[:, at] = col_matched
                    for group in groups:
                        rt[pl.ds(local[group], 8), :] = row_total[group]
                        rm[pl.ds(local[group], 8), :] = row_matched[group]
                        ex[pl.ds(local[group], 8), :] = picked[group]
            return carry

        lax.fori_loop(0, strips, body, 0)
        if tile > 0:
            sums = [lanes_summed(each[...]) for each in (rt, rm, ex)]
            for inner in range(TILE // SHARE):
                block = (tile - 1) * (TILE // SHARE) + inner
                at = slice(inner * SHARE, (inner + 1) * SHARE)
                z, first = (my_z + block // 2) & 7, (my_core ^ (block % 2)) * 3
                out = jnp.zeros((8, SHARE), jnp.float32) if block % 2 == 0 else rows_ref[z]
                for which in range(3):
                    out = jnp.where(row_of == first + which, sums[which][:, at], out)
                rows_ref[z] = out

    for chunk in range(SIDE):
        at = slice(chunk * 128, (chunk + 1) * 128)
        total = jnp.sum(ct[:, at], axis=0, keepdims=True)
        matched = jnp.sum(cm[:, at], axis=0, keepdims=True)
        cols_ref[chunk] = jnp.where(row_of == 0, total, matched)


def pair_sums(place, seq_blocks, struct_blocks):
    return pl.pallas_call(
        pair_kernel,
        out_shape=(
            jax.ShapeDtypeStruct((8, 8, SHARE), jnp.float32),
            jax.ShapeDtypeStruct((SIDE, 8, SHARE), jnp.float32),
        ),
        in_specs=[SMEM] + [VMEM] * (SIDE + 1),
        out_specs=(VMEM, VMEM),
        scratch_shapes=[
            pltpu.VMEM((EDGE, WIDTH), jnp.bfloat16),
            pltpu.VMEM((EDGE, 128), jnp.int32),
            pltpu.VMEM((TILE, EDGE), jnp.float32),
            pltpu.VMEM((TILE, EDGE), jnp.float32),
            pltpu.VMEM((8, EDGE), jnp.int32),
            pltpu.VMEM((8, EDGE), jnp.float32),
            pltpu.VMEM((8, EDGE), jnp.float32),
            pltpu.VMEM((TILE, 128), jnp.float32),
            pltpu.VMEM((TILE, 128), jnp.float32),
            pltpu.VMEM((TILE, 128), jnp.float32),
        ],
        compiler_params=pltpu.CompilerParams(vmem_limit_bytes=28 * 1024 * 1024),
        cost_estimate=pl.CostEstimate(
            flops=2 * EDGE * EDGE * WIDTH, bytes_accessed=4 * EDGE * WIDTH, transcendentals=EDGE * EDGE
        ),
        name="pair_sums",
    )(place, *seq_blocks, struct_blocks)


def over_z(block):
    found = {0: block, 1: shifted(block, "z", 1), 7: shifted(block, "z", -1)}
    found[2], found[6] = shifted(found[1], "z", 1), shifted(found[7], "z", -1)
    found[3], found[5] = shifted(found[2], "z", 1), shifted(found[6], "z", -1)
    found[4] = shifted(found[3], "z", 1)
    return [found[place] for place in range(8)]


def per_device(struct_feats, seq_feats, struct_proj, seq_proj, cluster_ids, hard_owner, hard_local, hard_valid):
    place = lambda axes: lax.axis_index(axes).astype(jnp.int32)
    core, yl = place("core"), place("yl")
    keep_s, send_s = project(core.reshape(1), struct_feats, struct_proj, False, "project_struct")
    got_s = shifted(send_s, "core", 1)
    keep_q, send_q = project(core.reshape(1), seq_feats.T, seq_proj, True, "project_seq")
    got_q = shifted(send_q, "core", 1)

    keep2_s, send2_s = merge(yl.reshape(1), keep_s, got_s, "merge_struct")
    got2_s = shifted(send2_s, "yl", 1)
    keep2_q, send2_q = merge(yl.reshape(1), keep_q, got_q, "merge_seq")
    got2_q = shifted(send2_q, "yl", 1)
    cluster_ids, hard_owner, hard_local, hard_valid, send2_q = lax.optimization_barrier(
        (cluster_ids, hard_owner, hard_local, hard_valid, send2_q)
    )
    own = lambda value: lax.dynamic_slice_in_dim(value, place(MP_AXES) * SHARE, SHARE, 0)
    labels = own(cluster_ids)
    owner = own(hard_owner[:, :, 0])
    local = own(hard_local)
    block = (owner >> 3) * 2 + ((local >> 7) & 1)
    chunk = (owner & 7) * 2 + (local >> 8)
    high = jnp.where(hard_valid > 0, block * 16 + chunk, -1).T
    low = (local & 127).T
    wide = lambda value: jnp.broadcast_to(value[None], (EXT, SHARE))
    seq_ext = jnp.concatenate([high, low, wide(labels >> 7), wide(labels & 127)], axis=1).astype(jnp.bfloat16)
    struct_ext = jnp.concatenate([wide(labels >> 7)[0:8], wide(labels & 127)[0:8]], axis=0).astype(jnp.bfloat16)

    struct_peers, seq_block, self_dot = finish(keep2_s, got2_s, keep2_q, got2_q, struct_ext, seq_ext)
    struct_blocks = lax.all_to_all(struct_peers, COL_AXES, split_axis=0, concat_axis=0, tiled=True)
    seq_blocks = [each for held in over_z(seq_block) for each in (held, shifted(held, "core", 1))]

    rows, cols = pair_sums(jnp.stack([place("z"), core]), seq_blocks, struct_blocks)
    rows = jnp.sum(lax.all_to_all(rows, "z", split_axis=0, concat_axis=0, tiled=True), axis=0)
    cols = jnp.sum(lax.all_to_all(cols, COL_AXES, split_axis=0, concat_axis=0, tiled=True), axis=0)
    rows = lax.all_gather(rows, MP_AXES, axis=0, tiled=False).reshape(2, 2, 8, SHARE)
    rows = jnp.sum(rows, axis=1)[:, 0:6].reshape(2, 2, 3, SHARE)

    seq_loss = (jnp.log(rows[:, :, 0]) - jnp.log(rows[:, :, 1])).reshape(4 * SHARE)
    struct_loss = jnp.log(cols[0]) - jnp.log(cols[1])
    self_logits = LOGIT_SCALE * self_dot[0]
    extra = rows[:, :, 2].reshape(4, SHARE)[place(MP_AXES)]
    hard_loss = jnp.log(jnp.exp(self_logits) + extra) - self_logits
    return (seq_loss, struct_loss, hard_loss)


def solution(mesh):
    fine = Mesh(mesh.devices.reshape(8, 2, 4, 2, 2), ("z", "yh", "x", "yl", "core"))
    blk = ("z", "yh", "x")
    both = blk + MP_AXES
    placed = (
        P(blk, MP_AXES),
        P(blk, MP_AXES),
        P(MP_AXES, None),
        P(MP_AXES, None),
        P(blk),
        P(blk, None, None),
        P(blk, None),
        P(both, None),
    )
    return jax.shard_map(
        per_device,
        mesh=fine,
        in_specs=placed,
        out_specs=(P(blk), P(both), P(both)),
        check_vma=False,
    )
```

```python
import functools
import math

import jax
import jax.numpy as jnp
from jax import lax
from jax.experimental import pallas as pl
from jax.experimental.pallas import tpu as pltpu
from jax.sharding import Mesh, PartitionSpec as P

LOGIT_SCALE = 14.285714285714286
EPSILON = 1e-06
LOG2E = math.log2(math.e)
POLYNOMIAL = (4.626287491105563e-06, 0.00010370556301479831, 0.001853591056490648, 0.024912203935707634, 0.22321428590727893, 1.0000000060541538)

SHARE = 128
SIDE = 16
EDGE = SHARE * SIDE
WIDTH = 512
SLOTS = 16
EXT = 16
TILE = 512
STRIP = 512
SUB = 32

COL_AXES = ("yh", "x", "yl")
MP_AXES = ("yl", "core")
SIZES = {"z": 8, "yh": 2, "x": 4, "yl": 2, "core": 2}

VMEM = pl.BlockSpec(memory_space=pltpu.VMEM)
SMEM = pl.BlockSpec(memory_space=pltpu.SMEM)
HBM = pl.BlockSpec(memory_space=pltpu.HBM)


def shifted(value, axes, steps):
    names = (axes,) if isinstance(axes, str) else axes
    count = math.prod(SIZES[name] for name in names)
    return lax.ppermute(value, axes, [((place + steps) % count, place) for place in range(count)])


def project_kernel(core_ref, feats_hbm, proj_hbm, keep_ref, send_ref, feats_ref, proj_ref, sems, *, turned):
    core = core_ref[0]
    copies = [
        pltpu.make_async_copy(feats_hbm, feats_ref, sems.at[0]),
        pltpu.make_async_copy(proj_hbm, proj_ref, sems.at[1]),
    ]
    for copy in copies:
        copy.start()
    for copy in copies:
        copy.wait()
    for out, which in ((send_ref, 1 - core), (keep_ref, core)):
        for half in range(2):
            rows = pl.ds(pl.multiple_of((half * 2 + which) * SHARE, SHARE), SHARE)
            feats, over = (feats_ref[:, rows], 0) if turned else (feats_ref[rows, :], 1)
            out[half] = lax.dot_general(
                feats, proj_ref[...], (((over,), (0,)), ((), ())), preferred_element_type=jnp.float32
            )


def project(core, feats, proj, turned, name):
    shape = jax.ShapeDtypeStruct((2, SHARE, WIDTH), jnp.float32)
    return pl.pallas_call(
        functools.partial(project_kernel, turned=turned),
        out_shape=(shape, shape),
        in_specs=[SMEM, HBM, HBM],
        out_specs=(VMEM, VMEM),
        scratch_shapes=[
            pltpu.VMEM(feats.shape, feats.dtype),
            pltpu.VMEM(proj.shape, proj.dtype),
            pltpu.SemaphoreType.DMA((2,)),
        ],
        compiler_params=pltpu.CompilerParams(vmem_limit_bytes=12 * 1024 * 1024),
        name=name,
    )(core, feats, proj)


def merge_kernel(yl_ref, keep_ref, got_ref, keep2_ref, send2_ref):
    yl = yl_ref[0]
    send2_ref[...] = (keep_ref[1 - yl] + got_ref[1 - yl]).astype(jnp.bfloat16)
    keep2_ref[...] = keep_ref[yl] + got_ref[yl]


def merge(yl, keep, got, name):
    return pl.pallas_call(
        merge_kernel,
        out_shape=(
            jax.ShapeDtypeStruct((SHARE, WIDTH), jnp.float32),
            jax.ShapeDtypeStruct((SHARE, WIDTH), jnp.bfloat16),
        ),
        in_specs=[SMEM, VMEM, VMEM],
        out_specs=(VMEM, VMEM),
        compiler_params=pltpu.CompilerParams(vmem_limit_bytes=12 * 1024 * 1024),
        name=name,
    )(yl, keep, got)


def lanes_summed(values):
    return lax.dot_general(
        jnp.ones((8, values.shape[1]), jnp.float32),
        values,
        (((1,), (1,)), ((), ())),
        precision=lax.Precision.HIGHEST,
        preferred_element_type=jnp.float32,
    )


def normalized(keep2_ref, got2_ref):
    raw = keep2_ref[...] + got2_ref[...].astype(jnp.float32)
    total = jnp.sum(raw * raw, axis=1, keepdims=True)
    return (raw * lax.rsqrt(total + EPSILON)).astype(jnp.bfloat16)


def finish_struct_kernel(keep2_ref, got2_ref, ext_ref, struct_ref, peers_ref):
    struct = normalized(keep2_ref, got2_ref)
    struct_ref[...] = struct
    turned = struct.astype(jnp.float32).T.astype(jnp.bfloat16)
    ext = ext_ref[...]
    for peer in range(SIDE):
        peers_ref[peer, 0:WIDTH, :] = turned
        peers_ref[peer, WIDTH:, :] = ext


def finish_struct(keep2, got2, ext):
    return pl.pallas_call(
        finish_struct_kernel,
        out_shape=(
            jax.ShapeDtypeStruct((SHARE, WIDTH), jnp.bfloat16),
            jax.ShapeDtypeStruct((SIDE, WIDTH + EXT, SHARE), jnp.bfloat16),
        ),
        in_specs=[VMEM] * 3,
        out_specs=(VMEM,) * 2,
        compiler_params=pltpu.CompilerParams(vmem_limit_bytes=12 * 1024 * 1024),
        name="finish_struct",
    )(keep2, got2, ext)


def finish_seq_kernel(keep2_ref, got2_ref, ext_ref, struct_ref, seq_ref, self_ref):
    seq = normalized(keep2_ref, got2_ref)
    seq_ref[0:SHARE, :] = seq
    seq_ref[SHARE:, :] = ext_ref[...]
    self_ref[...] = lanes_summed(seq.astype(jnp.float32) * struct_ref[...].astype(jnp.float32))


def finish_seq(keep2, got2, ext, struct):
    return pl.pallas_call(
        finish_seq_kernel,
        out_shape=(
            jax.ShapeDtypeStruct((SHARE + EXT, WIDTH), jnp.bfloat16),
            jax.ShapeDtypeStruct((8, SHARE), jnp.float32),
        ),
        in_specs=[VMEM] * 4,
        out_specs=(VMEM,) * 2,
        compiler_params=pltpu.CompilerParams(vmem_limit_bytes=12 * 1024 * 1024),
        name="finish_seq",
    )(keep2, got2, ext, struct)


def integers(values):
    return values.astype(jnp.float32).astype(jnp.int32)


def exponential(products):
    power = products * POLYNOMIAL[0] + POLYNOMIAL[1]
    for coefficient in POLYNOMIAL[2:]:
        power = power * products + coefficient
    for _ in range(6):
        power = power * power
    return power


def pair_kernel(place_ref, *refs):
    seq_refs, s, rows_ref, cols_ref = refs[0:SIDE], refs[SIDE], refs[SIDE + 1], refs[SIDE + 2]
    q, info, buf0, buf1, lab8, ct, cm, rt, rm, ex = refs[SIDE + 3 :]
    tiles = EDGE // TILE
    strips = EDGE // STRIP
    part = TILE // strips
    buffers = (buf0, buf1)
    my_z, my_core = place_ref[0], place_ref[1]
    my_block = my_z * 2 + my_core

    for block in range(SIDE):
        at = slice(block * SHARE, (block + 1) * SHARE)
        q[at, :] = seq_refs[block][0:SHARE, :]
        ext = integers(seq_refs[block][SHARE:, :])
        high, low = ext[:, 0:SHARE], ext[:, SHARE : 2 * SHARE]
        label = ext[:, 2 * SHARE : 3 * SHARE] * 128 + ext[:, 3 * SHARE :]
        code = jnp.where((high >> 4) == my_block, (high & 15) * 128 + low, -1)
        whole = jnp.concatenate(
            [code, -1 - label, jnp.full((128 - 2 * EXT, SHARE), -1, jnp.int32)], axis=0
        ).astype(jnp.float32)
        info[at, :] = whole.T.astype(jnp.int32)
    for chunk in range(SIDE):
        labels = integers(s[chunk, WIDTH:, :])
        lab8[:, chunk * 128 : (chunk + 1) * 128] = labels[0:8] * 128 + labels[8:16]
    ct[...] = jnp.zeros_like(ct)
    cm[...] = jnp.zeros_like(cm)
    row_of = lax.broadcasted_iota(jnp.int32, (8, SHARE), 0)

    for tile in range(tiles + 1):

        def body(step, carry, tile=tile):
            def piece(number):
                if tile == tiles:
                    return
                rows = (number % 4) * SHARE
                first = step * (STRIP // SHARE) + (number // 4) * 2
                cols = jnp.concatenate([s[first, 0:WIDTH, :], s[first + 1, 0:WIDTH, :]], axis=1)
                start = pl.multiple_of(first * SHARE, 2 * SHARE)
                buffers[tile % 2][rows : rows + SHARE, pl.ds(start, 2 * SHARE)] = jnp.dot(
                    q[tile * TILE + rows : tile * TILE + rows + SHARE, :], cols, preferred_element_type=jnp.float32
                )

            if tile == 0:
                for number in range(8):
                    piece(number)
            if tile > 0:
                products = buffers[(tile - 1) % 2]
                zero = jnp.zeros((8, 128), jnp.float32)
                groups = range(SUB // 8)
                for sub in range(part // SUB):
                    local = [pl.multiple_of(step * part + sub * SUB + group * 8, 8) for group in groups]
                    code = [info[pl.ds(pl.multiple_of((tile - 1) * TILE + each, 8), 8), :] for each in local]
                    label = [jnp.broadcast_to(-1 - each[:, SLOTS : SLOTS + 1], (8, 128)) for each in code]
                    lane = [each & 127 for each in code]
                    chunk_of = [each >> 7 for each in code]
                    row_total, row_matched, picked = [zero for _ in groups], [zero for _ in groups], [zero for _ in groups]
                    for chunk in range(SIDE):
                        if chunk % 8 == 0:
                            piece(sub * 2 + chunk // 8)
                        at = slice(chunk * 128, (chunk + 1) * 128)
                        col_label = lab8[:, at]
                        col_total, col_matched = ct[:, at], cm[:, at]
                        for group in groups:
                            product = products[pl.ds(local[group], 8), at]
                            if chunk % 2:
                                expo = exponential(product)
                            else:
                                expo = jnp.exp2(product * (LOGIT_SCALE * LOG2E))
                            kept = jnp.where(label[group] == col_label, expo, 0.0)
                            row_total[group] += expo
                            row_matched[group] += kept
                            col_total += expo
                            col_matched += kept
                            found = jnp.take_along_axis(expo, lane[group], axis=1, mode="promise_in_bounds")
                            picked[group] = jnp.where(chunk_of[group] == chunk, found, picked[group])
                        ct[:, at] = col_total
                        cm[:, at] = col_matched
                    for group in groups:
                        rt[pl.ds(local[group], 8), :] = row_total[group]
                        rm[pl.ds(local[group], 8), :] = row_matched[group]
                        ex[pl.ds(local[group], 8), :] = picked[group]
            return carry

        lax.fori_loop(0, strips, body, 0)
        if tile > 0:
            sums = [lanes_summed(each[...]) for each in (rt, rm, ex)]
            for inner in range(TILE // SHARE):
                block = (tile - 1) * (TILE // SHARE) + inner
                at = slice(inner * SHARE, (inner + 1) * SHARE)
                z, first = (my_z + block // 2) & 7, (my_core ^ (block % 2)) * 3
                out = jnp.zeros((8, SHARE), jnp.float32) if block % 2 == 0 else rows_ref[z]
                for which in range(3):
                    out = jnp.where(row_of == first + which, sums[which][:, at], out)
                rows_ref[z] = out

    for chunk in range(SIDE):
        at = slice(chunk * 128, (chunk + 1) * 128)
        total = jnp.sum(ct[:, at], axis=0, keepdims=True)
        matched = jnp.sum(cm[:, at], axis=0, keepdims=True)
        cols_ref[chunk] = jnp.where(row_of == 0, total, matched)


def pair_sums(place, seq_blocks, struct_blocks):
    return pl.pallas_call(
        pair_kernel,
        out_shape=(
            jax.ShapeDtypeStruct((8, 8, SHARE), jnp.float32),
            jax.ShapeDtypeStruct((SIDE, 8, SHARE), jnp.float32),
        ),
        in_specs=[SMEM] + [VMEM] * (SIDE + 1),
        out_specs=(VMEM, VMEM),
        scratch_shapes=[
            pltpu.VMEM((EDGE, WIDTH), jnp.bfloat16),
            pltpu.VMEM((EDGE, 128), jnp.int32),
            pltpu.VMEM((TILE, EDGE), jnp.float32),
            pltpu.VMEM((TILE, EDGE), jnp.float32),
            pltpu.VMEM((8, EDGE), jnp.int32),
            pltpu.VMEM((8, EDGE), jnp.float32),
            pltpu.VMEM((8, EDGE), jnp.float32),
            pltpu.VMEM((TILE, 128), jnp.float32),
            pltpu.VMEM((TILE, 128), jnp.float32),
            pltpu.VMEM((TILE, 128), jnp.float32),
        ],
        compiler_params=pltpu.CompilerParams(vmem_limit_bytes=28 * 1024 * 1024),
        cost_estimate=pl.CostEstimate(
            flops=2 * EDGE * EDGE * WIDTH, bytes_accessed=4 * EDGE * WIDTH, transcendentals=EDGE * EDGE
        ),
        name="pair_sums",
    )(place, *seq_blocks, struct_blocks)


def over_z(block):
    found = {0: block, 1: shifted(block, "z", 1), 7: shifted(block, "z", -1)}
    found[2], found[6] = shifted(found[1], "z", 1), shifted(found[7], "z", -1)
    found[3], found[5] = shifted(found[2], "z", 1), shifted(found[6], "z", -1)
    found[4] = shifted(found[3], "z", 1)
    return [found[place] for place in range(8)]


def per_device(struct_feats, seq_feats, struct_proj, seq_proj, cluster_ids, hard_owner, hard_local, hard_valid):
    place = lambda axes: lax.axis_index(axes).astype(jnp.int32)
    core, yl = place("core"), place("yl")
    keep_s, send_s = project(core.reshape(1), struct_feats, struct_proj, False, "project_struct")
    got_s = shifted(send_s, "core", 1)
    keep_q, send_q = project(core.reshape(1), seq_feats.T, seq_proj, True, "project_seq")
    got_q = shifted(send_q, "core", 1)

    keep2_s, send2_s = merge(yl.reshape(1), keep_s, got_s, "merge_struct")
    got2_s = shifted(send2_s, "yl", 1)
    keep2_q, send2_q = merge(yl.reshape(1), keep_q, got_q, "merge_seq")
    cluster_ids, hard_owner, hard_local, hard_valid, send2_q = lax.optimization_barrier(
        (cluster_ids, hard_owner, hard_local, hard_valid, send2_q)
    )
    got2_q = shifted(send2_q, "yl", 1)
    own = lambda value: lax.dynamic_slice_in_dim(value, place(MP_AXES) * SHARE, SHARE, 0)
    labels = own(cluster_ids)
    owner = own(hard_owner[:, :, 0])
    local = own(hard_local)
    block = (owner >> 3) * 2 + ((local >> 7) & 1)
    chunk = (owner & 7) * 2 + (local >> 8)
    high = jnp.where(hard_valid > 0, block * 16 + chunk, -1).T
    low = (local & 127).T
    wide = lambda value: jnp.broadcast_to(value[None], (EXT, SHARE))
    seq_ext = jnp.concatenate([high, low, wide(labels >> 7), wide(labels & 127)], axis=1).astype(jnp.bfloat16)
    struct_ext = jnp.concatenate([wide(labels >> 7)[0:8], wide(labels & 127)[0:8]], axis=0).astype(jnp.bfloat16)

    own_struct, struct_peers = finish_struct(keep2_s, got2_s, struct_ext)
    struct_blocks = lax.all_to_all(struct_peers, COL_AXES, split_axis=0, concat_axis=0, tiled=True)
    seq_block, self_dot = finish_seq(keep2_q, got2_q, seq_ext, own_struct)
    seq_blocks = [each for held in over_z(seq_block) for each in (held, shifted(held, "core", 1))]

    rows, cols = pair_sums(jnp.stack([place("z"), core]), seq_blocks, struct_blocks)
    rows = jnp.sum(lax.all_to_all(rows, "z", split_axis=0, concat_axis=0, tiled=True), axis=0)
    cols = jnp.sum(lax.all_to_all(cols, COL_AXES, split_axis=0, concat_axis=0, tiled=True), axis=0)
    rows = lax.all_gather(rows, MP_AXES, axis=0, tiled=False).reshape(2, 2, 8, SHARE)
    rows = jnp.sum(rows, axis=1)[:, 0:6].reshape(2, 2, 3, SHARE)

    seq_loss = (jnp.log(rows[:, :, 0]) - jnp.log(rows[:, :, 1])).reshape(4 * SHARE)
    struct_loss = jnp.log(cols[0]) - jnp.log(cols[1])
    self_logits = LOGIT_SCALE * self_dot[0]
    extra = rows[:, :, 2].reshape(4, SHARE)[place(MP_AXES)]
    hard_loss = jnp.log(jnp.exp(self_logits) + extra) - self_logits
    return (seq_loss, struct_loss, hard_loss)


def solution(mesh):
    fine = Mesh(mesh.devices.reshape(8, 2, 4, 2, 2), ("z", "yh", "x", "yl", "core"))
    blk = ("z", "yh", "x")
    both = blk + MP_AXES
    placed = (
        P(blk, MP_AXES),
        P(blk, MP_AXES),
        P(MP_AXES, None),
        P(MP_AXES, None),
        P(blk),
        P(blk, None, None),
        P(blk, None),
        P(both, None),
    )
    return jax.shard_map(
        per_device,
        mesh=fine,
        in_specs=placed,
        out_specs=(P(blk), P(both), P(both)),
        check_vma=False,
    )
```

```python
import functools
import math

import jax
import jax.numpy as jnp
from jax import lax
from jax.experimental import pallas as pl
from jax.experimental.pallas import tpu as pltpu
from jax.sharding import Mesh, PartitionSpec as P

LOGIT_SCALE = 14.285714285714286
EPSILON = 1e-06

SHARE = 128
SIDE = 16
EDGE = SHARE * SIDE
WIDTH = 512
SLOTS = 16
EXT = 16
TILE = 512
STRIP = 512
SUB = 32

COL_AXES = ("yh", "x", "yl")
MP_AXES = ("yl", "core")
SIZES = {"z": 8, "yh": 2, "x": 4, "yl": 2, "core": 2}

VMEM = pl.BlockSpec(memory_space=pltpu.VMEM)
SMEM = pl.BlockSpec(memory_space=pltpu.SMEM)
HBM = pl.BlockSpec(memory_space=pltpu.HBM)


def shifted(value, axes, steps):
    names = (axes,) if isinstance(axes, str) else axes
    count = math.prod(SIZES[name] for name in names)
    return lax.ppermute(value, axes, [((place + steps) % count, place) for place in range(count)])


def project_kernel(core_ref, feats_hbm, proj_hbm, keep_ref, send_ref, feats_ref, proj_ref, sems, *, turned):
    core = core_ref[0]
    copies = [
        pltpu.make_async_copy(feats_hbm, feats_ref, sems.at[0]),
        pltpu.make_async_copy(proj_hbm, proj_ref, sems.at[1]),
    ]
    for copy in copies:
        copy.start()
    for copy in copies:
        copy.wait()
    for out, which in ((send_ref, 1 - core), (keep_ref, core)):
        for half in range(2):
            rows = pl.ds(pl.multiple_of((half * 2 + which) * SHARE, SHARE), SHARE)
            feats, over = (feats_ref[:, rows], 0) if turned else (feats_ref[rows, :], 1)
            out[half] = lax.dot_general(
                feats, proj_ref[...], (((over,), (0,)), ((), ())), preferred_element_type=jnp.float32
            )


def project(core, feats, proj, turned, name):
    shape = jax.ShapeDtypeStruct((2, SHARE, WIDTH), jnp.float32)
    return pl.pallas_call(
        functools.partial(project_kernel, turned=turned),
        out_shape=(shape, shape),
        in_specs=[SMEM, HBM, HBM],
        out_specs=(VMEM, VMEM),
        scratch_shapes=[
            pltpu.VMEM(feats.shape, feats.dtype),
            pltpu.VMEM(proj.shape, proj.dtype),
            pltpu.SemaphoreType.DMA((2,)),
        ],
        compiler_params=pltpu.CompilerParams(vmem_limit_bytes=12 * 1024 * 1024),
        name=name,
    )(core, feats, proj)


def merge_kernel(yl_ref, keep_ref, got_ref, keep2_ref, send2_ref):
    yl = yl_ref[0]
    send2_ref[...] = (keep_ref[1 - yl] + got_ref[1 - yl]).astype(jnp.bfloat16)
    keep2_ref[...] = keep_ref[yl] + got_ref[yl]


def merge(yl, keep, got, name):
    return pl.pallas_call(
        merge_kernel,
        out_shape=(
            jax.ShapeDtypeStruct((SHARE, WIDTH), jnp.float32),
            jax.ShapeDtypeStruct((SHARE, WIDTH), jnp.bfloat16),
        ),
        in_specs=[SMEM, VMEM, VMEM],
        out_specs=(VMEM, VMEM),
        compiler_params=pltpu.CompilerParams(vmem_limit_bytes=12 * 1024 * 1024),
        name=name,
    )(yl, keep, got)


def lanes_summed(values):
    return lax.dot_general(
        jnp.ones((8, values.shape[1]), jnp.float32),
        values,
        (((1,), (1,)), ((), ())),
        precision=lax.Precision.HIGHEST,
        preferred_element_type=jnp.float32,
    )


def normalized(keep2_ref, got2_ref):
    raw = keep2_ref[...] + got2_ref[...].astype(jnp.float32)
    total = jnp.sum(raw * raw, axis=1, keepdims=True)
    return (raw * lax.rsqrt(total + EPSILON)).astype(jnp.bfloat16)


def finish_kernel(keep2_s, got2_s, keep2_q, got2_q, struct_ext_ref, seq_ext_ref, peers_ref, seq_ref, self_ref):
    struct = normalized(keep2_s, got2_s)
    turned = struct.astype(jnp.float32).T.astype(jnp.bfloat16)
    struct_ext = struct_ext_ref[...]
    for peer in range(SIDE):
        peers_ref[peer, 0:WIDTH, :] = turned
        peers_ref[peer, WIDTH:, :] = struct_ext
    seq = normalized(keep2_q, got2_q)
    seq_ref[0:SHARE, :] = seq
    seq_ref[SHARE:, :] = seq_ext_ref[...]
    self_ref[...] = lanes_summed(seq.astype(jnp.float32) * struct.astype(jnp.float32))


def finish(*held):
    return pl.pallas_call(
        finish_kernel,
        out_shape=(
            jax.ShapeDtypeStruct((SIDE, WIDTH + EXT, SHARE), jnp.bfloat16),
            jax.ShapeDtypeStruct((SHARE + EXT, WIDTH), jnp.bfloat16),
            jax.ShapeDtypeStruct((8, SHARE), jnp.float32),
        ),
        in_specs=[VMEM] * 6,
        out_specs=(VMEM,) * 3,
        compiler_params=pltpu.CompilerParams(vmem_limit_bytes=12 * 1024 * 1024),
        name="finish",
    )(*held)


def integers(values):
    return values.astype(jnp.float32).astype(jnp.int32)


def pair_kernel(place_ref, *refs):
    seq_refs, s, rows_ref, cols_ref = refs[0:SIDE], refs[SIDE], refs[SIDE + 1], refs[SIDE + 2]
    q, info, buf0, buf1, lab8, ct, cm, rt, rm, ex = refs[SIDE + 3 :]
    tiles = EDGE // TILE
    strips = EDGE // STRIP
    part = TILE // strips
    buffers = (buf0, buf1)
    my_z, my_core = place_ref[0], place_ref[1]
    my_block = my_z * 2 + my_core

    for block in range(SIDE):
        at = slice(block * SHARE, (block + 1) * SHARE)
        q[at, :] = seq_refs[block][0:SHARE, :]
        ext = integers(seq_refs[block][SHARE:, :])
        high, low = ext[:, 0:SHARE], ext[:, SHARE : 2 * SHARE]
        label = ext[:, 2 * SHARE : 3 * SHARE] * 128 + ext[:, 3 * SHARE :]
        code = jnp.where((high >> 4) == my_block, (high & 15) * 128 + low, -1)
        whole = jnp.concatenate(
            [code, -1 - label, jnp.full((128 - 2 * EXT, SHARE), -1, jnp.int32)], axis=0
        ).astype(jnp.float32)
        info[at, :] = whole.T.astype(jnp.int32)
    for chunk in range(SIDE):
        labels = integers(s[chunk, WIDTH:, :])
        lab8[:, chunk * 128 : (chunk + 1) * 128] = labels[0:8] * 128 + labels[8:16]
    ct[...] = jnp.zeros_like(ct)
    cm[...] = jnp.zeros_like(cm)
    row_of = lax.broadcasted_iota(jnp.int32, (8, SHARE), 0)

    for tile in range(tiles + 1):

        def body(step, carry, tile=tile):
            if tile < tiles:
                wide = STRIP // SHARE
                cols = jnp.concatenate([s[step * wide + each, 0:WIDTH, :] for each in range(wide)], axis=1)
                start = pl.multiple_of(step * STRIP, STRIP)
                buffers[tile % 2][:, pl.ds(start, STRIP)] = lax.dot_general(
                    q[tile * TILE : (tile + 1) * TILE, :],
                    cols,
                    (((1,), (0,)), ((), ())),
                    preferred_element_type=jnp.float32,
                )
            if tile > 0:
                products = buffers[(tile - 1) % 2]
                zero = jnp.zeros((8, 128), jnp.float32)
                groups = range(SUB // 8)
                for sub in range(part // SUB):
                    local = [pl.multiple_of(step * part + sub * SUB + group * 8, 8) for group in groups]
                    code = [info[pl.ds(pl.multiple_of((tile - 1) * TILE + each, 8), 8), :] for each in local]
                    label = [jnp.broadcast_to(-1 - each[:, SLOTS : SLOTS + 1], (8, 128)) for each in code]
                    lane = [each & 127 for each in code]
                    chunk_of = [each >> 7 for each in code]
                    row_total, row_matched, picked = [zero for _ in groups], [zero for _ in groups], [zero for _ in groups]
                    for chunk in range(SIDE):
                        at = slice(chunk * 128, (chunk + 1) * 128)
                        col_label = lab8[:, at]
                        col_total, col_matched = ct[:, at], cm[:, at]
                        for group in groups:
                            product = products[pl.ds(local[group], 8), at]
                            expo = jnp.exp(product * LOGIT_SCALE)
                            kept = jnp.where(label[group] == col_label, expo, 0.0)
                            row_total[group] += expo
                            row_matched[group] += kept
                            col_total += expo
                            col_matched += kept
                            found = jnp.take_along_axis(expo, lane[group], axis=1, mode="promise_in_bounds")
                            picked[group] = jnp.where(chunk_of[group] == chunk, found, picked[group])
                        ct[:, at] = col_total
                        cm[:, at] = col_matched
                    for group in groups:
                        rt[pl.ds(local[group], 8), :] = row_total[group]
                        rm[pl.ds(local[group], 8), :] = row_matched[group]
                        ex[pl.ds(local[group], 8), :] = picked[group]
            return carry

        lax.fori_loop(0, strips, body, 0)
        if tile > 0:
            sums = [lanes_summed(each[...]) for each in (rt, rm, ex)]
            for inner in range(TILE // SHARE):
                block = (tile - 1) * (TILE // SHARE) + inner
                at = slice(inner * SHARE, (inner + 1) * SHARE)
                z, first = (my_z + block // 2) & 7, (my_core ^ (block % 2)) * 3
                out = jnp.zeros((8, SHARE), jnp.float32) if block % 2 == 0 else rows_ref[z]
                for which in range(3):
                    out = jnp.where(row_of == first + which, sums[which][:, at], out)
                rows_ref[z] = out

    for chunk in range(SIDE):
        at = slice(chunk * 128, (chunk + 1) * 128)
        total = jnp.sum(ct[:, at], axis=0, keepdims=True)
        matched = jnp.sum(cm[:, at], axis=0, keepdims=True)
        cols_ref[chunk] = jnp.where(row_of == 6, total, jnp.where(row_of == 7, matched, 0.0))


def pair_sums(place, seq_blocks, struct_blocks):
    return pl.pallas_call(
        pair_kernel,
        out_shape=(
            jax.ShapeDtypeStruct((8, 8, SHARE), jnp.float32),
            jax.ShapeDtypeStruct((SIDE, 8, SHARE), jnp.float32),
        ),
        in_specs=[SMEM] + [VMEM] * (SIDE + 1),
        out_specs=(VMEM, VMEM),
        scratch_shapes=[
            pltpu.VMEM((EDGE, WIDTH), jnp.bfloat16),
            pltpu.VMEM((EDGE, 128), jnp.int32),
            pltpu.VMEM((TILE, EDGE), jnp.float32),
            pltpu.VMEM((TILE, EDGE), jnp.float32),
            pltpu.VMEM((8, EDGE), jnp.int32),
            pltpu.VMEM((8, EDGE), jnp.float32),
            pltpu.VMEM((8, EDGE), jnp.float32),
            pltpu.VMEM((TILE, 128), jnp.float32),
            pltpu.VMEM((TILE, 128), jnp.float32),
            pltpu.VMEM((TILE, 128), jnp.float32),
        ],
        compiler_params=pltpu.CompilerParams(vmem_limit_bytes=28 * 1024 * 1024),
        cost_estimate=pl.CostEstimate(
            flops=2 * EDGE * EDGE * WIDTH, bytes_accessed=4 * EDGE * WIDTH, transcendentals=EDGE * EDGE
        ),
        name="pair_sums",
    )(place, *seq_blocks, struct_blocks)


def over_z(block):
    found = {0: block, 1: shifted(block, "z", 1), 7: shifted(block, "z", -1)}
    found[2], found[6] = shifted(found[1], "z", 1), shifted(found[7], "z", -1)
    found[3], found[5] = shifted(found[2], "z", 1), shifted(found[6], "z", -1)
    found[4] = shifted(found[3], "z", 1)
    return [found[place] for place in range(8)]


def per_device(struct_feats, seq_feats, struct_proj, seq_proj, cluster_ids, hard_owner, hard_local, hard_valid):
    place = lambda axes: lax.axis_index(axes).astype(jnp.int32)
    core, yl = place("core"), place("yl")
    keep_s, send_s = project(core.reshape(1), struct_feats, struct_proj, False, "project_struct")
    got_s = shifted(send_s, "core", 1)
    keep_q, send_q = project(core.reshape(1), seq_feats.T, seq_proj, True, "project_seq")
    got_q = shifted(send_q, "core", 1)

    keep2_s, send2_s = merge(yl.reshape(1), keep_s, got_s, "merge_struct")
    got2_s = shifted(send2_s, "yl", 1)
    keep2_q, send2_q = merge(yl.reshape(1), keep_q, got_q, "merge_seq")
    got2_q = shifted(send2_q, "yl", 1)
    cluster_ids, hard_owner, hard_local, hard_valid, send2_q = lax.optimization_barrier(
        (cluster_ids, hard_owner, hard_local, hard_valid, send2_q)
    )
    own = lambda value: lax.dynamic_slice_in_dim(value, place(MP_AXES) * SHARE, SHARE, 0)
    labels = own(cluster_ids)
    owner = own(hard_owner[:, :, 0])
    local = own(hard_local)
    block = (owner >> 3) * 2 + ((local >> 7) & 1)
    chunk = (owner & 7) * 2 + (local >> 8)
    high = jnp.where(hard_valid > 0, block * 16 + chunk, -1).T
    low = (local & 127).T
    wide = lambda value: jnp.broadcast_to(value[None], (EXT, SHARE))
    seq_ext = jnp.concatenate([high, low, wide(labels >> 7), wide(labels & 127)], axis=1).astype(jnp.bfloat16)
    struct_ext = jnp.concatenate([wide(labels >> 7)[0:8], wide(labels & 127)[0:8]], axis=0).astype(jnp.bfloat16)

    struct_peers, seq_block, self_dot = finish(keep2_s, got2_s, keep2_q, got2_q, struct_ext, seq_ext)
    struct_blocks = lax.all_to_all(struct_peers, COL_AXES, split_axis=0, concat_axis=0, tiled=True)
    seq_blocks = [each for held in over_z(seq_block) for each in (held, shifted(held, "core", 1))]

    rows, cols = pair_sums(jnp.stack([place("z"), core]), seq_blocks, struct_blocks)
    rows = jnp.sum(lax.all_to_all(rows, "z", split_axis=0, concat_axis=0, tiled=True), axis=0)
    rows = rows + shifted(rows, "core", 1)
    sums = lax.all_to_all(cols + rows[None], COL_AXES, split_axis=0, concat_axis=0, tiled=True)
    cols = jnp.sum(sums[:, 6:8], axis=0)
    rows = lax.dynamic_slice_in_dim(sums, (place("yh") * 4 + place("x")) * 2, 2, 0)[:, 0:6].reshape(2, 2, 3, SHARE)

    seq_loss = (jnp.log(rows[:, :, 0]) - jnp.log(rows[:, :, 1])).reshape(4 * SHARE)
    struct_loss = jnp.log(cols[0]) - jnp.log(cols[1])
    self_logits = LOGIT_SCALE * self_dot[0]
    extra = rows[:, :, 2].reshape(4, SHARE)[place(MP_AXES)]
    hard_loss = jnp.log(jnp.exp(self_logits) + extra) - self_logits
    return (seq_loss, struct_loss, hard_loss)


def solution(mesh):
    fine = Mesh(mesh.devices.reshape(8, 2, 4, 2, 2), ("z", "yh", "x", "yl", "core"))
    blk = ("z", "yh", "x")
    both = blk + MP_AXES
    placed = (
        P(blk, MP_AXES),
        P(blk, MP_AXES),
        P(MP_AXES, None),
        P(MP_AXES, None),
        P(blk),
        P(blk, None, None),
        P(blk, None),
        P(both, None),
    )
    return jax.shard_map(
        per_device,
        mesh=fine,
        in_specs=placed,
        out_specs=(P(blk), P(both), P(both)),
        check_vma=False,
    )
```

```python
import functools
import math

import jax
import jax.numpy as jnp
from jax import lax
from jax.experimental import pallas as pl
from jax.experimental.pallas import tpu as pltpu
from jax.sharding import Mesh, PartitionSpec as P

LOGIT_SCALE = 14.285714285714286
EPSILON = 1e-06

SHARE = 128
SIDE = 16
EDGE = SHARE * SIDE
WIDTH = 512
SLOTS = 16
EXT = 16
SUB = 32

COL_AXES = ("yh", "x", "yl")
MP_AXES = ("yl", "core")
SIZES = {"z": 8, "yh": 2, "x": 4, "yl": 2, "core": 2}

VMEM = pl.BlockSpec(memory_space=pltpu.VMEM)
SMEM = pl.BlockSpec(memory_space=pltpu.SMEM)
HBM = pl.BlockSpec(memory_space=pltpu.HBM)


def shifted(value, axes, steps):
    names = (axes,) if isinstance(axes, str) else axes
    count = math.prod(SIZES[name] for name in names)
    return lax.ppermute(value, axes, [((place + steps) % count, place) for place in range(count)])


def project_kernel(core_ref, feats_hbm, proj_hbm, keep_ref, send_ref, feats_ref, proj_ref, sems, *, turned):
    core = core_ref[0]
    copies = [
        pltpu.make_async_copy(feats_hbm, feats_ref, sems.at[0]),
        pltpu.make_async_copy(proj_hbm, proj_ref, sems.at[1]),
    ]
    for copy in copies:
        copy.start()
    for copy in copies:
        copy.wait()
    for out, which in ((send_ref, 1 - core), (keep_ref, core)):
        for half in range(2):
            rows = pl.ds(pl.multiple_of((half * 2 + which) * SHARE, SHARE), SHARE)
            feats, over = (feats_ref[:, rows], 0) if turned else (feats_ref[rows, :], 1)
            out[half] = lax.dot_general(
                feats, proj_ref[...], (((over,), (0,)), ((), ())), preferred_element_type=jnp.float32
            )


def project(core, feats, proj, turned, name):
    shape = jax.ShapeDtypeStruct((2, SHARE, WIDTH), jnp.float32)
    return pl.pallas_call(
        functools.partial(project_kernel, turned=turned),
        out_shape=(shape, shape),
        in_specs=[SMEM, HBM, HBM],
        out_specs=(VMEM, VMEM),
        scratch_shapes=[
            pltpu.VMEM(feats.shape, feats.dtype),
            pltpu.VMEM(proj.shape, proj.dtype),
            pltpu.SemaphoreType.DMA((2,)),
        ],
        compiler_params=pltpu.CompilerParams(vmem_limit_bytes=12 * 1024 * 1024),
        name=name,
    )(core, feats, proj)


def merge_kernel(yl_ref, keep_ref, got_ref, keep2_ref, send2_ref):
    yl = yl_ref[0]
    send2_ref[...] = (keep_ref[1 - yl] + got_ref[1 - yl]).astype(jnp.bfloat16)
    keep2_ref[...] = keep_ref[yl] + got_ref[yl]


def merge(yl, keep, got, name):
    return pl.pallas_call(
        merge_kernel,
        out_shape=(
            jax.ShapeDtypeStruct((SHARE, WIDTH), jnp.float32),
            jax.ShapeDtypeStruct((SHARE, WIDTH), jnp.bfloat16),
        ),
        in_specs=[SMEM, VMEM, VMEM],
        out_specs=(VMEM, VMEM),
        compiler_params=pltpu.CompilerParams(vmem_limit_bytes=12 * 1024 * 1024),
        name=name,
    )(yl, keep, got)


def lanes_summed(values):
    return lax.dot_general(
        jnp.ones((8, values.shape[1]), jnp.float32),
        values,
        (((1,), (1,)), ((), ())),
        precision=lax.Precision.HIGHEST,
        preferred_element_type=jnp.float32,
    )


def normalized(keep2_ref, got2_ref):
    raw = keep2_ref[...] + got2_ref[...].astype(jnp.float32)
    total = jnp.sum(raw * raw, axis=1, keepdims=True)
    return (raw * lax.rsqrt(total + EPSILON)).astype(jnp.bfloat16)


def finish_kernel(keep2_s, got2_s, keep2_q, got2_q, struct_ext_ref, seq_ext_ref, peers_ref, seq_ref, self_ref):
    struct = normalized(keep2_s, got2_s)
    turned = struct.astype(jnp.float32).T.astype(jnp.bfloat16)
    struct_ext = struct_ext_ref[...]
    for peer in range(SIDE):
        peers_ref[peer, 0:WIDTH, :] = turned
        peers_ref[peer, WIDTH:, :] = struct_ext
    seq = normalized(keep2_q, got2_q)
    seq_ref[0:SHARE, :] = seq
    seq_ref[SHARE:, :] = seq_ext_ref[...]
    self_ref[...] = lanes_summed(seq.astype(jnp.float32) * struct.astype(jnp.float32))


def finish(*held):
    return pl.pallas_call(
        finish_kernel,
        out_shape=(
            jax.ShapeDtypeStruct((SIDE, WIDTH + EXT, SHARE), jnp.bfloat16),
            jax.ShapeDtypeStruct((SHARE + EXT, WIDTH), jnp.bfloat16),
            jax.ShapeDtypeStruct((8, SHARE), jnp.float32),
        ),
        in_specs=[VMEM] * 6,
        out_specs=(VMEM,) * 3,
        compiler_params=pltpu.CompilerParams(vmem_limit_bytes=12 * 1024 * 1024),
        name="finish",
    )(*held)


def integers(values):
    return values.astype(jnp.float32).astype(jnp.int32)


def pair_kernel(place_ref, *refs):
    seq_refs, s, rows_ref, cols_ref = refs[0:SIDE], refs[SIDE], refs[SIDE + 1], refs[SIDE + 2]
    q, info, buf0, buf1, lab8, ct, cm, rt, rm, ex = refs[SIDE + 3 :]
    my_z, my_core = place_ref[0], place_ref[1]
    my_block = my_z * 2 + my_core

    for block in range(SIDE):
        at = slice(block * SHARE, (block + 1) * SHARE)
        q[at, :] = seq_refs[block][0:SHARE, :]
        ext = integers(seq_refs[block][SHARE:, :])
        high, low = ext[:, 0:SHARE], ext[:, SHARE : 2 * SHARE]
        label = ext[:, 2 * SHARE : 3 * SHARE] * 128 + ext[:, 3 * SHARE :]
        code = jnp.where((high >> 4) == my_block, (high & 15) * 128 + low, -1)
        whole = jnp.concatenate(
            [code, -1 - label, jnp.full((128 - 2 * EXT, SHARE), -1, jnp.int32)], axis=0
        ).astype(jnp.float32)
        info[at, :] = whole.T.astype(jnp.int32)
    for chunk in range(SIDE):
        labels = integers(s[chunk, WIDTH:, :])
        lab8[:, chunk * 128 : (chunk + 1) * 128] = labels[0:8] * 128 + labels[8:16]
    ct[...] = jnp.zeros_like(ct)
    cm[...] = jnp.zeros_like(cm)
    row_of = lax.broadcasted_iota(jnp.int32, (8, SHARE), 0)

    zero = jnp.zeros((8, 128), jnp.float32)
    groups = range(SUB // 8)

    def piece(tile, target, pair):
        cols = jnp.concatenate([s[2 * pair, 0:WIDTH, :], s[2 * pair + 1, 0:WIDTH, :]], axis=1)
        rows = pl.ds(pl.multiple_of(tile * SHARE, SHARE), SHARE)
        target[:, 2 * pair * SHARE : 2 * (pair + 1) * SHARE] = jnp.dot(
            q[rows, :], cols, preferred_element_type=jnp.float32
        )

    def work(tile, products, next_tile, target):
        for sub in range(SHARE // SUB):
            here = [pl.ds(pl.multiple_of(tile * SHARE + sub * SUB + group * 8, 8), 8) for group in groups]
            code = [info[rows, :] for rows in here]
            label = [jnp.broadcast_to(-1 - each[:, SLOTS : SLOTS + 1], (8, 128)) for each in code]
            lane = [each & 127 for each in code]
            chunk_of = [each >> 7 for each in code]
            row_total, row_matched, picked = [zero for _ in groups], [zero for _ in groups], [zero for _ in groups]
            for chunk in range(SIDE):
                if chunk % 8 == 0:
                    piece(next_tile, target, sub * 2 + chunk // 8)
                at = slice(chunk * 128, (chunk + 1) * 128)
                col_label = lab8[:, at]
                col_total, col_matched = ct[:, at], cm[:, at]
                for group in groups:
                    local = sub * SUB + group * 8
                    expo = jnp.exp(products[local : local + 8, at] * LOGIT_SCALE)
                    kept = jnp.where(label[group] == col_label, expo, 0.0)
                    row_total[group] += expo
                    row_matched[group] += kept
                    col_total += expo
                    col_matched += kept
                    found = jnp.take_along_axis(expo, lane[group], axis=1, mode="promise_in_bounds")
                    picked[group] = jnp.where(chunk_of[group] == chunk, found, picked[group])
                ct[:, at] = col_total
                cm[:, at] = col_matched
            for group in groups:
                rt[here[group], :] = row_total[group]
                rm[here[group], :] = row_matched[group]
                ex[here[group], :] = picked[group]

    for pair in range(SIDE // 2):
        piece(0, buf0, pair)

    def body(step, carry):
        work(2 * step, buf0, 2 * step + 1, buf1)
        work(2 * step + 1, buf1, jnp.minimum(2 * step + 2, SIDE - 1), buf0)
        return carry

    lax.fori_loop(0, SIDE // 2, body, 0)
    for part in range(4):
        at = slice(part * 4 * SHARE, (part + 1) * 4 * SHARE)
        sums = [lanes_summed(each[at, :]) for each in (rt, rm, ex)]
        for inner in range(4):
            block = part * 4 + inner
            at = slice(inner * SHARE, (inner + 1) * SHARE)
            z, first = (my_z + block // 2) & 7, (my_core ^ (block % 2)) * 3
            out = jnp.zeros((8, SHARE), jnp.float32) if block % 2 == 0 else rows_ref[z]
            for which in range(3):
                out = jnp.where(row_of == first + which, sums[which][:, at], out)
            rows_ref[z] = out

    for chunk in range(SIDE):
        at = slice(chunk * 128, (chunk + 1) * 128)
        total = jnp.sum(ct[:, at], axis=0, keepdims=True)
        matched = jnp.sum(cm[:, at], axis=0, keepdims=True)
        cols_ref[chunk] = jnp.where(row_of == 0, total, matched)


def pair_sums(place, seq_blocks, struct_blocks):
    return pl.pallas_call(
        pair_kernel,
        out_shape=(
            jax.ShapeDtypeStruct((8, 8, SHARE), jnp.float32),
            jax.ShapeDtypeStruct((SIDE, 8, SHARE), jnp.float32),
        ),
        in_specs=[SMEM] + [VMEM] * (SIDE + 1),
        out_specs=(VMEM, VMEM),
        scratch_shapes=[
            pltpu.VMEM((EDGE, WIDTH), jnp.bfloat16),
            pltpu.VMEM((EDGE, 128), jnp.int32),
            pltpu.VMEM((SHARE, EDGE), jnp.float32),
            pltpu.VMEM((SHARE, EDGE), jnp.float32),
            pltpu.VMEM((8, EDGE), jnp.int32),
            pltpu.VMEM((8, EDGE), jnp.float32),
            pltpu.VMEM((8, EDGE), jnp.float32),
            pltpu.VMEM((EDGE, 128), jnp.float32),
            pltpu.VMEM((EDGE, 128), jnp.float32),
            pltpu.VMEM((EDGE, 128), jnp.float32),
        ],
        compiler_params=pltpu.CompilerParams(vmem_limit_bytes=28 * 1024 * 1024),
        cost_estimate=pl.CostEstimate(
            flops=2 * EDGE * EDGE * WIDTH, bytes_accessed=4 * EDGE * WIDTH, transcendentals=EDGE * EDGE
        ),
        name="pair_sums",
    )(place, *seq_blocks, struct_blocks)


def over_z(block):
    found = {0: block, 1: shifted(block, "z", 1), 7: shifted(block, "z", -1)}
    found[2], found[6] = shifted(found[1], "z", 1), shifted(found[7], "z", -1)
    found[3], found[5] = shifted(found[2], "z", 1), shifted(found[6], "z", -1)
    found[4] = shifted(found[3], "z", 1)
    return [found[place] for place in range(8)]


def per_device(struct_feats, seq_feats, struct_proj, seq_proj, cluster_ids, hard_owner, hard_local, hard_valid):
    place = lambda axes: lax.axis_index(axes).astype(jnp.int32)
    core, yl = place("core"), place("yl")
    keep_s, send_s = project(core.reshape(1), struct_feats, struct_proj, False, "project_struct")
    got_s = shifted(send_s, "core", 1)
    keep_q, send_q = project(core.reshape(1), seq_feats.T, seq_proj, True, "project_seq")
    got_q = shifted(send_q, "core", 1)

    keep2_s, send2_s = merge(yl.reshape(1), keep_s, got_s, "merge_struct")
    got2_s = shifted(send2_s, "yl", 1)
    keep2_q, send2_q = merge(yl.reshape(1), keep_q, got_q, "merge_seq")
    got2_q = shifted(send2_q, "yl", 1)
    cluster_ids, hard_owner, hard_local, hard_valid, send2_q = lax.optimization_barrier(
        (cluster_ids, hard_owner, hard_local, hard_valid, send2_q)
    )
    own = lambda value: lax.dynamic_slice_in_dim(value, place(MP_AXES) * SHARE, SHARE, 0)
    labels = own(cluster_ids)
    owner = own(hard_owner[:, :, 0])
    local = own(hard_local)
    block = (owner >> 3) * 2 + ((local >> 7) & 1)
    chunk = (owner & 7) * 2 + (local >> 8)
    high = jnp.where(hard_valid > 0, block * 16 + chunk, -1).T
    low = (local & 127).T
    wide = lambda value: jnp.broadcast_to(value[None], (EXT, SHARE))
    seq_ext = jnp.concatenate([high, low, wide(labels >> 7), wide(labels & 127)], axis=1).astype(jnp.bfloat16)
    struct_ext = jnp.concatenate([wide(labels >> 7)[0:8], wide(labels & 127)[0:8]], axis=0).astype(jnp.bfloat16)

    struct_peers, seq_block, self_dot = finish(keep2_s, got2_s, keep2_q, got2_q, struct_ext, seq_ext)
    struct_blocks = lax.all_to_all(struct_peers, COL_AXES, split_axis=0, concat_axis=0, tiled=True)
    seq_blocks = [each for held in over_z(seq_block) for each in (held, shifted(held, "core", 1))]

    rows, cols = pair_sums(jnp.stack([place("z"), core]), seq_blocks, struct_blocks)
    rows = jnp.sum(lax.all_to_all(rows, "z", split_axis=0, concat_axis=0, tiled=True), axis=0)
    cols = jnp.sum(lax.all_to_all(cols, COL_AXES, split_axis=0, concat_axis=0, tiled=True), axis=0)
    rows = lax.all_gather(rows, MP_AXES, axis=0, tiled=False).reshape(2, 2, 8, SHARE)
    rows = jnp.sum(rows, axis=1)[:, 0:6].reshape(2, 2, 3, SHARE)

    seq_loss = (jnp.log(rows[:, :, 0]) - jnp.log(rows[:, :, 1])).reshape(4 * SHARE)
    struct_loss = jnp.log(cols[0]) - jnp.log(cols[1])
    self_logits = LOGIT_SCALE * self_dot[0]
    extra = rows[:, :, 2].reshape(4, SHARE)[place(MP_AXES)]
    hard_loss = jnp.log(jnp.exp(self_logits) + extra) - self_logits
    return (seq_loss, struct_loss, hard_loss)


def solution(mesh):
    fine = Mesh(mesh.devices.reshape(8, 2, 4, 2, 2), ("z", "yh", "x", "yl", "core"))
    blk = ("z", "yh", "x")
    both = blk + MP_AXES
    placed = (
        P(blk, MP_AXES),
        P(blk, MP_AXES),
        P(MP_AXES, None),
        P(MP_AXES, None),
        P(blk),
        P(blk, None, None),
        P(blk, None),
        P(both, None),
    )
    return jax.shard_map(
        per_device,
        mesh=fine,
        in_specs=placed,
        out_specs=(P(blk), P(both), P(both)),
        check_vma=False,
    )
```

```python
import functools
import math

import jax
import jax.numpy as jnp
from jax import lax
from jax.experimental import pallas as pl
from jax.experimental.pallas import tpu as pltpu
from jax.sharding import Mesh, PartitionSpec as P

LOGIT_SCALE = 14.285714285714286
EPSILON = 1e-06

SHARE = 128
SIDE = 16
EDGE = SHARE * SIDE
WIDTH = 512
SLOTS = 16
EXT = 16
FIXED = 32000.0
SUB = 32

COL_AXES = ("yh", "x", "yl")
MP_AXES = ("yl", "core")
SIZES = {"z": 8, "yh": 2, "x": 4, "yl": 2, "core": 2}

VMEM = pl.BlockSpec(memory_space=pltpu.VMEM)
SMEM = pl.BlockSpec(memory_space=pltpu.SMEM)
HBM = pl.BlockSpec(memory_space=pltpu.HBM)


def shifted(value, axes, steps):
    names = (axes,) if isinstance(axes, str) else axes
    count = math.prod(SIZES[name] for name in names)
    return lax.ppermute(value, axes, [((place + steps) % count, place) for place in range(count)])


def project_kernel(core_ref, feats_hbm, proj_hbm, keep_ref, send_ref, feats_ref, proj_ref, sems, *, turned):
    core = core_ref[0]
    copies = [
        pltpu.make_async_copy(feats_hbm, feats_ref, sems.at[0]),
        pltpu.make_async_copy(proj_hbm, proj_ref, sems.at[1]),
    ]
    for copy in copies:
        copy.start()
    for copy in copies:
        copy.wait()
    for out, which in ((send_ref, 1 - core), (keep_ref, core)):
        for half in range(2):
            rows = pl.ds(pl.multiple_of((half * 2 + which) * SHARE, SHARE), SHARE)
            feats, over = (feats_ref[:, rows], 0) if turned else (feats_ref[rows, :], 1)
            out[half] = lax.dot_general(
                feats, proj_ref[...], (((over,), (0,)), ((), ())), preferred_element_type=jnp.float32
            )


def project(core, feats, proj, turned, name):
    shape = jax.ShapeDtypeStruct((2, SHARE, WIDTH), jnp.float32)
    return pl.pallas_call(
        functools.partial(project_kernel, turned=turned),
        out_shape=(shape, shape),
        in_specs=[SMEM, HBM, HBM],
        out_specs=(VMEM, VMEM),
        scratch_shapes=[
            pltpu.VMEM(feats.shape, feats.dtype),
            pltpu.VMEM(proj.shape, proj.dtype),
            pltpu.SemaphoreType.DMA((2,)),
        ],
        compiler_params=pltpu.CompilerParams(vmem_limit_bytes=12 * 1024 * 1024),
        name=name,
    )(core, feats, proj)


def merge_kernel(yl_ref, keep_ref, got_ref, keep2_ref, send2_ref):
    yl = yl_ref[0]
    send2_ref[...] = (keep_ref[1 - yl] + got_ref[1 - yl]).astype(jnp.bfloat16)
    keep2_ref[...] = keep_ref[yl] + got_ref[yl]


def merge(yl, keep, got, name):
    return pl.pallas_call(
        merge_kernel,
        out_shape=(
            jax.ShapeDtypeStruct((SHARE, WIDTH), jnp.float32),
            jax.ShapeDtypeStruct((SHARE, WIDTH), jnp.bfloat16),
        ),
        in_specs=[SMEM, VMEM, VMEM],
        out_specs=(VMEM, VMEM),
        compiler_params=pltpu.CompilerParams(vmem_limit_bytes=12 * 1024 * 1024),
        name=name,
    )(yl, keep, got)


def lanes_summed(values):
    return lax.dot_general(
        jnp.ones((8, values.shape[1]), jnp.float32),
        values,
        (((1,), (1,)), ((), ())),
        precision=lax.Precision.HIGHEST,
        preferred_element_type=jnp.float32,
    )


def normalized(keep2_ref, got2_ref):
    raw = keep2_ref[...] + got2_ref[...].astype(jnp.float32)
    total = jnp.sum(raw * raw, axis=1, keepdims=True)
    return (raw * lax.rsqrt(total + EPSILON)).astype(jnp.bfloat16)


def finish_kernel(keep2_s, got2_s, keep2_q, got2_q, struct_ext_ref, seq_ext_ref, peers_ref, seq_ref, self_ref):
    struct = normalized(keep2_s, got2_s)
    turned = struct.astype(jnp.float32).T.astype(jnp.bfloat16)
    struct_ext = struct_ext_ref[...]
    for peer in range(SIDE):
        peers_ref[peer, 0:WIDTH, :] = turned
        peers_ref[peer, WIDTH:, :] = struct_ext
    seq = normalized(keep2_q, got2_q)
    seq_ref[0:SHARE, :] = seq
    seq_ref[SHARE:, :] = seq_ext_ref[...]
    self_ref[...] = lanes_summed(seq.astype(jnp.float32) * struct.astype(jnp.float32))


def finish(*held):
    return pl.pallas_call(
        finish_kernel,
        out_shape=(
            jax.ShapeDtypeStruct((SIDE, WIDTH + EXT, SHARE), jnp.bfloat16),
            jax.ShapeDtypeStruct((SHARE + EXT, WIDTH), jnp.bfloat16),
            jax.ShapeDtypeStruct((8, SHARE), jnp.float32),
        ),
        in_specs=[VMEM] * 6,
        out_specs=(VMEM,) * 3,
        compiler_params=pltpu.CompilerParams(vmem_limit_bytes=12 * 1024 * 1024),
        name="finish",
    )(*held)


def integers(values):
    return values.astype(jnp.float32).astype(jnp.int32)


def pair_kernel(place_ref, *refs):
    seq_refs, s, rows_ref, cols_ref = refs[0:SIDE], refs[SIDE], refs[SIDE + 1], refs[SIDE + 2]
    q, info, buf0, buf1, lab8, ct, cm, rt, rm, ex = refs[SIDE + 3 :]
    my_z, my_core = place_ref[0], place_ref[1]
    my_block = my_z * 2 + my_core

    for block in range(SIDE):
        at = slice(block * SHARE, (block + 1) * SHARE)
        q[at, :] = seq_refs[block][0:SHARE, :]
        ext = integers(seq_refs[block][SHARE:, :])
        high, low = ext[:, 0:SHARE], ext[:, SHARE : 2 * SHARE]
        label = ext[:, 2 * SHARE : 3 * SHARE] * 128 + ext[:, 3 * SHARE :]
        code = jnp.where((high >> 4) == my_block, (high & 15) * 128 + low, -1)
        info[at, :] = jnp.full((SHARE, 128), -1, jnp.int32)
        info[at, 0 : 2 * EXT] = jnp.concatenate([code, -1 - label], axis=0).astype(jnp.float32).T.astype(jnp.int32)
    for chunk in range(SIDE):
        labels = integers(s[chunk, WIDTH:, :])
        lab8[:, chunk * 128 : (chunk + 1) * 128] = labels[0:8] * 128 + labels[8:16]
    ct[...] = jnp.zeros_like(ct)
    cm[...] = jnp.zeros_like(cm)
    row_of = lax.broadcasted_iota(jnp.int32, (8, SHARE), 0)

    zero = jnp.zeros((8, 128), jnp.float32)
    groups = range(SUB // 8)

    def piece(tile, target, pair):
        cols = jnp.concatenate([s[2 * pair, 0:WIDTH, :], s[2 * pair + 1, 0:WIDTH, :]], axis=1)
        rows = pl.ds(pl.multiple_of(tile * SHARE, SHARE), SHARE)
        target[:, 2 * pair * SHARE : 2 * (pair + 1) * SHARE] = jnp.dot(
            q[rows, :], cols, preferred_element_type=jnp.float32
        )

    def work(tile, products, next_tile, target):
        for sub in range(SHARE // SUB):
            here = [pl.ds(pl.multiple_of(tile * SHARE + sub * SUB + group * 8, 8), 8) for group in groups]
            code = [info[rows, :] for rows in here]
            label = [jnp.broadcast_to(-1 - each[:, SLOTS : SLOTS + 1], (8, 128)) for each in code]
            lane = [each & 127 for each in code]
            pair_of = [each >> 8 for each in code]
            row_total, row_matched = [zero for _ in groups], [zero for _ in groups]
            picked = [jnp.zeros((8, 128), jnp.int32) for _ in groups]
            even = [None for _ in groups]
            for chunk in range(SIDE):
                if chunk % 8 == 0:
                    piece(next_tile, target, sub * 2 + chunk // 8)
                at = slice(chunk * 128, (chunk + 1) * 128)
                col_label = lab8[:, at]
                col_total, col_matched = ct[:, at], cm[:, at]
                for group in groups:
                    local = sub * SUB + group * 8
                    product = products[local : local + 8, at]
                    expo = jnp.exp(product * LOGIT_SCALE)
                    fixed = (product * FIXED).astype(jnp.int32)
                    kept = jnp.where(label[group] == col_label, expo, 0.0)
                    row_total[group] += expo
                    row_matched[group] += kept
                    col_total += expo
                    col_matched += kept
                    if chunk % 2 == 0:
                        even[group] = fixed
                    else:
                        both = (even[group] << 16) + fixed
                        found = jnp.take_along_axis(both, lane[group], axis=1, mode="promise_in_bounds")
                        picked[group] = jnp.where(pair_of[group] == chunk // 2, found, picked[group])
                ct[:, at] = col_total
                cm[:, at] = col_matched
            for group in groups:
                rt[here[group], :] = row_total[group]
                rm[here[group], :] = row_matched[group]
                odd = (picked[group] << 16) >> 16
                fixed = jnp.where((code[group] & 128) > 0, odd, (picked[group] - odd) >> 16).astype(jnp.float32)
                fixed = fixed + jnp.where(fixed > 0, 0.5, jnp.where(fixed < 0, -0.5, 0.0))
                hard = jnp.exp(fixed * (LOGIT_SCALE / FIXED))
                ex[here[group], :] = jnp.where(code[group] >= 0, hard, 0.0)

    for pair in range(SIDE // 2):
        piece(0, buf0, pair)

    def body(step, carry):
        work(2 * step, buf0, 2 * step + 1, buf1)
        work(2 * step + 1, buf1, jnp.minimum(2 * step + 2, SIDE - 1), buf0)
        return carry

    lax.fori_loop(0, SIDE // 2, body, 0)
    for part in range(4):
        at = slice(part * 4 * SHARE, (part + 1) * 4 * SHARE)
        sums = [lanes_summed(each[at, :]) for each in (rt, rm, ex)]
        for inner in range(4):
            block = part * 4 + inner
            at = slice(inner * SHARE, (inner + 1) * SHARE)
            z, first = (my_z + block // 2) & 7, (my_core ^ (block % 2)) * 3
            out = jnp.zeros((8, SHARE), jnp.float32) if block % 2 == 0 else rows_ref[z]
            for which in range(3):
                out = jnp.where(row_of == first + which, sums[which][:, at], out)
            rows_ref[z] = out

    for chunk in range(SIDE):
        at = slice(chunk * 128, (chunk + 1) * 128)
        total = jnp.sum(ct[:, at], axis=0, keepdims=True)
        matched = jnp.sum(cm[:, at], axis=0, keepdims=True)
        cols_ref[chunk] = jnp.where(row_of == 0, total, matched)


def pair_sums(place, seq_blocks, struct_blocks):
    return pl.pallas_call(
        pair_kernel,
        out_shape=(
            jax.ShapeDtypeStruct((8, 8, SHARE), jnp.float32),
            jax.ShapeDtypeStruct((SIDE, 8, SHARE), jnp.float32),
        ),
        in_specs=[SMEM] + [VMEM] * (SIDE + 1),
        out_specs=(VMEM, VMEM),
        scratch_shapes=[
            pltpu.VMEM((EDGE, WIDTH), jnp.bfloat16),
            pltpu.VMEM((EDGE, 128), jnp.int32),
            pltpu.VMEM((SHARE, EDGE), jnp.float32),
            pltpu.VMEM((SHARE, EDGE), jnp.float32),
            pltpu.VMEM((8, EDGE), jnp.int32),
            pltpu.VMEM((8, EDGE), jnp.float32),
            pltpu.VMEM((8, EDGE), jnp.float32),
            pltpu.VMEM((EDGE, 128), jnp.float32),
            pltpu.VMEM((EDGE, 128), jnp.float32),
            pltpu.VMEM((EDGE, 128), jnp.float32),
        ],
        compiler_params=pltpu.CompilerParams(vmem_limit_bytes=28 * 1024 * 1024),
        cost_estimate=pl.CostEstimate(
            flops=2 * EDGE * EDGE * WIDTH, bytes_accessed=4 * EDGE * WIDTH, transcendentals=EDGE * EDGE
        ),
        name="pair_sums",
    )(place, *seq_blocks, struct_blocks)


def over_z(block):
    found = {0: block, 1: shifted(block, "z", 1), 7: shifted(block, "z", -1)}
    found[2], found[6] = shifted(found[1], "z", 1), shifted(found[7], "z", -1)
    found[3], found[5] = shifted(found[2], "z", 1), shifted(found[6], "z", -1)
    found[4] = shifted(found[3], "z", 1)
    return [found[place] for place in range(8)]


def per_device(struct_feats, seq_feats, struct_proj, seq_proj, cluster_ids, hard_owner, hard_local, hard_valid):
    place = lambda axes: lax.axis_index(axes).astype(jnp.int32)
    core, yl = place("core"), place("yl")
    keep_s, send_s = project(core.reshape(1), struct_feats, struct_proj, False, "project_struct")
    got_s = shifted(send_s, "core", 1)
    keep_q, send_q = project(core.reshape(1), seq_feats.T, seq_proj, True, "project_seq")
    got_q = shifted(send_q, "core", 1)

    keep2_s, send2_s = merge(yl.reshape(1), keep_s, got_s, "merge_struct")
    got2_s = shifted(send2_s, "yl", 1)
    keep2_q, send2_q = merge(yl.reshape(1), keep_q, got_q, "merge_seq")
    got2_q = shifted(send2_q, "yl", 1)
    cluster_ids, hard_owner, hard_local, hard_valid, send2_q = lax.optimization_barrier(
        (cluster_ids, hard_owner, hard_local, hard_valid, send2_q)
    )
    own = lambda value: lax.dynamic_slice_in_dim(value, place(MP_AXES) * SHARE, SHARE, 0)
    labels = own(cluster_ids)
    owner = own(hard_owner[:, :, 0])
    local = own(hard_local)
    block = (owner >> 3) * 2 + ((local >> 7) & 1)
    chunk = (owner & 7) * 2 + (local >> 8)
    high = jnp.where(hard_valid > 0, block * 16 + chunk, -1).T
    low = (local & 127).T
    wide = lambda value: jnp.broadcast_to(value[None], (EXT, SHARE))
    seq_ext = jnp.concatenate([high, low, wide(labels >> 7), wide(labels & 127)], axis=1).astype(jnp.bfloat16)
    struct_ext = jnp.concatenate([wide(labels >> 7)[0:8], wide(labels & 127)[0:8]], axis=0).astype(jnp.bfloat16)

    struct_peers, seq_block, self_dot = finish(keep2_s, got2_s, keep2_q, got2_q, struct_ext, seq_ext)
    struct_blocks = lax.all_to_all(struct_peers, COL_AXES, split_axis=0, concat_axis=0, tiled=True)
    seq_blocks = [each for held in over_z(seq_block) for each in (held, shifted(held, "core", 1))]

    rows, cols = pair_sums(jnp.stack([place("z"), core]), seq_blocks, struct_blocks)
    rows = jnp.sum(lax.all_to_all(rows, "z", split_axis=0, concat_axis=0, tiled=True), axis=0)
    cols = jnp.sum(lax.all_to_all(cols, COL_AXES, split_axis=0, concat_axis=0, tiled=True), axis=0)
    rows = lax.all_gather(rows, MP_AXES, axis=0, tiled=False).reshape(2, 2, 8, SHARE)
    rows = jnp.sum(rows, axis=1)[:, 0:6].reshape(2, 2, 3, SHARE)

    seq_loss = (jnp.log(rows[:, :, 0]) - jnp.log(rows[:, :, 1])).reshape(4 * SHARE)
    struct_loss = jnp.log(cols[0]) - jnp.log(cols[1])
    self_logits = LOGIT_SCALE * self_dot[0]
    extra = rows[:, :, 2].reshape(4, SHARE)[place(MP_AXES)]
    hard_loss = jnp.log(jnp.exp(self_logits) + extra) - self_logits
    return (seq_loss, struct_loss, hard_loss)


def solution(mesh):
    fine = Mesh(mesh.devices.reshape(8, 2, 4, 2, 2), ("z", "yh", "x", "yl", "core"))
    blk = ("z", "yh", "x")
    both = blk + MP_AXES
    placed = (
        P(blk, MP_AXES),
        P(blk, MP_AXES),
        P(MP_AXES, None),
        P(MP_AXES, None),
        P(blk),
        P(blk, None, None),
        P(blk, None),
        P(both, None),
    )
    return jax.shard_map(
        per_device,
        mesh=fine,
        in_specs=placed,
        out_specs=(P(blk), P(both), P(both)),
        check_vma=False,
    )
```

```python
import functools
import math

import jax
import jax.numpy as jnp
from jax import lax
from jax.experimental import pallas as pl
from jax.experimental.pallas import tpu as pltpu
from jax.sharding import Mesh, PartitionSpec as P

LOGIT_SCALE = 14.285714285714286
EPSILON = 1e-06

SHARE = 128
SIDE = 16
EDGE = SHARE * SIDE
WIDTH = 512
SLOTS = 16
EXT = 16
FIXED = 32000.0
SUB = 32

COL_AXES = ("yh", "x", "yl")
MP_AXES = ("yl", "core")
SIZES = {"z": 8, "yh": 2, "x": 4, "yl": 2, "core": 2}

VMEM = pl.BlockSpec(memory_space=pltpu.VMEM)
SMEM = pl.BlockSpec(memory_space=pltpu.SMEM)
HBM = pl.BlockSpec(memory_space=pltpu.HBM)


def shifted(value, axes, steps):
    names = (axes,) if isinstance(axes, str) else axes
    count = math.prod(SIZES[name] for name in names)
    return lax.ppermute(value, axes, [((place + steps) % count, place) for place in range(count)])


def project_kernel(core_ref, feats_hbm, proj_hbm, keep_ref, send_ref, feats_ref, proj_ref, sems, *, turned):
    core = core_ref[0]
    copies = [
        pltpu.make_async_copy(feats_hbm, feats_ref, sems.at[0]),
        pltpu.make_async_copy(proj_hbm, proj_ref, sems.at[1]),
    ]
    for copy in copies:
        copy.start()
    for copy in copies:
        copy.wait()
    for out, which in ((send_ref, 1 - core), (keep_ref, core)):
        for half in range(2):
            rows = pl.ds(pl.multiple_of((half * 2 + which) * SHARE, SHARE), SHARE)
            feats, over = (feats_ref[:, rows], 0) if turned else (feats_ref[rows, :], 1)
            out[half] = lax.dot_general(
                feats, proj_ref[...], (((over,), (0,)), ((), ())), preferred_element_type=jnp.float32
            )


def project(core, feats, proj, turned, name):
    shape = jax.ShapeDtypeStruct((2, SHARE, WIDTH), jnp.float32)
    return pl.pallas_call(
        functools.partial(project_kernel, turned=turned),
        out_shape=(shape, shape),
        in_specs=[SMEM, HBM, HBM],
        out_specs=(VMEM, VMEM),
        scratch_shapes=[
            pltpu.VMEM(feats.shape, feats.dtype),
            pltpu.VMEM(proj.shape, proj.dtype),
            pltpu.SemaphoreType.DMA((2,)),
        ],
        compiler_params=pltpu.CompilerParams(vmem_limit_bytes=12 * 1024 * 1024),
        name=name,
    )(core, feats, proj)


def merge_kernel(yl_ref, keep_ref, got_ref, keep2_ref, send2_ref):
    yl = yl_ref[0]
    send2_ref[...] = (keep_ref[1 - yl] + got_ref[1 - yl]).astype(jnp.bfloat16)
    keep2_ref[...] = keep_ref[yl] + got_ref[yl]


def merge(yl, keep, got, name):
    return pl.pallas_call(
        merge_kernel,
        out_shape=(
            jax.ShapeDtypeStruct((SHARE, WIDTH), jnp.float32),
            jax.ShapeDtypeStruct((SHARE, WIDTH), jnp.bfloat16),
        ),
        in_specs=[SMEM, VMEM, VMEM],
        out_specs=(VMEM, VMEM),
        compiler_params=pltpu.CompilerParams(vmem_limit_bytes=12 * 1024 * 1024),
        name=name,
    )(yl, keep, got)


def normalized(keep2_ref, got2_ref):
    raw = keep2_ref[...] + got2_ref[...].astype(jnp.float32)
    total = jnp.sum(raw * raw, axis=1, keepdims=True)
    return (raw * lax.rsqrt(total + EPSILON)).astype(jnp.bfloat16)


def finish_kernel(keep2_s, got2_s, keep2_q, got2_q, struct_ext_ref, seq_ext_ref, peers_ref, seq_ref):
    struct = normalized(keep2_s, got2_s)
    turned = struct.astype(jnp.float32).T.astype(jnp.bfloat16)
    struct_ext = struct_ext_ref[...]
    for peer in range(SIDE):
        peers_ref[peer, 0:WIDTH, :] = turned
        peers_ref[peer, WIDTH:, :] = struct_ext
    seq = normalized(keep2_q, got2_q)
    seq_ref[0:SHARE, :] = seq
    seq_ref[SHARE:, :] = seq_ext_ref[...]


def finish(*held):
    return pl.pallas_call(
        finish_kernel,
        out_shape=(
            jax.ShapeDtypeStruct((SIDE, WIDTH + EXT, SHARE), jnp.bfloat16),
            jax.ShapeDtypeStruct((SHARE + EXT, WIDTH), jnp.bfloat16),
        ),
        in_specs=[VMEM] * 6,
        out_specs=(VMEM,) * 2,
        compiler_params=pltpu.CompilerParams(vmem_limit_bytes=12 * 1024 * 1024),
        name="finish",
    )(*held)


def integers(values):
    return values.astype(jnp.float32).astype(jnp.int32)


def pair_kernel(place_ref, *refs):
    seq_refs, s, rows_ref, cols_ref, self_ref = refs[0:SIDE], refs[SIDE], refs[SIDE + 1], refs[SIDE + 2], refs[SIDE + 3]
    q, info, buf0, buf1, lab8, ct, cm, held0, held1, row_sums, chosen = refs[SIDE + 4 :]
    my_z, my_core = place_ref[0], place_ref[1]
    my_block = my_z * 2 + my_core

    for block in range(SIDE):
        at = slice(block * SHARE, (block + 1) * SHARE)
        q[at, :] = seq_refs[block][0:SHARE, :]
        ext = integers(seq_refs[block][SHARE:, :])
        high, low = ext[:, 0:SHARE], ext[:, SHARE : 2 * SHARE]
        label = ext[:, 2 * SHARE : 3 * SHARE] * 128 + ext[:, 3 * SHARE :]
        code = jnp.where((high >> 4) == my_block, (high & 15) * 128 + low, -1)
        info[at, :] = jnp.full((SHARE, 128), -1, jnp.int32)
        info[at, 0 : 2 * EXT] = jnp.concatenate([code, -1 - label], axis=0).astype(jnp.float32).T.astype(jnp.int32)
    for chunk in range(SIDE):
        labels = integers(s[chunk, WIDTH:, :])
        lab8[:, chunk * 128 : (chunk + 1) * 128] = labels[0:8] * 128 + labels[8:16]
    ct[...] = jnp.zeros_like(ct)
    cm[...] = jnp.zeros_like(cm)
    row_of = lax.broadcasted_iota(jnp.int32, (8, SHARE), 0)
    held1[...] = jnp.zeros_like(held1)
    lane_of = lax.broadcasted_iota(jnp.int32, (3 * SHARE, 128), 1)
    for which in range(3):
        chosen[which * 3 * SHARE : (which + 1) * 3 * SHARE, :] = jnp.where(lane_of == which, 1.0, 0.0).astype(jnp.bfloat16)

    zero = jnp.zeros((8, 128), jnp.float32)
    groups = range(SUB // 8)

    def piece(tile, target, pair):
        cols = jnp.concatenate([s[2 * pair, 0:WIDTH, :], s[2 * pair + 1, 0:WIDTH, :]], axis=1)
        rows = pl.ds(pl.multiple_of(tile * SHARE, SHARE), SHARE)
        target[:, 2 * pair * SHARE : 2 * (pair + 1) * SHARE] = jnp.dot(
            q[rows, :], cols, preferred_element_type=jnp.float32
        )

    def gather_sums(slot, held):
        parts = []
        for which in range(3):
            rest = held[which]
            for _ in range(3):
                part = rest.astype(jnp.bfloat16)
                parts.append(part)
                rest = rest - part.astype(jnp.float32)
        summed = jnp.dot(jnp.concatenate(parts, axis=1), chosen[...], preferred_element_type=jnp.float32)
        row_sums[slot] = summed.T[0:8, :]

    def work(tile, products, next_tile, target, held, last_slot, last_held):
        for sub in range(SHARE // SUB):
            if sub == 1:
                gather_sums(last_slot, last_held)
            here = [pl.ds(pl.multiple_of(tile * SHARE + sub * SUB + group * 8, 8), 8) for group in groups]
            code = [info[rows, :] for rows in here]
            label = [jnp.broadcast_to(-1 - each[:, SLOTS : SLOTS + 1], (8, 128)) for each in code]
            lane = [each & 127 for each in code]
            pair_of = [each >> 8 for each in code]
            row_total, row_matched = [zero for _ in groups], [zero for _ in groups]
            picked = [jnp.zeros((8, 128), jnp.int32) for _ in groups]
            even = [None for _ in groups]
            for chunk in range(SIDE):
                if chunk % 8 == 0:
                    piece(next_tile, target, sub * 2 + chunk // 8)
                at = slice(chunk * 128, (chunk + 1) * 128)
                col_label = lab8[:, at]
                col_total, col_matched = ct[:, at], cm[:, at]
                for group in groups:
                    local = sub * SUB + group * 8
                    product = products[local : local + 8, at]
                    expo = jnp.exp(product * LOGIT_SCALE)
                    fixed = (product * FIXED).astype(jnp.int32)
                    kept = jnp.where(label[group] == col_label, expo, 0.0)
                    row_total[group] += expo
                    row_matched[group] += kept
                    col_total += expo
                    col_matched += kept
                    if chunk % 2 == 0:
                        even[group] = fixed
                    else:
                        both = (even[group] << 16) + fixed
                        found = jnp.take_along_axis(both, lane[group], axis=1, mode="promise_in_bounds")
                        picked[group] = jnp.where(pair_of[group] == chunk // 2, found, picked[group])
                ct[:, at] = col_total
                cm[:, at] = col_matched
            for group in groups:
                local = slice(sub * SUB + group * 8, sub * SUB + group * 8 + 8)
                held[0, local, :] = row_total[group]
                held[1, local, :] = row_matched[group]
                odd = (picked[group] << 16) >> 16
                fixed = jnp.where((code[group] & 128) > 0, odd, (picked[group] - odd) >> 16).astype(jnp.float32)
                fixed = fixed + jnp.where(fixed > 0, 0.5, jnp.where(fixed < 0, -0.5, 0.0))
                hard = jnp.exp(fixed * (LOGIT_SCALE / FIXED))
                held[2, local, :] = jnp.where(code[group] >= 0, hard, 0.0)

    for pair in range(SIDE // 2):
        piece(0, buf0, pair)

    def body(step, carry):
        work(2 * step, buf0, 2 * step + 1, buf1, held0, jnp.where(step == 0, SIDE, 2 * step - 1), held1)
        work(2 * step + 1, buf1, jnp.minimum(2 * step + 2, SIDE - 1), buf0, held1, 2 * step, held0)
        return carry

    lax.fori_loop(0, SIDE // 2, body, 0)
    gather_sums(SIDE - 1, held1)
    for far in range(8):
        out = jnp.zeros((8, SHARE), jnp.float32)
        for mate in range(2):
            first = (my_core ^ mate) * 3
            for which in range(3):
                out = jnp.where(row_of == first + which, row_sums[far * 2 + mate][which : which + 1], out)
        rows_ref[(my_z + far) & 7] = out
    own = jnp.dot(q[0:SHARE, :], s[place_ref[2], 0:WIDTH, :], preferred_element_type=jnp.float32)
    diagonal = lax.broadcasted_iota(jnp.int32, own.shape, 0) == lax.broadcasted_iota(jnp.int32, own.shape, 1)
    self_ref[...] = jnp.broadcast_to(jnp.sum(jnp.where(diagonal, own, 0.0), axis=0, keepdims=True), (8, SHARE))

    for chunk in range(SIDE):
        at = slice(chunk * 128, (chunk + 1) * 128)
        total = jnp.sum(ct[:, at], axis=0, keepdims=True)
        matched = jnp.sum(cm[:, at], axis=0, keepdims=True)
        cols_ref[chunk] = jnp.where(row_of == 0, total, matched)


def pair_sums(place, seq_blocks, struct_blocks):
    return pl.pallas_call(
        pair_kernel,
        out_shape=(
            jax.ShapeDtypeStruct((8, 8, SHARE), jnp.float32),
            jax.ShapeDtypeStruct((SIDE, 8, SHARE), jnp.float32),
            jax.ShapeDtypeStruct((8, SHARE), jnp.float32),
        ),
        in_specs=[SMEM] + [VMEM] * (SIDE + 1),
        out_specs=(VMEM, VMEM, VMEM),
        scratch_shapes=[
            pltpu.VMEM((EDGE, WIDTH), jnp.bfloat16),
            pltpu.VMEM((EDGE, 128), jnp.int32),
            pltpu.VMEM((SHARE, EDGE), jnp.float32),
            pltpu.VMEM((SHARE, EDGE), jnp.float32),
            pltpu.VMEM((8, EDGE), jnp.int32),
            pltpu.VMEM((8, EDGE), jnp.float32),
            pltpu.VMEM((8, EDGE), jnp.float32),
            pltpu.VMEM((3, SHARE, 128), jnp.float32),
            pltpu.VMEM((3, SHARE, 128), jnp.float32),
            pltpu.VMEM((SIDE + 1, 8, SHARE), jnp.float32),
            pltpu.VMEM((9 * SHARE, 128), jnp.bfloat16),
        ],
        compiler_params=pltpu.CompilerParams(vmem_limit_bytes=28 * 1024 * 1024),
        cost_estimate=pl.CostEstimate(
            flops=2 * EDGE * EDGE * WIDTH, bytes_accessed=4 * EDGE * WIDTH, transcendentals=EDGE * EDGE
        ),
        name="pair_sums",
    )(place, *seq_blocks, struct_blocks)


def over_z(block):
    found = {0: block, 1: shifted(block, "z", 1), 7: shifted(block, "z", -1)}
    found[2], found[6] = shifted(found[1], "z", 1), shifted(found[7], "z", -1)
    found[3], found[5] = shifted(found[2], "z", 1), shifted(found[6], "z", -1)
    found[4] = shifted(found[3], "z", 1)
    return [found[place] for place in range(8)]


def per_device(struct_feats, seq_feats, struct_proj, seq_proj, cluster_ids, hard_owner, hard_local, hard_valid):
    place = lambda axes: lax.axis_index(axes).astype(jnp.int32)
    core, yl = place("core"), place("yl")
    keep_s, send_s = project(core.reshape(1), struct_feats, struct_proj, False, "project_struct")
    got_s = shifted(send_s, "core", 1)
    keep_q, send_q = project(core.reshape(1), seq_feats.T, seq_proj, True, "project_seq")
    got_q = shifted(send_q, "core", 1)

    keep2_s, send2_s = merge(yl.reshape(1), keep_s, got_s, "merge_struct")
    got2_s = shifted(send2_s, "yl", 1)
    keep2_q, send2_q = merge(yl.reshape(1), keep_q, got_q, "merge_seq")
    got2_q = shifted(send2_q, "yl", 1)
    cluster_ids, hard_owner, hard_local, hard_valid, send2_q = lax.optimization_barrier(
        (cluster_ids, hard_owner, hard_local, hard_valid, send2_q)
    )
    own = lambda value: lax.dynamic_slice_in_dim(value, place(MP_AXES) * SHARE, SHARE, 0)
    labels = own(cluster_ids)
    owner = own(hard_owner[:, :, 0])
    local = own(hard_local)
    block = (owner >> 3) * 2 + ((local >> 7) & 1)
    chunk = (owner & 7) * 2 + (local >> 8)
    high = jnp.where(hard_valid > 0, block * 16 + chunk, -1).T
    low = (local & 127).T
    wide = lambda value: jnp.broadcast_to(value[None], (EXT, SHARE))
    seq_ext = jnp.concatenate([high, low, wide(labels >> 7), wide(labels & 127)], axis=1).astype(jnp.bfloat16)
    struct_ext = jnp.concatenate([wide(labels >> 7)[0:8], wide(labels & 127)[0:8]], axis=0).astype(jnp.bfloat16)

    struct_peers, seq_block = finish(keep2_s, got2_s, keep2_q, got2_q, struct_ext, seq_ext)
    struct_blocks = lax.all_to_all(struct_peers, COL_AXES, split_axis=0, concat_axis=0, tiled=True)
    seq_blocks = [each for held in over_z(seq_block) for each in (held, shifted(held, "core", 1))]

    rows, cols, self_dot = pair_sums(jnp.stack([place("z"), core, place(COL_AXES)]), seq_blocks, struct_blocks)
    rows = jnp.sum(lax.all_to_all(rows, "z", split_axis=0, concat_axis=0, tiled=True), axis=0)
    cols = jnp.sum(lax.all_to_all(cols, COL_AXES, split_axis=0, concat_axis=0, tiled=True), axis=0)
    rows = lax.all_gather(rows, MP_AXES, axis=0, tiled=False).reshape(2, 2, 8, SHARE)
    rows = jnp.sum(rows, axis=1)[:, 0:6].reshape(2, 2, 3, SHARE)

    seq_loss = (jnp.log(rows[:, :, 0]) - jnp.log(rows[:, :, 1])).reshape(4 * SHARE)
    struct_loss = jnp.log(cols[0]) - jnp.log(cols[1])
    self_logits = LOGIT_SCALE * self_dot[0]
    extra = rows[:, :, 2].reshape(4, SHARE)[place(MP_AXES)]
    hard_loss = jnp.log(jnp.exp(self_logits) + extra) - self_logits
    return (seq_loss, struct_loss, hard_loss)


def solution(mesh):
    fine = Mesh(mesh.devices.reshape(8, 2, 4, 2, 2), ("z", "yh", "x", "yl", "core"))
    blk = ("z", "yh", "x")
    both = blk + MP_AXES
    placed = (
        P(blk, MP_AXES),
        P(blk, MP_AXES),
        P(MP_AXES, None),
        P(MP_AXES, None),
        P(blk),
        P(blk, None, None),
        P(blk, None),
        P(both, None),
    )
    return jax.shard_map(
        per_device,
        mesh=fine,
        in_specs=placed,
        out_specs=(P(blk), P(both), P(both)),
        check_vma=False,
    )
```

```python
import functools
import math

import jax
import jax.numpy as jnp
from jax import lax
from jax.experimental import pallas as pl
from jax.experimental.pallas import tpu as pltpu
from jax.sharding import Mesh, PartitionSpec as P

LOGIT_SCALE = 14.285714285714286
EPSILON = 1e-06

SHARE = 128
SIDE = 16
EDGE = SHARE * SIDE
WIDTH = 512
SLOTS = 16
EXT = 16
FIXED = 32000.0
SUB = 32

COL_AXES = ("yh", "x", "yl")
MP_AXES = ("yl", "core")
SIZES = {"z": 8, "yh": 2, "x": 4, "yl": 2, "core": 2}

VMEM = pl.BlockSpec(memory_space=pltpu.VMEM)
SMEM = pl.BlockSpec(memory_space=pltpu.SMEM)
HBM = pl.BlockSpec(memory_space=pltpu.HBM)


def shifted(value, axes, steps):
    names = (axes,) if isinstance(axes, str) else axes
    count = math.prod(SIZES[name] for name in names)
    return lax.ppermute(value, axes, [((place + steps) % count, place) for place in range(count)])


def project_kernel(core_ref, feats_hbm, proj_hbm, keep_ref, send_ref, feats_ref, proj_ref, sems, *, turned):
    core = core_ref[0]
    copies = [
        pltpu.make_async_copy(feats_hbm, feats_ref, sems.at[0]),
        pltpu.make_async_copy(proj_hbm, proj_ref, sems.at[1]),
    ]
    for copy in copies:
        copy.start()
    for copy in copies:
        copy.wait()
    for out, which in ((send_ref, 1 - core), (keep_ref, core)):
        for half in range(2):
            rows = pl.ds(pl.multiple_of((half * 2 + which) * SHARE, SHARE), SHARE)
            feats, over = (feats_ref[:, rows], 0) if turned else (feats_ref[rows, :], 1)
            out[half] = lax.dot_general(
                feats, proj_ref[...], (((over,), (0,)), ((), ())), preferred_element_type=jnp.float32
            )


def project(core, feats, proj, turned, name):
    shape = jax.ShapeDtypeStruct((2, SHARE, WIDTH), jnp.float32)
    return pl.pallas_call(
        functools.partial(project_kernel, turned=turned),
        out_shape=(shape, shape),
        in_specs=[SMEM, HBM, HBM],
        out_specs=(VMEM, VMEM),
        scratch_shapes=[
            pltpu.VMEM(feats.shape, feats.dtype),
            pltpu.VMEM(proj.shape, proj.dtype),
            pltpu.SemaphoreType.DMA((2,)),
        ],
        compiler_params=pltpu.CompilerParams(vmem_limit_bytes=12 * 1024 * 1024),
        name=name,
    )(core, feats, proj)


def merge_kernel(yl_ref, keep_ref, got_ref, keep2_ref, send2_ref):
    yl = yl_ref[0]
    send2_ref[...] = (keep_ref[1 - yl] + got_ref[1 - yl]).astype(jnp.bfloat16)
    keep2_ref[...] = keep_ref[yl] + got_ref[yl]


def merge(yl, keep, got, name):
    return pl.pallas_call(
        merge_kernel,
        out_shape=(
            jax.ShapeDtypeStruct((SHARE, WIDTH), jnp.float32),
            jax.ShapeDtypeStruct((SHARE, WIDTH), jnp.bfloat16),
        ),
        in_specs=[SMEM, VMEM, VMEM],
        out_specs=(VMEM, VMEM),
        compiler_params=pltpu.CompilerParams(vmem_limit_bytes=12 * 1024 * 1024),
        name=name,
    )(yl, keep, got)


def normalized(keep2_ref, got2_ref):
    raw = keep2_ref[...] + got2_ref[...].astype(jnp.float32)
    total = jnp.sum(raw * raw, axis=1, keepdims=True)
    return (raw * lax.rsqrt(total + EPSILON)).astype(jnp.bfloat16)


def finish_kernel(keep2_s, got2_s, keep2_q, got2_q, struct_ext_ref, seq_ext_ref, peers_ref, seq_ref):
    struct = normalized(keep2_s, got2_s)
    turned = struct.astype(jnp.float32).T.astype(jnp.bfloat16)
    struct_ext = struct_ext_ref[...]
    for peer in range(SIDE):
        peers_ref[peer, 0:WIDTH, :] = turned
        peers_ref[peer, WIDTH:, :] = struct_ext
    seq = normalized(keep2_q, got2_q)
    seq_ref[0:SHARE, :] = seq
    seq_ref[SHARE:, :] = seq_ext_ref[...]


def finish(*held):
    return pl.pallas_call(
        finish_kernel,
        out_shape=(
            jax.ShapeDtypeStruct((SIDE, WIDTH + EXT, SHARE), jnp.bfloat16),
            jax.ShapeDtypeStruct((SHARE + EXT, WIDTH), jnp.bfloat16),
        ),
        in_specs=[VMEM] * 6,
        out_specs=(VMEM,) * 2,
        compiler_params=pltpu.CompilerParams(vmem_limit_bytes=12 * 1024 * 1024),
        name="finish",
    )(*held)


def integers(values):
    return values.astype(jnp.float32).astype(jnp.int32)


def pair_kernel(place_ref, *refs):
    seq_refs, s, rows_ref, cols_ref, self_ref = refs[0:SIDE], refs[SIDE], refs[SIDE + 1], refs[SIDE + 2], refs[SIDE + 3]
    q, info, buf0, buf1, lab8, ct, cm, held0, held1, row_sums, chosen = refs[SIDE + 4 :]
    my_z, my_core = place_ref[0], place_ref[1]
    my_block = my_z * 2 + my_core

    for block in range(SIDE):
        at = slice(block * SHARE, (block + 1) * SHARE)
        q[at, :] = seq_refs[block][0:SHARE, :]
        ext = integers(seq_refs[block][SHARE:, :])
        high, low = ext[:, 0:SHARE], ext[:, SHARE : 2 * SHARE]
        label = ext[:, 2 * SHARE : 3 * SHARE] * 128 + ext[:, 3 * SHARE :]
        code = jnp.where((high >> 4) == my_block, (high & 15) * 128 + low, -1)
        info[at, :] = jnp.full((SHARE, 128), -1, jnp.int32)
        info[at, 0 : 2 * EXT] = jnp.concatenate([code, -1 - label], axis=0).astype(jnp.float32).T.astype(jnp.int32)
    for chunk in range(SIDE):
        labels = integers(s[chunk, WIDTH:, :])
        lab8[:, chunk * 128 : (chunk + 1) * 128] = labels[0:8] * 128 + labels[8:16]
    ct[...] = jnp.zeros_like(ct)
    cm[...] = jnp.zeros_like(cm)
    row_of = lax.broadcasted_iota(jnp.int32, (8, SHARE), 0)
    held1[...] = jnp.zeros_like(held1)
    lane_of = lax.broadcasted_iota(jnp.int32, (3 * SHARE, 128), 1)
    for which in range(3):
        chosen[which * 3 * SHARE : (which + 1) * 3 * SHARE, :] = jnp.where(lane_of == which, 1.0, 0.0).astype(jnp.bfloat16)

    zero = jnp.zeros((8, 128), jnp.float32)
    groups = range(SUB // 8)

    def piece(tile, target, pair):
        cols = jnp.concatenate([s[2 * pair, 0:WIDTH, :], s[2 * pair + 1, 0:WIDTH, :]], axis=1)
        rows = pl.ds(pl.multiple_of(tile * SHARE, SHARE), SHARE)
        target[:, 2 * pair * SHARE : 2 * (pair + 1) * SHARE] = jnp.dot(
            q[rows, :], cols, preferred_element_type=jnp.float32
        )

    def gather_sums(slot, held):
        parts = []
        for which in range(3):
            rest = held[which]
            for _ in range(3):
                part = rest.astype(jnp.bfloat16)
                parts.append(part)
                rest = rest - part.astype(jnp.float32)
        summed = jnp.dot(jnp.concatenate(parts, axis=1), chosen[...], preferred_element_type=jnp.float32)
        row_sums[slot] = summed.T[0:8, :]

    def work(tile, products, next_tile, target, held, last_slot, last_held):
        for sub in range(SHARE // SUB):
            if sub == 1:
                gather_sums(last_slot, last_held)
            here = [pl.ds(pl.multiple_of(tile * SHARE + sub * SUB + group * 8, 8), 8) for group in groups]
            code = [info[rows, :] for rows in here]
            label = [jnp.broadcast_to(-1 - each[:, SLOTS : SLOTS + 1], (8, 128)) for each in code]
            lane = [each & 127 for each in code]
            pair_of = [each >> 8 for each in code]
            row_total, row_matched = [zero for _ in groups], [zero for _ in groups]
            picked = [jnp.zeros((8, 128), jnp.int32) for _ in groups]
            even = [None for _ in groups]
            for chunk in range(SIDE):
                if chunk % 8 == 0:
                    piece(next_tile, target, sub * 2 + chunk // 8)
                at = slice(chunk * 128, (chunk + 1) * 128)
                col_label = lab8[:, at]
                col_total, col_matched = ct[:, at], cm[:, at]
                for group in groups:
                    local = sub * SUB + group * 8
                    product = products[local : local + 8, at]
                    expo = jnp.exp(product * LOGIT_SCALE)
                    fixed = (product * FIXED).astype(jnp.int32)
                    kept = jnp.where(label[group] == col_label, expo, 0.0)
                    row_total[group] += expo
                    row_matched[group] += kept
                    col_total += expo
                    col_matched += kept
                    if chunk % 2 == 0:
                        even[group] = fixed
                    else:
                        both = (even[group] << 16) + fixed
                        found = jnp.take_along_axis(both, lane[group], axis=1, mode="promise_in_bounds")
                        picked[group] = jnp.where(pair_of[group] == chunk // 2, found, picked[group])
                ct[:, at] = col_total
                cm[:, at] = col_matched
            for group in groups:
                local = slice(sub * SUB + group * 8, sub * SUB + group * 8 + 8)
                held[0, local, :] = row_total[group]
                held[1, local, :] = row_matched[group]
                odd = (picked[group] << 16) >> 16
                fixed = jnp.where((code[group] & 128) > 0, odd, (picked[group] - odd) >> 16).astype(jnp.float32)
                fixed = fixed + jnp.where(fixed > 0, 0.5, jnp.where(fixed < 0, -0.5, 0.0))
                hard = jnp.exp(fixed * (LOGIT_SCALE / FIXED))
                held[2, local, :] = jnp.where(code[group] >= 0, hard, 0.0)

    for pair in range(SIDE // 2):
        piece(0, buf0, pair)

    def body(step, carry):
        work(2 * step, buf0, 2 * step + 1, buf1, held0, jnp.where(step == 0, SIDE, 2 * step - 1), held1)
        work(2 * step + 1, buf1, jnp.minimum(2 * step + 2, SIDE - 1), buf0, held1, 2 * step, held0)
        return carry

    lax.fori_loop(0, SIDE // 2, body, 0)
    gather_sums(SIDE - 1, held1)
    for far in range(8):
        out = jnp.zeros((8, SHARE), jnp.float32)
        for mate in range(2):
            first = (my_core ^ mate) * 3
            for which in range(3):
                out = jnp.where(row_of == first + which, row_sums[far * 2 + mate][which : which + 1], out)
        rows_ref[(my_z + far) & 7] = out
    own = jnp.dot(q[0:SHARE, :], s[place_ref[2], 0:WIDTH, :], preferred_element_type=jnp.float32)
    diagonal = lax.broadcasted_iota(jnp.int32, own.shape, 0) == lax.broadcasted_iota(jnp.int32, own.shape, 1)
    self_ref[...] = jnp.broadcast_to(jnp.sum(jnp.where(diagonal, own, 0.0), axis=0, keepdims=True), (8, SHARE))

    for chunk in range(SIDE):
        at = slice(chunk * 128, (chunk + 1) * 128)
        total = jnp.sum(ct[:, at], axis=0, keepdims=True)
        matched = jnp.sum(cm[:, at], axis=0, keepdims=True)
        cols_ref[chunk] = jnp.where(row_of == 0, total, matched)


def pair_sums(place, seq_blocks, struct_blocks):
    return pl.pallas_call(
        pair_kernel,
        out_shape=(
            jax.ShapeDtypeStruct((8, 8, SHARE), jnp.float32),
            jax.ShapeDtypeStruct((SIDE, 8, SHARE), jnp.float32),
            jax.ShapeDtypeStruct((8, SHARE), jnp.float32),
        ),
        in_specs=[SMEM] + [VMEM] * (SIDE + 1),
        out_specs=(VMEM, VMEM, VMEM),
        scratch_shapes=[
            pltpu.VMEM((EDGE, WIDTH), jnp.bfloat16),
            pltpu.VMEM((EDGE, 128), jnp.int32),
            pltpu.VMEM((SHARE, EDGE), jnp.float32),
            pltpu.VMEM((SHARE, EDGE), jnp.float32),
            pltpu.VMEM((8, EDGE), jnp.int32),
            pltpu.VMEM((8, EDGE), jnp.float32),
            pltpu.VMEM((8, EDGE), jnp.float32),
            pltpu.VMEM((3, SHARE, 128), jnp.float32),
            pltpu.VMEM((3, SHARE, 128), jnp.float32),
            pltpu.VMEM((SIDE + 1, 8, SHARE), jnp.float32),
            pltpu.VMEM((9 * SHARE, 128), jnp.bfloat16),
        ],
        compiler_params=pltpu.CompilerParams(vmem_limit_bytes=28 * 1024 * 1024),
        cost_estimate=pl.CostEstimate(
            flops=2 * EDGE * EDGE * WIDTH, bytes_accessed=4 * EDGE * WIDTH, transcendentals=EDGE * EDGE
        ),
        name="pair_sums",
    )(place, *seq_blocks, struct_blocks)


def losses_kernel(place_ref, rows_ref, cols_ref, self_ref, seq_ref, struct_ref, hard_ref):
    rows = jnp.sum(rows_ref[...], axis=0)
    own, other = rows[0:8], rows[8:16]
    lower, upper = (place_ref[0] == 0), (place_ref[0] == 1)
    for place, held in ((0, jnp.where(lower, own, other)), (1, jnp.where(upper, own, other))):
        for core in range(2):
            at = slice(place * 2 + core, place * 2 + core + 1)
            seq_ref[at, :] = jnp.log(held[core * 3 : core * 3 + 1]) - jnp.log(held[core * 3 + 1 : core * 3 + 2])
    cols = jnp.sum(cols_ref[...], axis=0)
    struct_ref[...] = jnp.log(cols[0:1]) - jnp.log(cols[1:2])
    extra = jnp.where(place_ref[1] == 0, own[2:3], own[5:6])
    self_logits = LOGIT_SCALE * self_ref[0:1]
    hard_ref[...] = jnp.log(jnp.exp(self_logits) + extra) - self_logits


def losses(place, rows, cols, self_dot):
    return pl.pallas_call(
        losses_kernel,
        out_shape=(
            jax.ShapeDtypeStruct((4, SHARE), jnp.float32),
            jax.ShapeDtypeStruct((1, SHARE), jnp.float32),
            jax.ShapeDtypeStruct((1, SHARE), jnp.float32),
        ),
        in_specs=[SMEM, VMEM, VMEM, VMEM],
        out_specs=(VMEM, VMEM, VMEM),
        compiler_params=pltpu.CompilerParams(vmem_limit_bytes=4 * 1024 * 1024),
        name="losses",
    )(place, rows, cols, self_dot)


def over_z(block):
    found = {0: block, 1: shifted(block, "z", 1), 7: shifted(block, "z", -1)}
    found[2], found[6] = shifted(found[1], "z", 1), shifted(found[7], "z", -1)
    found[3], found[5] = shifted(found[2], "z", 1), shifted(found[6], "z", -1)
    found[4] = shifted(found[3], "z", 1)
    return [found[place] for place in range(8)]


def per_device(struct_feats, seq_feats, struct_proj, seq_proj, cluster_ids, hard_owner, hard_local, hard_valid):
    place = lambda axes: lax.axis_index(axes).astype(jnp.int32)
    core, yl = place("core"), place("yl")
    keep_s, send_s = project(core.reshape(1), struct_feats, struct_proj, False, "project_struct")
    got_s = shifted(send_s, "core", 1)
    keep_q, send_q = project(core.reshape(1), seq_feats.T, seq_proj, True, "project_seq")
    got_q = shifted(send_q, "core", 1)

    keep2_s, send2_s = merge(yl.reshape(1), keep_s, got_s, "merge_struct")
    got2_s = shifted(send2_s, "yl", 1)
    keep2_q, send2_q = merge(yl.reshape(1), keep_q, got_q, "merge_seq")
    got2_q = shifted(send2_q, "yl", 1)
    cluster_ids, hard_owner, hard_local, hard_valid, send2_q = lax.optimization_barrier(
        (cluster_ids, hard_owner, hard_local, hard_valid, send2_q)
    )
    own = lambda value: lax.dynamic_slice_in_dim(value, place(MP_AXES) * SHARE, SHARE, 0)
    labels = own(cluster_ids)
    owner = own(hard_owner[:, :, 0])
    local = own(hard_local)
    block = (owner >> 3) * 2 + ((local >> 7) & 1)
    chunk = (owner & 7) * 2 + (local >> 8)
    high = jnp.where(hard_valid > 0, block * 16 + chunk, -1).T
    low = (local & 127).T
    wide = lambda value: jnp.broadcast_to(value[None], (EXT, SHARE))
    seq_ext = jnp.concatenate([high, low, wide(labels >> 7), wide(labels & 127)], axis=1).astype(jnp.bfloat16)
    struct_ext = jnp.concatenate([wide(labels >> 7)[0:8], wide(labels & 127)[0:8]], axis=0).astype(jnp.bfloat16)

    struct_peers, seq_block = finish(keep2_s, got2_s, keep2_q, got2_q, struct_ext, seq_ext)
    struct_blocks = lax.all_to_all(struct_peers, COL_AXES, split_axis=0, concat_axis=0, tiled=True)
    seq_blocks = [each for held in over_z(seq_block) for each in (held, shifted(held, "core", 1))]

    rows, cols, self_dot = pair_sums(jnp.stack([place("z"), core, place(COL_AXES)]), seq_blocks, struct_blocks)
    cols = lax.all_to_all(cols, COL_AXES, split_axis=0, concat_axis=0, tiled=True)
    rows = rows + shifted(rows, "core", 1)
    rows = jnp.concatenate([rows, shifted(rows, "yl", 1)], axis=1)
    rows, cols = lax.optimization_barrier((rows, cols))
    rows = lax.all_to_all(rows, "z", split_axis=0, concat_axis=0, tiled=True)
    seq_loss, struct_loss, hard_loss = losses(jnp.stack([yl, core]), rows, cols, self_dot)
    return (seq_loss.reshape(4 * SHARE), struct_loss.reshape(SHARE), hard_loss.reshape(SHARE))


def solution(mesh):
    fine = Mesh(mesh.devices.reshape(8, 2, 4, 2, 2), ("z", "yh", "x", "yl", "core"))
    blk = ("z", "yh", "x")
    both = blk + MP_AXES
    placed = (
        P(blk, MP_AXES),
        P(blk, MP_AXES),
        P(MP_AXES, None),
        P(MP_AXES, None),
        P(blk),
        P(blk, None, None),
        P(blk, None),
        P(both, None),
    )
    return jax.shard_map(
        per_device,
        mesh=fine,
        in_specs=placed,
        out_specs=(P(blk), P(both), P(both)),
        check_vma=False,
    )
```

```python
import functools
import math

import jax
import jax.numpy as jnp
from jax import lax
from jax.experimental import pallas as pl
from jax.experimental.pallas import tpu as pltpu
from jax.sharding import Mesh, PartitionSpec as P

LOGIT_SCALE = 14.285714285714286
EPSILON = 1e-06
LOG2E = math.log2(math.e)

SHARE = 128
SIDE = 16
EDGE = SHARE * SIDE
WIDTH = 512
SLOTS = 16
EXT = 16
FIXED = 32000.0
SUB = 32

COL_AXES = ("yh", "x", "yl")
MP_AXES = ("yl", "core")
SIZES = {"z": 8, "yh": 2, "x": 4, "yl": 2, "core": 2}

VMEM = pl.BlockSpec(memory_space=pltpu.VMEM)
SMEM = pl.BlockSpec(memory_space=pltpu.SMEM)
HBM = pl.BlockSpec(memory_space=pltpu.HBM)


def shifted(value, axes, steps):
    names = (axes,) if isinstance(axes, str) else axes
    count = math.prod(SIZES[name] for name in names)
    return lax.ppermute(value, axes, [((place + steps) % count, place) for place in range(count)])


def project_kernel(core_ref, feats_hbm, proj_hbm, keep_ref, send_ref, feats_ref, proj_ref, sems, *, turned):
    core = core_ref[0]
    copies = [
        pltpu.make_async_copy(feats_hbm, feats_ref, sems.at[0]),
        pltpu.make_async_copy(proj_hbm, proj_ref, sems.at[1]),
    ]
    for copy in copies:
        copy.start()
    for copy in copies:
        copy.wait()
    for out, which in ((send_ref, 1 - core), (keep_ref, core)):
        for half in range(2):
            rows = pl.ds(pl.multiple_of((half * 2 + which) * SHARE, SHARE), SHARE)
            feats, over = (feats_ref[:, rows], 0) if turned else (feats_ref[rows, :], 1)
            out[half] = lax.dot_general(
                feats, proj_ref[...], (((over,), (0,)), ((), ())), preferred_element_type=jnp.float32
            )


def project(core, feats, proj, turned, name):
    shape = jax.ShapeDtypeStruct((2, SHARE, WIDTH), jnp.float32)
    return pl.pallas_call(
        functools.partial(project_kernel, turned=turned),
        out_shape=(shape, shape),
        in_specs=[SMEM, HBM, HBM],
        out_specs=(VMEM, VMEM),
        scratch_shapes=[
            pltpu.VMEM(feats.shape, feats.dtype),
            pltpu.VMEM(proj.shape, proj.dtype),
            pltpu.SemaphoreType.DMA((2,)),
        ],
        compiler_params=pltpu.CompilerParams(vmem_limit_bytes=12 * 1024 * 1024),
        name=name,
    )(core, feats, proj)


def merge_kernel(yl_ref, keep_ref, got_ref, keep2_ref, send2_ref):
    yl = yl_ref[0]
    send2_ref[...] = (keep_ref[1 - yl] + got_ref[1 - yl]).astype(jnp.bfloat16)
    keep2_ref[...] = keep_ref[yl] + got_ref[yl]


def merge(yl, keep, got, name):
    return pl.pallas_call(
        merge_kernel,
        out_shape=(
            jax.ShapeDtypeStruct((SHARE, WIDTH), jnp.float32),
            jax.ShapeDtypeStruct((SHARE, WIDTH), jnp.bfloat16),
        ),
        in_specs=[SMEM, VMEM, VMEM],
        out_specs=(VMEM, VMEM),
        compiler_params=pltpu.CompilerParams(vmem_limit_bytes=12 * 1024 * 1024),
        name=name,
    )(yl, keep, got)


def normalized(keep2_ref, got2_ref):
    raw = keep2_ref[...] + got2_ref[...].astype(jnp.float32)
    total = jnp.sum(raw * raw, axis=1, keepdims=True)
    return (raw * lax.rsqrt(total + EPSILON)).astype(jnp.bfloat16)


def finish_kernel(keep2_s, got2_s, keep2_q, got2_q, struct_ext_ref, seq_ext_ref, struct_ref, seq_ref):
    struct = normalized(keep2_s, got2_s)
    struct_ref[0:WIDTH, :] = struct.astype(jnp.float32).T.astype(jnp.bfloat16)
    struct_ref[WIDTH:, :] = struct_ext_ref[...]
    seq = normalized(keep2_q, got2_q)
    seq_ref[0:SHARE, :] = seq
    seq_ref[SHARE:, :] = seq_ext_ref[...]


def finish(*held):
    return pl.pallas_call(
        finish_kernel,
        out_shape=(
            jax.ShapeDtypeStruct((WIDTH + EXT, SHARE), jnp.bfloat16),
            jax.ShapeDtypeStruct((SHARE + EXT, WIDTH), jnp.bfloat16),
        ),
        in_specs=[VMEM] * 6,
        out_specs=(VMEM,) * 2,
        compiler_params=pltpu.CompilerParams(vmem_limit_bytes=12 * 1024 * 1024),
        name="finish",
    )(*held)


def integers(values):
    return values.astype(jnp.float32).astype(jnp.int32)


def pair_kernel(place_ref, *refs):
    seq_refs, s, rows_ref, cols_ref, self_ref = refs[0:SIDE], refs[SIDE], refs[SIDE + 1], refs[SIDE + 2], refs[SIDE + 3]
    q, info, buf0, buf1, lab8, ct, cm, held0, held1, row_sums, chosen = refs[SIDE + 4 :]
    my_z, my_core = place_ref[0], place_ref[1]
    my_block = my_z * 2 + my_core

    for block in range(SIDE):
        at = slice(block * SHARE, (block + 1) * SHARE)
        q[at, :] = seq_refs[block][0:SHARE, :]
        ext = integers(seq_refs[block][SHARE:, :])
        high, low = ext[:, 0:SHARE], ext[:, SHARE : 2 * SHARE]
        label = ext[:, 2 * SHARE : 3 * SHARE] * 128 + ext[:, 3 * SHARE :]
        code = jnp.where((high >> 4) == my_block, (high & 15) * 128 + low, -1)
        info[at, :] = jnp.full((SHARE, 128), -1, jnp.int32)
        info[at, 0 : 2 * EXT] = jnp.concatenate([code, -1 - label], axis=0).astype(jnp.float32).T.astype(jnp.int32)
    for chunk in range(SIDE):
        labels = integers(s[chunk, WIDTH:, :])
        lab8[:, chunk * 128 : (chunk + 1) * 128] = labels[0:8] * 128 + labels[8:16]
    ct[...] = jnp.zeros_like(ct)
    cm[...] = jnp.zeros_like(cm)
    row_of = lax.broadcasted_iota(jnp.int32, (8, SHARE), 0)
    held1[...] = jnp.zeros_like(held1)
    lane_of = lax.broadcasted_iota(jnp.int32, (3 * SHARE, 128), 1)
    for which in range(3):
        chosen[which * 3 * SHARE : (which + 1) * 3 * SHARE, :] = jnp.where(lane_of == which, 1.0, 0.0).astype(jnp.bfloat16)

    zero = jnp.zeros((8, 128), jnp.float32)
    groups = range(SUB // 8)

    def piece(tile, target, pair):
        cols = jnp.concatenate([s[2 * pair, 0:WIDTH, :], s[2 * pair + 1, 0:WIDTH, :]], axis=1)
        rows = pl.ds(pl.multiple_of(tile * SHARE, SHARE), SHARE)
        target[:, 2 * pair * SHARE : 2 * (pair + 1) * SHARE] = jnp.dot(
            q[rows, :], cols, preferred_element_type=jnp.float32
        )

    def gather_sums(slot, held):
        parts = []
        for which in range(3):
            rest = held[which]
            for _ in range(3):
                part = rest.astype(jnp.bfloat16)
                parts.append(part)
                rest = rest - part.astype(jnp.float32)
        summed = jnp.dot(jnp.concatenate(parts, axis=1), chosen[...], preferred_element_type=jnp.float32)
        row_sums[slot] = summed.T[0:8, :]

    def work(tile, products, next_tile, target, held, last_slot, last_held):
        for sub in range(SHARE // SUB):
            if sub == 1:
                gather_sums(last_slot, last_held)
            here = [pl.ds(pl.multiple_of(tile * SHARE + sub * SUB + group * 8, 8), 8) for group in groups]
            code = [info[rows, :] for rows in here]
            label = [jnp.broadcast_to(-1 - each[:, SLOTS : SLOTS + 1], (8, 128)) for each in code]
            lane = [each & 127 for each in code]
            pair_of = [each >> 8 for each in code]
            row_total, row_matched = [zero for _ in groups], [zero for _ in groups]
            picked = [jnp.zeros((8, 128), jnp.int32) for _ in groups]
            even = [None for _ in groups]
            for chunk in range(SIDE):
                if chunk % 8 == 0:
                    piece(next_tile, target, sub * 2 + chunk // 8)
                at = slice(chunk * 128, (chunk + 1) * 128)
                col_label = lab8[:, at]
                col_total, col_matched = ct[:, at], cm[:, at]
                for group in groups:
                    local = sub * SUB + group * 8
                    product = products[local : local + 8, at]
                    expo = jnp.exp2(product * (LOGIT_SCALE * LOG2E))
                    fixed = (product * FIXED).astype(jnp.int32)
                    kept = jnp.where(label[group] == col_label, expo, 0.0)
                    row_total[group] += expo
                    row_matched[group] += kept
                    col_total += expo
                    col_matched += kept
                    if chunk % 2 == 0:
                        even[group] = fixed
                    else:
                        both = (even[group] << 16) + fixed
                        found = jnp.take_along_axis(both, lane[group], axis=1, mode="promise_in_bounds")
                        picked[group] = jnp.where(pair_of[group] == chunk // 2, found, picked[group])
                ct[:, at] = col_total
                cm[:, at] = col_matched
            for group in groups:
                local = slice(sub * SUB + group * 8, sub * SUB + group * 8 + 8)
                held[0, local, :] = row_total[group]
                held[1, local, :] = row_matched[group]
                odd = (picked[group] << 16) >> 16
                fixed = jnp.where((code[group] & 128) > 0, odd, (picked[group] - odd) >> 16).astype(jnp.float32)
                fixed = fixed + jnp.where(fixed > 0, 0.5, jnp.where(fixed < 0, -0.5, 0.0))
                hard = jnp.exp(fixed * (LOGIT_SCALE / FIXED))
                held[2, local, :] = jnp.where(code[group] >= 0, hard, 0.0)

    for pair in range(SIDE // 2):
        piece(0, buf0, pair)

    def body(step, carry):
        work(2 * step, buf0, 2 * step + 1, buf1, held0, jnp.where(step == 0, SIDE, 2 * step - 1), held1)
        work(2 * step + 1, buf1, jnp.minimum(2 * step + 2, SIDE - 1), buf0, held1, 2 * step, held0)
        return carry

    lax.fori_loop(0, SIDE // 2, body, 0)
    gather_sums(SIDE - 1, held1)
    for far in range(8):
        out = jnp.zeros((8, SHARE), jnp.float32)
        for mate in range(2):
            first = (my_core ^ mate) * 3
            for which in range(3):
                out = jnp.where(row_of == first + which, row_sums[far * 2 + mate][which : which + 1], out)
        rows_ref[(my_z + far) & 7] = out
    own = jnp.dot(q[0:SHARE, :], s[place_ref[2], 0:WIDTH, :], preferred_element_type=jnp.float32)
    diagonal = lax.broadcasted_iota(jnp.int32, own.shape, 0) == lax.broadcasted_iota(jnp.int32, own.shape, 1)
    self_ref[...] = jnp.broadcast_to(jnp.sum(jnp.where(diagonal, own, 0.0), axis=0, keepdims=True), (8, SHARE))

    for chunk in range(SIDE):
        at = slice(chunk * 128, (chunk + 1) * 128)
        total = jnp.sum(ct[:, at], axis=0, keepdims=True)
        matched = jnp.sum(cm[:, at], axis=0, keepdims=True)
        cols_ref[chunk] = jnp.where(row_of == 0, total, matched)


def pair_sums(place, seq_blocks, struct_blocks):
    return pl.pallas_call(
        pair_kernel,
        out_shape=(
            jax.ShapeDtypeStruct((8, 8, SHARE), jnp.float32),
            jax.ShapeDtypeStruct((SIDE, 8, SHARE), jnp.float32),
            jax.ShapeDtypeStruct((8, SHARE), jnp.float32),
        ),
        in_specs=[SMEM] + [VMEM] * (SIDE + 1),
        out_specs=(VMEM, VMEM, VMEM),
        scratch_shapes=[
            pltpu.VMEM((EDGE, WIDTH), jnp.bfloat16),
            pltpu.VMEM((EDGE, 128), jnp.int32),
            pltpu.VMEM((SHARE, EDGE), jnp.float32),
            pltpu.VMEM((SHARE, EDGE), jnp.float32),
            pltpu.VMEM((8, EDGE), jnp.int32),
            pltpu.VMEM((8, EDGE), jnp.float32),
            pltpu.VMEM((8, EDGE), jnp.float32),
            pltpu.VMEM((3, SHARE, 128), jnp.float32),
            pltpu.VMEM((3, SHARE, 128), jnp.float32),
            pltpu.VMEM((SIDE + 1, 8, SHARE), jnp.float32),
            pltpu.VMEM((9 * SHARE, 128), jnp.bfloat16),
        ],
        compiler_params=pltpu.CompilerParams(vmem_limit_bytes=28 * 1024 * 1024),
        cost_estimate=pl.CostEstimate(
            flops=2 * EDGE * EDGE * WIDTH, bytes_accessed=4 * EDGE * WIDTH, transcendentals=EDGE * EDGE
        ),
        name="pair_sums",
    )(place, *seq_blocks, struct_blocks)


def losses_kernel(place_ref, rows_ref, other_ref, cols_ref, self_ref, seq_ref, struct_ref, hard_ref):
    own, other = rows_ref[...], other_ref[...]
    lower, upper = (place_ref[0] == 0), (place_ref[0] == 1)
    for place, held in ((0, jnp.where(lower, own, other)), (1, jnp.where(upper, own, other))):
        for core in range(2):
            at = slice(place * 2 + core, place * 2 + core + 1)
            seq_ref[at, :] = jnp.log(held[core * 3 : core * 3 + 1]) - jnp.log(held[core * 3 + 1 : core * 3 + 2])
    cols = jnp.sum(cols_ref[...], axis=0)
    struct_ref[...] = jnp.log(cols[0:1]) - jnp.log(cols[1:2])
    extra = jnp.where(place_ref[1] == 0, own[2:3], own[5:6])
    self_logits = LOGIT_SCALE * self_ref[0:1]
    hard_ref[...] = jnp.log(jnp.exp(self_logits) + extra) - self_logits


def losses(place, rows, other_rows, cols, self_dot):
    return pl.pallas_call(
        losses_kernel,
        out_shape=(
            jax.ShapeDtypeStruct((4, SHARE), jnp.float32),
            jax.ShapeDtypeStruct((1, SHARE), jnp.float32),
            jax.ShapeDtypeStruct((1, SHARE), jnp.float32),
        ),
        in_specs=[SMEM, VMEM, VMEM, VMEM, VMEM],
        out_specs=(VMEM, VMEM, VMEM),
        compiler_params=pltpu.CompilerParams(vmem_limit_bytes=4 * 1024 * 1024),
        name="losses",
    )(place, rows, other_rows, cols, self_dot)


def over_z(block):
    found = {0: block, 1: shifted(block, "z", 1), 7: shifted(block, "z", -1)}
    found[2], found[6] = shifted(found[1], "z", 1), shifted(found[7], "z", -1)
    found[3], found[5] = shifted(found[2], "z", 1), shifted(found[6], "z", -1)
    found[4] = shifted(found[3], "z", 1)
    return [found[place] for place in range(8)]


def per_device(struct_feats, seq_feats, struct_proj, seq_proj, cluster_ids, hard_owner, hard_local, hard_valid):
    place = lambda axes: lax.axis_index(axes).astype(jnp.int32)
    core, yl = place("core"), place("yl")
    keep_s, send_s = project(core.reshape(1), struct_feats, struct_proj, False, "project_struct")
    got_s = shifted(send_s, "core", 1)
    keep_q, send_q = project(core.reshape(1), seq_feats.T, seq_proj, True, "project_seq")
    got_q = shifted(send_q, "core", 1)

    keep2_s, send2_s = merge(yl.reshape(1), keep_s, got_s, "merge_struct")
    got2_s = shifted(send2_s, "yl", 1)
    keep2_q, send2_q = merge(yl.reshape(1), keep_q, got_q, "merge_seq")
    got2_q = shifted(send2_q, "yl", 1)
    cluster_ids, hard_owner, hard_local, hard_valid, send2_q = lax.optimization_barrier(
        (cluster_ids, hard_owner, hard_local, hard_valid, send2_q)
    )
    own = lambda value: lax.dynamic_slice_in_dim(value, place(MP_AXES) * SHARE, SHARE, 0)
    labels = own(cluster_ids)
    owner = own(hard_owner[:, :, 0])
    local = own(hard_local)
    block = (owner >> 3) * 2 + ((local >> 7) & 1)
    chunk = (owner & 7) * 2 + (local >> 8)
    high = jnp.where(hard_valid > 0, block * 16 + chunk, -1).T
    low = (local & 127).T
    wide = lambda value: jnp.broadcast_to(value[None], (EXT, SHARE))
    seq_ext = jnp.concatenate([high, low, wide(labels >> 7), wide(labels & 127)], axis=1).astype(jnp.bfloat16)
    struct_ext = jnp.concatenate([wide(labels >> 7)[0:8], wide(labels & 127)[0:8]], axis=0).astype(jnp.bfloat16)

    struct_block, seq_block = finish(keep2_s, got2_s, keep2_q, got2_q, struct_ext, seq_ext)
    struct_peers = jnp.broadcast_to(struct_block[None], (SIDE, *struct_block.shape))
    struct_blocks = lax.all_to_all(struct_peers, COL_AXES, split_axis=0, concat_axis=0, tiled=True)
    seq_blocks = [each for held in over_z(seq_block) for each in (held, shifted(held, "core", 1))]

    rows, cols, self_dot = pair_sums(jnp.stack([place("z"), core, place(COL_AXES)]), seq_blocks, struct_blocks)
    rows = jnp.sum(lax.all_to_all(rows, "z", split_axis=0, concat_axis=0, tiled=True), axis=0)
    cols = lax.all_to_all(cols, COL_AXES, split_axis=0, concat_axis=0, tiled=True)
    rows = rows + shifted(rows, "core", 1)
    other_rows = shifted(rows, "yl", 1)
    seq_loss, struct_loss, hard_loss = losses(jnp.stack([yl, core]), rows, other_rows, cols, self_dot)
    return (seq_loss.reshape(4 * SHARE), struct_loss.reshape(SHARE), hard_loss.reshape(SHARE))


def solution(mesh):
    fine = Mesh(mesh.devices.reshape(8, 2, 4, 2, 2), ("z", "yh", "x", "yl", "core"))
    blk = ("z", "yh", "x")
    both = blk + MP_AXES
    placed = (
        P(blk, MP_AXES),
        P(blk, MP_AXES),
        P(MP_AXES, None),
        P(MP_AXES, None),
        P(blk),
        P(blk, None, None),
        P(blk, None),
        P(both, None),
    )
    return jax.shard_map(
        per_device,
        mesh=fine,
        in_specs=placed,
        out_specs=(P(blk), P(both), P(both)),
        check_vma=False,
    )
```

```python
import functools
import math

import jax
import jax.numpy as jnp
from jax import lax
from jax.experimental import pallas as pl
from jax.experimental.pallas import tpu as pltpu
from jax.sharding import Mesh, PartitionSpec as P

LOGIT_SCALE = 14.285714285714286
EPSILON = 1e-06
LOG2E = math.log2(math.e)

SHARE = 128
SIDE = 16
EDGE = SHARE * SIDE
WIDTH = 512
SLOTS = 16
EXT = 16
FIXED = 32000.0
SUB = 32

COL_AXES = ("yh", "x", "yl")
MP_AXES = ("yl", "core")
SIZES = {"z": 8, "yh": 2, "x": 4, "yl": 2, "core": 2}

VMEM = pl.BlockSpec(memory_space=pltpu.VMEM)
SMEM = pl.BlockSpec(memory_space=pltpu.SMEM)
HBM = pl.BlockSpec(memory_space=pltpu.HBM)


def shifted(value, axes, steps):
    names = (axes,) if isinstance(axes, str) else axes
    count = math.prod(SIZES[name] for name in names)
    return lax.ppermute(value, axes, [((place + steps) % count, place) for place in range(count)])


def project_kernel(core_ref, struct_hbm, ws_hbm, seq_hbm, wq_hbm, *refs):
    core = core_ref[0]
    keep_s, send_s, keep_q, send_q, struct_ref, ws_ref, seq_ref, wq_ref, sems = refs
    held = ((struct_hbm, struct_ref), (ws_hbm, ws_ref), (seq_hbm, seq_ref), (wq_hbm, wq_ref))
    copies = [pltpu.make_async_copy(source, target, sems.at[place]) for place, (source, target) in enumerate(held)]
    for copy in copies:
        copy.start()
    rows_of = lambda half, which: pl.ds(pl.multiple_of((half * 2 + which) * SHARE, SHARE), SHARE)
    copies[0].wait()
    copies[1].wait()
    for out, which in ((send_s, 1 - core), (keep_s, core)):
        for half in range(2):
            out[half] = jnp.dot(struct_ref[rows_of(half, which), :], ws_ref[...], preferred_element_type=jnp.float32)
    copies[2].wait()
    copies[3].wait()
    for out, which in ((send_q, 1 - core), (keep_q, core)):
        for half in range(2):
            out[half] = lax.dot_general(
                seq_ref[:, rows_of(half, which)],
                wq_ref[...],
                (((0,), (0,)), ((), ())),
                preferred_element_type=jnp.float32,
            )


def project(core, struct_feats, struct_proj, seq_feats_turned, seq_proj):
    shape = jax.ShapeDtypeStruct((2, SHARE, WIDTH), jnp.float32)
    held = (struct_feats, struct_proj, seq_feats_turned, seq_proj)
    return pl.pallas_call(
        project_kernel,
        out_shape=(shape,) * 4,
        in_specs=[SMEM] + [HBM] * 4,
        out_specs=(VMEM,) * 4,
        scratch_shapes=[pltpu.VMEM(each.shape, each.dtype) for each in held] + [pltpu.SemaphoreType.DMA((4,))],
        compiler_params=pltpu.CompilerParams(vmem_limit_bytes=56 * 1024 * 1024),
        name="project",
    )(core, *held)


def merge_kernel(yl_ref, keep_ref, got_ref, keep2_ref, send2_ref):
    yl = yl_ref[0]
    send2_ref[...] = (keep_ref[1 - yl] + got_ref[1 - yl]).astype(jnp.bfloat16)
    keep2_ref[...] = keep_ref[yl] + got_ref[yl]


def merge(yl, keep, got, name):
    return pl.pallas_call(
        merge_kernel,
        out_shape=(
            jax.ShapeDtypeStruct((SHARE, WIDTH), jnp.float32),
            jax.ShapeDtypeStruct((SHARE, WIDTH), jnp.bfloat16),
        ),
        in_specs=[SMEM, VMEM, VMEM],
        out_specs=(VMEM, VMEM),
        compiler_params=pltpu.CompilerParams(vmem_limit_bytes=12 * 1024 * 1024),
        name=name,
    )(yl, keep, got)


def normalized(keep2_ref, got2_ref):
    raw = keep2_ref[...] + got2_ref[...].astype(jnp.float32)
    total = jnp.sum(raw * raw, axis=1, keepdims=True)
    return (raw * lax.rsqrt(total + EPSILON)).astype(jnp.bfloat16)


def finish_kernel(keep2_s, got2_s, keep2_q, got2_q, struct_ext_ref, seq_ext_ref, struct_ref, seq_ref):
    struct = normalized(keep2_s, got2_s)
    struct_ref[0:WIDTH, :] = struct.astype(jnp.float32).T.astype(jnp.bfloat16)
    struct_ref[WIDTH:, :] = struct_ext_ref[...]
    seq = normalized(keep2_q, got2_q)
    seq_ref[0:SHARE, :] = seq
    seq_ref[SHARE:, :] = seq_ext_ref[...]


def finish(*held):
    return pl.pallas_call(
        finish_kernel,
        out_shape=(
            jax.ShapeDtypeStruct((WIDTH + EXT, SHARE), jnp.bfloat16),
            jax.ShapeDtypeStruct((SHARE + EXT, WIDTH), jnp.bfloat16),
        ),
        in_specs=[VMEM] * 6,
        out_specs=(VMEM,) * 2,
        compiler_params=pltpu.CompilerParams(vmem_limit_bytes=12 * 1024 * 1024),
        name="finish",
    )(*held)


def integers(values):
    return values.astype(jnp.float32).astype(jnp.int32)


def pair_kernel(place_ref, *refs):
    seq_refs, s, rows_ref, cols_ref, self_ref = refs[0:SIDE], refs[SIDE], refs[SIDE + 1], refs[SIDE + 2], refs[SIDE + 3]
    q, info, buf0, buf1, lab8, ct, cm, held0, held1, row_sums, chosen = refs[SIDE + 4 :]
    my_z, my_core = place_ref[0], place_ref[1]
    my_block = my_z * 2 + my_core

    for block in range(SIDE):
        at = slice(block * SHARE, (block + 1) * SHARE)
        q[at, :] = seq_refs[block][0:SHARE, :]
        ext = integers(seq_refs[block][SHARE:, :])
        high, low = ext[:, 0:SHARE], ext[:, SHARE : 2 * SHARE]
        label = ext[:, 2 * SHARE : 3 * SHARE] * 128 + ext[:, 3 * SHARE :]
        code = jnp.where((high >> 4) == my_block, (high & 15) * 128 + low, -1)
        info[at, :] = jnp.full((SHARE, 128), -1, jnp.int32)
        info[at, 0 : 2 * EXT] = jnp.concatenate([code, -1 - label], axis=0).astype(jnp.float32).T.astype(jnp.int32)
    for chunk in range(SIDE):
        labels = integers(s[chunk, WIDTH:, :])
        lab8[:, chunk * 128 : (chunk + 1) * 128] = labels[0:8] * 128 + labels[8:16]
    ct[...] = jnp.zeros_like(ct)
    cm[...] = jnp.zeros_like(cm)
    row_of = lax.broadcasted_iota(jnp.int32, (8, SHARE), 0)
    held1[...] = jnp.zeros_like(held1)
    lane_of = lax.broadcasted_iota(jnp.int32, (3 * SHARE, 128), 1)
    for which in range(3):
        chosen[which * 3 * SHARE : (which + 1) * 3 * SHARE, :] = jnp.where(lane_of == which, 1.0, 0.0).astype(jnp.bfloat16)

    zero = jnp.zeros((8, 128), jnp.float32)
    groups = range(SUB // 8)

    def piece(tile, target, pair):
        cols = jnp.concatenate([s[2 * pair, 0:WIDTH, :], s[2 * pair + 1, 0:WIDTH, :]], axis=1)
        rows = pl.ds(pl.multiple_of(tile * SHARE, SHARE), SHARE)
        target[:, 2 * pair * SHARE : 2 * (pair + 1) * SHARE] = jnp.dot(
            q[rows, :], cols, preferred_element_type=jnp.float32
        )

    def gather_sums(slot, held):
        parts = []
        for which in range(3):
            rest = held[which]
            for _ in range(3):
                part = rest.astype(jnp.bfloat16)
                parts.append(part)
                rest = rest - part.astype(jnp.float32)
        summed = jnp.dot(jnp.concatenate(parts, axis=1), chosen[...], preferred_element_type=jnp.float32)
        row_sums[slot] = summed.T[0:8, :]

    def work(tile, products, next_tile, target, held, last_slot, last_held):
        for sub in range(SHARE // SUB):
            if sub == 1:
                gather_sums(last_slot, last_held)
            here = [pl.ds(pl.multiple_of(tile * SHARE + sub * SUB + group * 8, 8), 8) for group in groups]
            code = [info[rows, :] for rows in here]
            label = [jnp.broadcast_to(-1 - each[:, SLOTS : SLOTS + 1], (8, 128)) for each in code]
            lane = [each & 127 for each in code]
            pair_of = [each >> 8 for each in code]
            row_total, row_matched = [zero for _ in groups], [zero for _ in groups]
            picked = [jnp.zeros((8, 128), jnp.int32) for _ in groups]
            even = [None for _ in groups]
            for chunk in range(SIDE):
                if chunk % 8 == 0:
                    piece(next_tile, target, sub * 2 + chunk // 8)
                at = slice(chunk * 128, (chunk + 1) * 128)
                col_label = lab8[:, at]
                col_total, col_matched = ct[:, at], cm[:, at]
                for group in groups:
                    local = sub * SUB + group * 8
                    product = products[local : local + 8, at]
                    expo = jnp.exp2(product * (LOGIT_SCALE * LOG2E))
                    fixed = (product * FIXED).astype(jnp.int32)
                    kept = jnp.where(label[group] == col_label, expo, 0.0)
                    row_total[group] += expo
                    row_matched[group] += kept
                    col_total += expo
                    col_matched += kept
                    if chunk % 2 == 0:
                        even[group] = fixed
                    else:
                        both = (even[group] << 16) + fixed
                        found = jnp.take_along_axis(both, lane[group], axis=1, mode="promise_in_bounds")
                        picked[group] = jnp.where(pair_of[group] == chunk // 2, found, picked[group])
                ct[:, at] = col_total
                cm[:, at] = col_matched
            for group in groups:
                local = slice(sub * SUB + group * 8, sub * SUB + group * 8 + 8)
                held[0, local, :] = row_total[group]
                held[1, local, :] = row_matched[group]
                odd = (picked[group] << 16) >> 16
                fixed = jnp.where((code[group] & 128) > 0, odd, (picked[group] - odd) >> 16).astype(jnp.float32)
                fixed = fixed + jnp.where(fixed > 0, 0.5, jnp.where(fixed < 0, -0.5, 0.0))
                hard = jnp.exp(fixed * (LOGIT_SCALE / FIXED))
                held[2, local, :] = jnp.where(code[group] >= 0, hard, 0.0)

    for pair in range(SIDE // 2):
        piece(0, buf0, pair)

    def body(step, carry):
        work(2 * step, buf0, 2 * step + 1, buf1, held0, jnp.where(step == 0, SIDE, 2 * step - 1), held1)
        work(2 * step + 1, buf1, jnp.minimum(2 * step + 2, SIDE - 1), buf0, held1, 2 * step, held0)
        return carry

    lax.fori_loop(0, SIDE // 2, body, 0)
    gather_sums(SIDE - 1, held1)
    for far in range(8):
        out = jnp.zeros((8, SHARE), jnp.float32)
        for mate in range(2):
            first = (my_core ^ mate) * 3
            for which in range(3):
                out = jnp.where(row_of == first + which, row_sums[far * 2 + mate][which : which + 1], out)
        rows_ref[(my_z + far) & 7] = out
    own = jnp.dot(q[0:SHARE, :], s[place_ref[2], 0:WIDTH, :], preferred_element_type=jnp.float32)
    diagonal = lax.broadcasted_iota(jnp.int32, own.shape, 0) == lax.broadcasted_iota(jnp.int32, own.shape, 1)
    self_ref[...] = jnp.broadcast_to(jnp.sum(jnp.where(diagonal, own, 0.0), axis=0, keepdims=True), (8, SHARE))

    for chunk in range(SIDE):
        at = slice(chunk * 128, (chunk + 1) * 128)
        total = jnp.sum(ct[:, at], axis=0, keepdims=True)
        matched = jnp.sum(cm[:, at], axis=0, keepdims=True)
        cols_ref[chunk] = jnp.where(row_of == 0, total, matched)


def pair_sums(place, seq_blocks, struct_blocks):
    return pl.pallas_call(
        pair_kernel,
        out_shape=(
            jax.ShapeDtypeStruct((8, 8, SHARE), jnp.float32),
            jax.ShapeDtypeStruct((SIDE, 8, SHARE), jnp.float32),
            jax.ShapeDtypeStruct((8, SHARE), jnp.float32),
        ),
        in_specs=[SMEM] + [VMEM] * (SIDE + 1),
        out_specs=(VMEM, VMEM, VMEM),
        scratch_shapes=[
            pltpu.VMEM((EDGE, WIDTH), jnp.bfloat16),
            pltpu.VMEM((EDGE, 128), jnp.int32),
            pltpu.VMEM((SHARE, EDGE), jnp.float32),
            pltpu.VMEM((SHARE, EDGE), jnp.float32),
            pltpu.VMEM((8, EDGE), jnp.int32),
            pltpu.VMEM((8, EDGE), jnp.float32),
            pltpu.VMEM((8, EDGE), jnp.float32),
            pltpu.VMEM((3, SHARE, 128), jnp.float32),
            pltpu.VMEM((3, SHARE, 128), jnp.float32),
            pltpu.VMEM((SIDE + 1, 8, SHARE), jnp.float32),
            pltpu.VMEM((9 * SHARE, 128), jnp.bfloat16),
        ],
        compiler_params=pltpu.CompilerParams(vmem_limit_bytes=28 * 1024 * 1024),
        cost_estimate=pl.CostEstimate(
            flops=2 * EDGE * EDGE * WIDTH, bytes_accessed=4 * EDGE * WIDTH, transcendentals=EDGE * EDGE
        ),
        name="pair_sums",
    )(place, *seq_blocks, struct_blocks)


def losses_kernel(place_ref, rows_ref, other_ref, cols_ref, self_ref, seq_ref, struct_ref, hard_ref):
    own, other = rows_ref[...], other_ref[...]
    lower, upper = (place_ref[0] == 0), (place_ref[0] == 1)
    for place, held in ((0, jnp.where(lower, own, other)), (1, jnp.where(upper, own, other))):
        for core in range(2):
            at = slice(place * 2 + core, place * 2 + core + 1)
            seq_ref[at, :] = jnp.log(held[core * 3 : core * 3 + 1]) - jnp.log(held[core * 3 + 1 : core * 3 + 2])
    cols = jnp.sum(cols_ref[...], axis=0)
    struct_ref[...] = jnp.log(cols[0:1]) - jnp.log(cols[1:2])
    extra = jnp.where(place_ref[1] == 0, own[2:3], own[5:6])
    self_logits = LOGIT_SCALE * self_ref[0:1]
    hard_ref[...] = jnp.log(jnp.exp(self_logits) + extra) - self_logits


def losses(place, rows, other_rows, cols, self_dot):
    return pl.pallas_call(
        losses_kernel,
        out_shape=(
            jax.ShapeDtypeStruct((4, SHARE), jnp.float32),
            jax.ShapeDtypeStruct((1, SHARE), jnp.float32),
            jax.ShapeDtypeStruct((1, SHARE), jnp.float32),
        ),
        in_specs=[SMEM, VMEM, VMEM, VMEM, VMEM],
        out_specs=(VMEM, VMEM, VMEM),
        compiler_params=pltpu.CompilerParams(vmem_limit_bytes=4 * 1024 * 1024),
        name="losses",
    )(place, rows, other_rows, cols, self_dot)


def over_z(block):
    found = {0: block, 1: shifted(block, "z", 1), 7: shifted(block, "z", -1)}
    found[2], found[6] = shifted(found[1], "z", 1), shifted(found[7], "z", -1)
    found[3], found[5] = shifted(found[2], "z", 1), shifted(found[6], "z", -1)
    found[4] = shifted(found[3], "z", 1)
    return [found[place] for place in range(8)]


def per_device(struct_feats, seq_feats, struct_proj, seq_proj, cluster_ids, hard_owner, hard_local, hard_valid):
    place = lambda axes: lax.axis_index(axes).astype(jnp.int32)
    core, yl = place("core"), place("yl")
    keep_s, send_s, keep_q, send_q = project(core.reshape(1), struct_feats, struct_proj, seq_feats.T, seq_proj)
    got_s = shifted(send_s, "core", 1)
    got_q = shifted(send_q, "core", 1)

    keep2_s, send2_s = merge(yl.reshape(1), keep_s, got_s, "merge_struct")
    got2_s = shifted(send2_s, "yl", 1)
    keep2_q, send2_q = merge(yl.reshape(1), keep_q, got_q, "merge_seq")
    got2_q = shifted(send2_q, "yl", 1)
    cluster_ids, hard_owner, hard_local, hard_valid, send2_q = lax.optimization_barrier(
        (cluster_ids, hard_owner, hard_local, hard_valid, send2_q)
    )
    own = lambda value: lax.dynamic_slice_in_dim(value, place(MP_AXES) * SHARE, SHARE, 0)
    labels = own(cluster_ids)
    owner = own(hard_owner[:, :, 0])
    local = own(hard_local)
    block = (owner >> 3) * 2 + ((local >> 7) & 1)
    chunk = (owner & 7) * 2 + (local >> 8)
    high = jnp.where(hard_valid > 0, block * 16 + chunk, -1).T
    low = (local & 127).T
    wide = lambda value: jnp.broadcast_to(value[None], (EXT, SHARE))
    seq_ext = jnp.concatenate([high, low, wide(labels >> 7), wide(labels & 127)], axis=1).astype(jnp.bfloat16)
    struct_ext = jnp.concatenate([wide(labels >> 7)[0:8], wide(labels & 127)[0:8]], axis=0).astype(jnp.bfloat16)

    struct_block, seq_block = finish(keep2_s, got2_s, keep2_q, got2_q, struct_ext, seq_ext)
    struct_peers = jnp.broadcast_to(struct_block[None], (SIDE, *struct_block.shape))
    struct_blocks = lax.all_to_all(struct_peers, COL_AXES, split_axis=0, concat_axis=0, tiled=True)
    seq_blocks = [each for held in over_z(seq_block) for each in (held, shifted(held, "core", 1))]

    rows, cols, self_dot = pair_sums(jnp.stack([place("z"), core, place(COL_AXES)]), seq_blocks, struct_blocks)
    rows = jnp.sum(lax.all_to_all(rows, "z", split_axis=0, concat_axis=0, tiled=True), axis=0)
    cols = lax.all_to_all(cols, COL_AXES, split_axis=0, concat_axis=0, tiled=True)
    rows = rows + shifted(rows, "core", 1)
    other_rows = shifted(rows, "yl", 1)
    seq_loss, struct_loss, hard_loss = losses(jnp.stack([yl, core]), rows, other_rows, cols, self_dot)
    return (seq_loss.reshape(4 * SHARE), struct_loss.reshape(SHARE), hard_loss.reshape(SHARE))


def solution(mesh):
    fine = Mesh(mesh.devices.reshape(8, 2, 4, 2, 2), ("z", "yh", "x", "yl", "core"))
    blk = ("z", "yh", "x")
    both = blk + MP_AXES
    placed = (
        P(blk, MP_AXES),
        P(blk, MP_AXES),
        P(MP_AXES, None),
        P(MP_AXES, None),
        P(blk),
        P(blk, None, None),
        P(blk, None),
        P(both, None),
    )
    return jax.shard_map(
        per_device,
        mesh=fine,
        in_specs=placed,
        out_specs=(P(blk), P(both), P(both)),
        check_vma=False,
    )
```

```python
import functools
import math

import jax
import jax.numpy as jnp
from jax import lax
from jax.experimental import pallas as pl
from jax.experimental.pallas import tpu as pltpu
from jax.sharding import Mesh, PartitionSpec as P

LOGIT_SCALE = 14.285714285714286
EPSILON = 1e-06
LOG2E = math.log2(math.e)

SHARE = 128
SIDE = 16
EDGE = SHARE * SIDE
WIDTH = 512
SLOTS = 16
EXT = 16
FIXED = 32000.0
SUB = 32

COL_AXES = ("yh", "x", "yl")
MP_AXES = ("yl", "core")
SIZES = {"z": 8, "yh": 2, "x": 4, "yl": 2, "core": 2}

VMEM = pl.BlockSpec(memory_space=pltpu.VMEM)
SMEM = pl.BlockSpec(memory_space=pltpu.SMEM)
HBM = pl.BlockSpec(memory_space=pltpu.HBM)


def shifted(value, axes, steps):
    names = (axes,) if isinstance(axes, str) else axes
    count = math.prod(SIZES[name] for name in names)
    return lax.ppermute(value, axes, [((place + steps) % count, place) for place in range(count)])


def project_kernel(core_ref, feats_hbm, proj_hbm, keep_ref, send_ref, feats_ref, proj_ref, sems, *, turned):
    core = core_ref[0]
    copies = [
        pltpu.make_async_copy(feats_hbm, feats_ref, sems.at[0]),
        pltpu.make_async_copy(proj_hbm, proj_ref, sems.at[1]),
    ]
    for copy in copies:
        copy.start()
    for copy in copies:
        copy.wait()
    for out, which in ((send_ref, 1 - core), (keep_ref, core)):
        for half in range(2):
            rows = pl.ds(pl.multiple_of((half * 2 + which) * SHARE, SHARE), SHARE)
            feats, over = (feats_ref[:, rows], 0) if turned else (feats_ref[rows, :], 1)
            out[half] = lax.dot_general(
                feats, proj_ref[...], (((over,), (0,)), ((), ())), preferred_element_type=jnp.float32
            )


def project(core, feats, proj, turned, name):
    shape = jax.ShapeDtypeStruct((2, SHARE, WIDTH), jnp.float32)
    return pl.pallas_call(
        functools.partial(project_kernel, turned=turned),
        out_shape=(shape, shape),
        in_specs=[SMEM, HBM, HBM],
        out_specs=(VMEM, VMEM),
        scratch_shapes=[
            pltpu.VMEM(feats.shape, feats.dtype),
            pltpu.VMEM(proj.shape, proj.dtype),
            pltpu.SemaphoreType.DMA((2,)),
        ],
        compiler_params=pltpu.CompilerParams(vmem_limit_bytes=12 * 1024 * 1024),
        name=name,
    )(core, feats, proj)


def merge_kernel(yl_ref, keep_ref, got_ref, keep2_ref, send2_ref):
    yl = yl_ref[0]
    send2_ref[...] = (keep_ref[1 - yl] + got_ref[1 - yl]).astype(jnp.bfloat16)
    keep2_ref[...] = keep_ref[yl] + got_ref[yl]


def merge(yl, keep, got, name):
    return pl.pallas_call(
        merge_kernel,
        out_shape=(
            jax.ShapeDtypeStruct((SHARE, WIDTH), jnp.float32),
            jax.ShapeDtypeStruct((SHARE, WIDTH), jnp.bfloat16),
        ),
        in_specs=[SMEM, VMEM, VMEM],
        out_specs=(VMEM, VMEM),
        compiler_params=pltpu.CompilerParams(vmem_limit_bytes=12 * 1024 * 1024),
        name=name,
    )(yl, keep, got)


def normalized(keep2_ref, got2_ref):
    raw = keep2_ref[...] + got2_ref[...].astype(jnp.float32)
    total = jnp.sum(raw * raw, axis=1, keepdims=True)
    return (raw * lax.rsqrt(total + EPSILON)).astype(jnp.bfloat16)


def finish_kernel(keep2_s, got2_s, keep2_q, got2_q, struct_ext_ref, seq_ext_ref, struct_ref, seq_ref):
    struct = normalized(keep2_s, got2_s)
    struct_ref[0:WIDTH, :] = struct.astype(jnp.float32).T.astype(jnp.bfloat16)
    struct_ref[WIDTH:, :] = struct_ext_ref[...]
    seq = normalized(keep2_q, got2_q)
    seq_ref[0:SHARE, :] = seq
    seq_ref[SHARE:, :] = seq_ext_ref[...]


def finish(*held):
    return pl.pallas_call(
        finish_kernel,
        out_shape=(
            jax.ShapeDtypeStruct((WIDTH + EXT, SHARE), jnp.bfloat16),
            jax.ShapeDtypeStruct((SHARE + EXT, WIDTH), jnp.bfloat16),
        ),
        in_specs=[VMEM] * 6,
        out_specs=(VMEM,) * 2,
        compiler_params=pltpu.CompilerParams(vmem_limit_bytes=12 * 1024 * 1024),
        name="finish",
    )(*held)


def integers(values):
    return values.astype(jnp.float32).astype(jnp.int32)


def pair_kernel(place_ref, *refs):
    seq_refs, s, rows_ref, cols_ref, self_ref = refs[0:SIDE], refs[SIDE], refs[SIDE + 1], refs[SIDE + 2], refs[SIDE + 3]
    q, info, buf0, buf1, lab8, ct, cm, held0, held1, row_sums, chosen = refs[SIDE + 4 :]
    my_z, my_core = place_ref[0], place_ref[1]
    my_block = my_z * 2 + my_core

    for block in range(SIDE):
        at = slice(block * SHARE, (block + 1) * SHARE)
        q[at, :] = seq_refs[block][0:SHARE, :]
        ext = integers(seq_refs[block][SHARE:, :])
        high, low = ext[:, 0:SHARE], ext[:, SHARE : 2 * SHARE]
        label = ext[:, 2 * SHARE : 3 * SHARE] * 128 + ext[:, 3 * SHARE :]
        code = jnp.where((high >> 4) == my_block, (high & 15) * 128 + low, -1)
        info[at, :] = jnp.full((SHARE, 128), -1, jnp.int32)
        info[at, 0 : 2 * EXT] = jnp.concatenate([code, -1 - label], axis=0).astype(jnp.float32).T.astype(jnp.int32)
    for chunk in range(SIDE):
        labels = integers(s[chunk, WIDTH:, :])
        lab8[:, chunk * 128 : (chunk + 1) * 128] = labels[0:8] * 128 + labels[8:16]
    ct[...] = jnp.zeros_like(ct)
    cm[...] = jnp.zeros_like(cm)
    row_of = lax.broadcasted_iota(jnp.int32, (8, SHARE), 0)
    held1[...] = jnp.zeros_like(held1)
    lane_of = lax.broadcasted_iota(jnp.int32, (3 * SHARE, 128), 1)
    for which in range(3):
        chosen[which * 3 * SHARE : (which + 1) * 3 * SHARE, :] = jnp.where(lane_of == which, 1.0, 0.0).astype(jnp.bfloat16)

    zero = jnp.zeros((8, 128), jnp.float32)
    groups = range(SUB // 8)

    def piece(tile, target, pair):
        cols = jnp.concatenate([s[2 * pair, 0:WIDTH, :], s[2 * pair + 1, 0:WIDTH, :]], axis=1)
        rows = pl.ds(pl.multiple_of(tile * SHARE, SHARE), SHARE)
        target[:, 2 * pair * SHARE : 2 * (pair + 1) * SHARE] = jnp.dot(
            q[rows, :], cols, preferred_element_type=jnp.float32
        )

    def gather_sums(slot, held):
        parts = []
        for which in range(3):
            rest = held[which]
            for _ in range(3):
                part = rest.astype(jnp.bfloat16)
                parts.append(part)
                rest = rest - part.astype(jnp.float32)
        summed = jnp.dot(jnp.concatenate(parts, axis=1), chosen[...], preferred_element_type=jnp.float32)
        row_sums[slot] = summed.T[0:8, :]

    def work(tile, products, next_tile, target, held, last_slot, last_held):
        for sub in range(SHARE // SUB):
            if sub == 1:
                gather_sums(last_slot, last_held)
            here = [pl.ds(pl.multiple_of(tile * SHARE + sub * SUB + group * 8, 8), 8) for group in groups]
            code = [info[rows, :] for rows in here]
            label = [jnp.broadcast_to(-1 - each[:, SLOTS : SLOTS + 1], (8, 128)) for each in code]
            lane = [each & 127 for each in code]
            pair_of = [each >> 8 for each in code]
            row_total, row_matched = [zero for _ in groups], [zero for _ in groups]
            picked = [jnp.zeros((8, 128), jnp.int32) for _ in groups]
            even = [None for _ in groups]
            for chunk in range(SIDE):
                if chunk % 8 == 0:
                    piece(next_tile, target, sub * 2 + chunk // 8)
                at = slice(chunk * 128, (chunk + 1) * 128)
                col_label = lab8[:, at]
                col_total, col_matched = ct[:, at], cm[:, at]
                for group in groups:
                    local = sub * SUB + group * 8
                    product = products[local : local + 8, at]
                    expo = jnp.exp2(product * (LOGIT_SCALE * LOG2E))
                    fixed = (product * FIXED).astype(jnp.int32)
                    kept = jnp.where(label[group] == col_label, expo, 0.0)
                    row_total[group] += expo
                    row_matched[group] += kept
                    col_total += expo
                    col_matched += kept
                    if chunk % 2 == 0:
                        even[group] = fixed
                    else:
                        both = (even[group] << 16) + fixed
                        found = jnp.take_along_axis(both, lane[group], axis=1, mode="promise_in_bounds")
                        picked[group] = jnp.where(pair_of[group] == chunk // 2, found, picked[group])
                ct[:, at] = col_total
                cm[:, at] = col_matched
            for group in groups:
                local = slice(sub * SUB + group * 8, sub * SUB + group * 8 + 8)
                held[0, local, :] = row_total[group]
                held[1, local, :] = row_matched[group]
                odd = (picked[group] << 16) >> 16
                fixed = jnp.where((code[group] & 128) > 0, odd, (picked[group] - odd) >> 16).astype(jnp.float32)
                fixed = fixed + jnp.where(fixed > 0, 0.5, jnp.where(fixed < 0, -0.5, 0.0))
                hard = jnp.exp(fixed * (LOGIT_SCALE / FIXED))
                held[2, local, :] = jnp.where(code[group] >= 0, hard, 0.0)

    for pair in range(SIDE // 2):
        piece(0, buf0, pair)

    def body(step, carry):
        work(2 * step, buf0, 2 * step + 1, buf1, held0, jnp.where(step == 0, SIDE, 2 * step - 1), held1)
        work(2 * step + 1, buf1, jnp.minimum(2 * step + 2, SIDE - 1), buf0, held1, 2 * step, held0)
        return carry

    lax.fori_loop(0, SIDE // 2, body, 0)
    gather_sums(SIDE - 1, held1)
    for far in range(8):
        out = jnp.zeros((8, SHARE), jnp.float32)
        for mate in range(2):
            first = (my_core ^ mate) * 3
            for which in range(3):
                out = jnp.where(row_of == first + which, row_sums[far * 2 + mate][which : which + 1], out)
        rows_ref[(my_z + far) & 7] = out
    own = jnp.dot(q[0:SHARE, :], s[place_ref[2], 0:WIDTH, :], preferred_element_type=jnp.float32)
    diagonal = lax.broadcasted_iota(jnp.int32, own.shape, 0) == lax.broadcasted_iota(jnp.int32, own.shape, 1)
    self_ref[...] = jnp.broadcast_to(jnp.sum(jnp.where(diagonal, own, 0.0), axis=0, keepdims=True), (8, SHARE))

    for chunk in range(SIDE):
        at = slice(chunk * 128, (chunk + 1) * 128)
        total = jnp.sum(ct[:, at], axis=0, keepdims=True)
        matched = jnp.sum(cm[:, at], axis=0, keepdims=True)
        cols_ref[chunk] = jnp.where(row_of == 0, total, matched)


def pair_sums(place, seq_blocks, struct_blocks):
    return pl.pallas_call(
        pair_kernel,
        out_shape=(
            jax.ShapeDtypeStruct((8, 8, SHARE), jnp.float32),
            jax.ShapeDtypeStruct((SIDE, 8, SHARE), jnp.float32),
            jax.ShapeDtypeStruct((8, SHARE), jnp.float32),
        ),
        in_specs=[SMEM] + [VMEM] * (SIDE + 1),
        out_specs=(VMEM, VMEM, VMEM),
        scratch_shapes=[
            pltpu.VMEM((EDGE, WIDTH), jnp.bfloat16),
            pltpu.VMEM((EDGE, 128), jnp.int32),
            pltpu.VMEM((SHARE, EDGE), jnp.float32),
            pltpu.VMEM((SHARE, EDGE), jnp.float32),
            pltpu.VMEM((8, EDGE), jnp.int32),
            pltpu.VMEM((8, EDGE), jnp.float32),
            pltpu.VMEM((8, EDGE), jnp.float32),
            pltpu.VMEM((3, SHARE, 128), jnp.float32),
            pltpu.VMEM((3, SHARE, 128), jnp.float32),
            pltpu.VMEM((SIDE + 1, 8, SHARE), jnp.float32),
            pltpu.VMEM((9 * SHARE, 128), jnp.bfloat16),
        ],
        compiler_params=pltpu.CompilerParams(vmem_limit_bytes=28 * 1024 * 1024),
        cost_estimate=pl.CostEstimate(
            flops=2 * EDGE * EDGE * WIDTH, bytes_accessed=4 * EDGE * WIDTH, transcendentals=EDGE * EDGE
        ),
        name="pair_sums",
    )(place, *seq_blocks, struct_blocks)


def losses_kernel(place_ref, rows_ref, other_ref, cols_ref, self_ref, seq_ref, struct_ref, hard_ref):
    own, other = rows_ref[...], other_ref[...]
    lower, upper = (place_ref[0] == 0), (place_ref[0] == 1)
    for place, held in ((0, jnp.where(lower, own, other)), (1, jnp.where(upper, own, other))):
        for core in range(2):
            at = slice(place * 2 + core, place * 2 + core + 1)
            seq_ref[at, :] = jnp.log(held[core * 3 : core * 3 + 1]) - jnp.log(held[core * 3 + 1 : core * 3 + 2])
    cols = jnp.sum(cols_ref[...], axis=0)
    struct_ref[...] = jnp.log(cols[0:1]) - jnp.log(cols[1:2])
    extra = jnp.where(place_ref[1] == 0, own[2:3], own[5:6])
    self_logits = LOGIT_SCALE * self_ref[0:1]
    hard_ref[...] = jnp.log(jnp.exp(self_logits) + extra) - self_logits


def losses(place, rows, other_rows, cols, self_dot):
    return pl.pallas_call(
        losses_kernel,
        out_shape=(
            jax.ShapeDtypeStruct((4, SHARE), jnp.float32),
            jax.ShapeDtypeStruct((1, SHARE), jnp.float32),
            jax.ShapeDtypeStruct((1, SHARE), jnp.float32),
        ),
        in_specs=[SMEM, VMEM, VMEM, VMEM, VMEM],
        out_specs=(VMEM, VMEM, VMEM),
        compiler_params=pltpu.CompilerParams(vmem_limit_bytes=4 * 1024 * 1024),
        name="losses",
    )(place, rows, other_rows, cols, self_dot)


def over_z(block):
    found = {0: block, 1: shifted(block, "z", 1), 7: shifted(block, "z", -1)}
    found[2], found[6] = shifted(found[1], "z", 1), shifted(found[7], "z", -1)
    found[3], found[5] = shifted(found[2], "z", 1), shifted(found[6], "z", -1)
    found[4] = shifted(found[3], "z", 1)
    return [found[place] for place in range(8)]


def per_device(struct_feats, seq_feats, struct_proj, seq_proj, cluster_ids, hard_owner, hard_local, hard_valid):
    place = lambda axes: lax.axis_index(axes).astype(jnp.int32)
    core, yl = place("core"), place("yl")
    keep_s, send_s = project(core.reshape(1), struct_feats, struct_proj, False, "project_struct")
    got_s = shifted(send_s, "core", 1)
    keep_q, send_q = project(core.reshape(1), seq_feats.T, seq_proj, True, "project_seq")
    got_q = shifted(send_q, "core", 1)

    keep2_s, send2_s = merge(yl.reshape(1), keep_s, got_s, "merge_struct")
    got2_s = shifted(send2_s, "yl", 1)
    keep2_q, send2_q = merge(yl.reshape(1), keep_q, got_q, "merge_seq")
    got2_q = shifted(send2_q, "yl", 1)
    cluster_ids, hard_owner, hard_local, hard_valid, send2_s, send2_q = lax.optimization_barrier(
        (cluster_ids, hard_owner, hard_local, hard_valid, send2_s, send2_q)
    )
    own = lambda value: lax.dynamic_slice_in_dim(value, place(MP_AXES) * SHARE, SHARE, 0)
    labels = own(cluster_ids)
    owner = own(hard_owner[:, :, 0])
    local = own(hard_local)
    block = (owner >> 3) * 2 + ((local >> 7) & 1)
    chunk = (owner & 7) * 2 + (local >> 8)
    high = jnp.where(hard_valid > 0, block * 16 + chunk, -1).T
    low = (local & 127).T
    wide = lambda value: jnp.broadcast_to(value[None], (EXT, SHARE))
    seq_ext = jnp.concatenate([high, low, wide(labels >> 7), wide(labels & 127)], axis=1).astype(jnp.bfloat16)
    struct_ext = jnp.concatenate([wide(labels >> 7)[0:8], wide(labels & 127)[0:8]], axis=0).astype(jnp.bfloat16)

    struct_block, seq_block = finish(keep2_s, got2_s, keep2_q, got2_q, struct_ext, seq_ext)
    struct_peers = jnp.broadcast_to(struct_block[None], (SIDE, *struct_block.shape))
    struct_blocks = lax.all_to_all(struct_peers, COL_AXES, split_axis=0, concat_axis=0, tiled=True)
    seq_blocks = [each for held in over_z(seq_block) for each in (held, shifted(held, "core", 1))]

    rows, cols, self_dot = pair_sums(jnp.stack([place("z"), core, place(COL_AXES)]), seq_blocks, struct_blocks)
    rows = jnp.sum(lax.all_to_all(rows, "z", split_axis=0, concat_axis=0, tiled=True), axis=0)
    cols = lax.all_to_all(cols, COL_AXES, split_axis=0, concat_axis=0, tiled=True)
    rows = rows + shifted(rows, "core", 1)
    other_rows = shifted(rows, "yl", 1)
    seq_loss, struct_loss, hard_loss = losses(jnp.stack([yl, core]), rows, other_rows, cols, self_dot)
    return (seq_loss.reshape(4 * SHARE), struct_loss.reshape(SHARE), hard_loss.reshape(SHARE))


def solution(mesh):
    fine = Mesh(mesh.devices.reshape(8, 2, 4, 2, 2), ("z", "yh", "x", "yl", "core"))
    blk = ("z", "yh", "x")
    both = blk + MP_AXES
    placed = (
        P(blk, MP_AXES),
        P(blk, MP_AXES),
        P(MP_AXES, None),
        P(MP_AXES, None),
        P(blk),
        P(blk, None, None),
        P(blk, None),
        P(both, None),
    )
    return jax.shard_map(
        per_device,
        mesh=fine,
        in_specs=placed,
        out_specs=(P(blk), P(both), P(both)),
        check_vma=False,
    )
```

```python
import functools
import math

import jax
import jax.numpy as jnp
from jax import lax
from jax.experimental import pallas as pl
from jax.experimental.pallas import tpu as pltpu
from jax.sharding import Mesh, PartitionSpec as P

LOGIT_SCALE = 14.285714285714286
EPSILON = 1e-06
LOG2E = math.log2(math.e)

SHARE = 128
SIDE = 16
EDGE = SHARE * SIDE
WIDTH = 512
SLOTS = 16
EXT = 16
FIXED = 32000.0
SUB = 32

COL_AXES = ("yh", "x", "yl")
MP_AXES = ("yl", "core")
SIZES = {"z": 8, "yh": 2, "x": 4, "yl": 2, "core": 2}

VMEM = pl.BlockSpec(memory_space=pltpu.VMEM)
SMEM = pl.BlockSpec(memory_space=pltpu.SMEM)
HBM = pl.BlockSpec(memory_space=pltpu.HBM)


def shifted(value, axes, steps):
    names = (axes,) if isinstance(axes, str) else axes
    count = math.prod(SIZES[name] for name in names)
    return lax.ppermute(value, axes, [((place + steps) % count, place) for place in range(count)])


def project_kernel(core_ref, feats_hbm, proj_hbm, keep_ref, send_ref, feats_ref, proj_ref, sems, *, turned):
    core = core_ref[0]
    copies = [
        pltpu.make_async_copy(feats_hbm, feats_ref, sems.at[0]),
        pltpu.make_async_copy(proj_hbm, proj_ref, sems.at[1]),
    ]
    for copy in copies:
        copy.start()
    for copy in copies:
        copy.wait()
    for out, which in ((send_ref, 1 - core), (keep_ref, core)):
        for half in range(2):
            rows = pl.ds(pl.multiple_of((half * 2 + which) * SHARE, SHARE), SHARE)
            feats, over = (feats_ref[:, rows], 0) if turned else (feats_ref[rows, :], 1)
            out[half] = lax.dot_general(
                feats, proj_ref[...], (((over,), (0,)), ((), ())), preferred_element_type=jnp.float32
            )


def project(core, feats, proj, turned, name):
    shape = jax.ShapeDtypeStruct((2, SHARE, WIDTH), jnp.float32)
    return pl.pallas_call(
        functools.partial(project_kernel, turned=turned),
        out_shape=(shape, shape),
        in_specs=[SMEM, HBM, HBM],
        out_specs=(VMEM, VMEM),
        scratch_shapes=[
            pltpu.VMEM(feats.shape, feats.dtype),
            pltpu.VMEM(proj.shape, proj.dtype),
            pltpu.SemaphoreType.DMA((2,)),
        ],
        compiler_params=pltpu.CompilerParams(vmem_limit_bytes=12 * 1024 * 1024),
        name=name,
    )(core, feats, proj)


def merge_kernel(yl_ref, keep_ref, got_ref, keep2_ref, send2_ref):
    yl = yl_ref[0]
    send2_ref[...] = (keep_ref[1 - yl] + got_ref[1 - yl]).astype(jnp.bfloat16)
    keep2_ref[...] = keep_ref[yl] + got_ref[yl]


def merge(yl, keep, got, name):
    return pl.pallas_call(
        merge_kernel,
        out_shape=(
            jax.ShapeDtypeStruct((SHARE, WIDTH), jnp.float32),
            jax.ShapeDtypeStruct((SHARE, WIDTH), jnp.bfloat16),
        ),
        in_specs=[SMEM, VMEM, VMEM],
        out_specs=(VMEM, VMEM),
        compiler_params=pltpu.CompilerParams(vmem_limit_bytes=12 * 1024 * 1024),
        name=name,
    )(yl, keep, got)


def normalized(keep2_ref, got2_ref):
    raw = keep2_ref[...] + got2_ref[...].astype(jnp.float32)
    total = jnp.sum(raw * raw, axis=1, keepdims=True)
    return (raw * lax.rsqrt(total + EPSILON)).astype(jnp.bfloat16)


def finish_kernel(keep2_s, got2_s, keep2_q, got2_q, struct_ext_ref, seq_ext_ref, struct_ref, seq_ref):
    struct = normalized(keep2_s, got2_s)
    turned = struct.astype(jnp.float32).T.astype(jnp.bfloat16)
    for peer in range(SIDE):
        struct_ref[peer, 0:WIDTH, :] = turned
        struct_ref[peer, WIDTH:, :] = struct_ext_ref[...]
    seq = normalized(keep2_q, got2_q)
    seq_ref[0:SHARE, :] = seq
    seq_ref[SHARE:, :] = seq_ext_ref[...]


def finish(*held):
    return pl.pallas_call(
        finish_kernel,
        out_shape=(
            jax.ShapeDtypeStruct((SIDE, WIDTH + EXT, SHARE), jnp.bfloat16),
            jax.ShapeDtypeStruct((SHARE + EXT, WIDTH), jnp.bfloat16),
        ),
        in_specs=[VMEM] * 6,
        out_specs=(VMEM,) * 2,
        compiler_params=pltpu.CompilerParams(vmem_limit_bytes=12 * 1024 * 1024),
        name="finish",
    )(*held)


def integers(values):
    return values.astype(jnp.float32).astype(jnp.int32)


def pair_kernel(place_ref, *refs):
    seq_refs, s, rows_ref, cols_ref, self_ref = refs[0:SIDE], refs[SIDE], refs[SIDE + 1], refs[SIDE + 2], refs[SIDE + 3]
    q, info, buf0, buf1, lab8, ct, cm, held0, held1, row_sums, chosen = refs[SIDE + 4 :]
    my_z, my_core = place_ref[0], place_ref[1]
    my_block = my_z * 2 + my_core

    for block in range(SIDE):
        at = slice(block * SHARE, (block + 1) * SHARE)
        q[at, :] = seq_refs[block][0:SHARE, :]
        ext = integers(seq_refs[block][SHARE:, :])
        high, low = ext[:, 0:SHARE], ext[:, SHARE : 2 * SHARE]
        label = ext[:, 2 * SHARE : 3 * SHARE] * 128 + ext[:, 3 * SHARE :]
        code = jnp.where((high >> 4) == my_block, (high & 15) * 128 + low, -1)
        info[at, :] = jnp.full((SHARE, 128), -1, jnp.int32)
        info[at, 0 : 2 * EXT] = jnp.concatenate([code, -1 - label], axis=0).astype(jnp.float32).T.astype(jnp.int32)
    for chunk in range(SIDE):
        labels = integers(s[chunk, WIDTH:, :])
        lab8[:, chunk * 128 : (chunk + 1) * 128] = labels[0:8] * 128 + labels[8:16]
    ct[...] = jnp.zeros_like(ct)
    cm[...] = jnp.zeros_like(cm)
    row_of = lax.broadcasted_iota(jnp.int32, (8, SHARE), 0)
    held1[...] = jnp.zeros_like(held1)
    lane_of = lax.broadcasted_iota(jnp.int32, (3 * SHARE, 128), 1)
    for which in range(3):
        chosen[which * 3 * SHARE : (which + 1) * 3 * SHARE, :] = jnp.where(lane_of == which, 1.0, 0.0).astype(jnp.bfloat16)

    zero = jnp.zeros((8, 128), jnp.float32)
    groups = range(SUB // 8)

    def piece(tile, target, pair):
        cols = jnp.concatenate([s[2 * pair, 0:WIDTH, :], s[2 * pair + 1, 0:WIDTH, :]], axis=1)
        rows = pl.ds(pl.multiple_of(tile * SHARE, SHARE), SHARE)
        target[:, 2 * pair * SHARE : 2 * (pair + 1) * SHARE] = jnp.dot(
            q[rows, :], cols, preferred_element_type=jnp.float32
        )

    def gather_sums(slot, held):
        parts = []
        for which in range(3):
            rest = held[which]
            for _ in range(3):
                part = rest.astype(jnp.bfloat16)
                parts.append(part)
                rest = rest - part.astype(jnp.float32)
        summed = jnp.dot(jnp.concatenate(parts, axis=1), chosen[...], preferred_element_type=jnp.float32)
        row_sums[slot] = summed.T[0:8, :]

    def work(tile, products, next_tile, target, held, last_slot, last_held):
        for sub in range(SHARE // SUB):
            if sub == 1:
                gather_sums(last_slot, last_held)
            here = [pl.ds(pl.multiple_of(tile * SHARE + sub * SUB + group * 8, 8), 8) for group in groups]
            code = [info[rows, :] for rows in here]
            label = [jnp.broadcast_to(-1 - each[:, SLOTS : SLOTS + 1], (8, 128)) for each in code]
            lane = [each & 127 for each in code]
            pair_of = [each >> 8 for each in code]
            row_total, row_matched = [zero for _ in groups], [zero for _ in groups]
            picked = [jnp.zeros((8, 128), jnp.int32) for _ in groups]
            even = [None for _ in groups]
            for chunk in range(SIDE):
                if chunk % 8 == 0:
                    piece(next_tile, target, sub * 2 + chunk // 8)
                at = slice(chunk * 128, (chunk + 1) * 128)
                col_label = lab8[:, at]
                col_total, col_matched = ct[:, at], cm[:, at]
                for group in groups:
                    local = sub * SUB + group * 8
                    product = products[local : local + 8, at]
                    expo = jnp.exp2(product * (LOGIT_SCALE * LOG2E))
                    fixed = (product * FIXED).astype(jnp.int32)
                    kept = jnp.where(label[group] == col_label, expo, 0.0)
                    row_total[group] += expo
                    row_matched[group] += kept
                    col_total += expo
                    col_matched += kept
                    if chunk % 2 == 0:
                        even[group] = fixed
                    else:
                        both = (even[group] << 16) + fixed
                        found = jnp.take_along_axis(both, lane[group], axis=1, mode="promise_in_bounds")
                        picked[group] = jnp.where(pair_of[group] == chunk // 2, found, picked[group])
                ct[:, at] = col_total
                cm[:, at] = col_matched
            for group in groups:
                local = slice(sub * SUB + group * 8, sub * SUB + group * 8 + 8)
                held[0, local, :] = row_total[group]
                held[1, local, :] = row_matched[group]
                odd = (picked[group] << 16) >> 16
                fixed = jnp.where((code[group] & 128) > 0, odd, (picked[group] - odd) >> 16).astype(jnp.float32)
                fixed = fixed + jnp.where(fixed > 0, 0.5, jnp.where(fixed < 0, -0.5, 0.0))
                hard = jnp.exp(fixed * (LOGIT_SCALE / FIXED))
                held[2, local, :] = jnp.where(code[group] >= 0, hard, 0.0)

    for pair in range(SIDE // 2):
        piece(0, buf0, pair)

    def body(step, carry):
        work(2 * step, buf0, 2 * step + 1, buf1, held0, jnp.where(step == 0, SIDE, 2 * step - 1), held1)
        work(2 * step + 1, buf1, jnp.minimum(2 * step + 2, SIDE - 1), buf0, held1, 2 * step, held0)
        return carry

    lax.fori_loop(0, SIDE // 2, body, 0)
    gather_sums(SIDE - 1, held1)
    for far in range(8):
        out = jnp.zeros((8, SHARE), jnp.float32)
        for mate in range(2):
            first = (my_core ^ mate) * 3
            for which in range(3):
                out = jnp.where(row_of == first + which, row_sums[far * 2 + mate][which : which + 1], out)
        rows_ref[(my_z + far) & 7] = out
    own = jnp.dot(q[0:SHARE, :], s[place_ref[2], 0:WIDTH, :], preferred_element_type=jnp.float32)
    diagonal = lax.broadcasted_iota(jnp.int32, own.shape, 0) == lax.broadcasted_iota(jnp.int32, own.shape, 1)
    self_ref[...] = jnp.broadcast_to(jnp.sum(jnp.where(diagonal, own, 0.0), axis=0, keepdims=True), (8, SHARE))

    for chunk in range(SIDE):
        at = slice(chunk * 128, (chunk + 1) * 128)
        total = jnp.sum(ct[:, at], axis=0, keepdims=True)
        matched = jnp.sum(cm[:, at], axis=0, keepdims=True)
        cols_ref[chunk] = jnp.where(row_of == 0, total, matched)


def pair_sums(place, seq_blocks, struct_blocks):
    return pl.pallas_call(
        pair_kernel,
        out_shape=(
            jax.ShapeDtypeStruct((8, 8, SHARE), jnp.float32),
            jax.ShapeDtypeStruct((SIDE, 8, SHARE), jnp.float32),
            jax.ShapeDtypeStruct((8, SHARE), jnp.float32),
        ),
        in_specs=[SMEM] + [VMEM] * (SIDE + 1),
        out_specs=(VMEM, VMEM, VMEM),
        scratch_shapes=[
            pltpu.VMEM((EDGE, WIDTH), jnp.bfloat16),
            pltpu.VMEM((EDGE, 128), jnp.int32),
            pltpu.VMEM((SHARE, EDGE), jnp.float32),
            pltpu.VMEM((SHARE, EDGE), jnp.float32),
            pltpu.VMEM((8, EDGE), jnp.int32),
            pltpu.VMEM((8, EDGE), jnp.float32),
            pltpu.VMEM((8, EDGE), jnp.float32),
            pltpu.VMEM((3, SHARE, 128), jnp.float32),
            pltpu.VMEM((3, SHARE, 128), jnp.float32),
            pltpu.VMEM((SIDE + 1, 8, SHARE), jnp.float32),
            pltpu.VMEM((9 * SHARE, 128), jnp.bfloat16),
        ],
        compiler_params=pltpu.CompilerParams(vmem_limit_bytes=28 * 1024 * 1024),
        cost_estimate=pl.CostEstimate(
            flops=2 * EDGE * EDGE * WIDTH, bytes_accessed=4 * EDGE * WIDTH, transcendentals=EDGE * EDGE
        ),
        name="pair_sums",
    )(place, *seq_blocks, struct_blocks)


def losses_kernel(place_ref, rows_ref, other_ref, cols_ref, self_ref, seq_ref, struct_ref, hard_ref):
    own, other = rows_ref[...], other_ref[...]
    lower, upper = (place_ref[0] == 0), (place_ref[0] == 1)
    for place, held in ((0, jnp.where(lower, own, other)), (1, jnp.where(upper, own, other))):
        for core in range(2):
            at = slice(place * 2 + core, place * 2 + core + 1)
            seq_ref[at, :] = jnp.log(held[core * 3 : core * 3 + 1]) - jnp.log(held[core * 3 + 1 : core * 3 + 2])
    cols = jnp.sum(cols_ref[...], axis=0)
    struct_ref[...] = jnp.log(cols[0:1]) - jnp.log(cols[1:2])
    extra = jnp.where(place_ref[1] == 0, own[2:3], own[5:6])
    self_logits = LOGIT_SCALE * self_ref[0:1]
    hard_ref[...] = jnp.log(jnp.exp(self_logits) + extra) - self_logits


def losses(place, rows, other_rows, cols, self_dot):
    return pl.pallas_call(
        losses_kernel,
        out_shape=(
            jax.ShapeDtypeStruct((4, SHARE), jnp.float32),
            jax.ShapeDtypeStruct((1, SHARE), jnp.float32),
            jax.ShapeDtypeStruct((1, SHARE), jnp.float32),
        ),
        in_specs=[SMEM, VMEM, VMEM, VMEM, VMEM],
        out_specs=(VMEM, VMEM, VMEM),
        compiler_params=pltpu.CompilerParams(vmem_limit_bytes=4 * 1024 * 1024),
        name="losses",
    )(place, rows, other_rows, cols, self_dot)


def over_z(block):
    found = {0: block, 1: shifted(block, "z", 1), 7: shifted(block, "z", -1)}
    found[2], found[6] = shifted(found[1], "z", 1), shifted(found[7], "z", -1)
    found[3], found[5] = shifted(found[2], "z", 1), shifted(found[6], "z", -1)
    found[4] = shifted(found[3], "z", 1)
    return [found[place] for place in range(8)]


def per_device(struct_feats, seq_feats, struct_proj, seq_proj, cluster_ids, hard_owner, hard_local, hard_valid):
    place = lambda axes: lax.axis_index(axes).astype(jnp.int32)
    core, yl = place("core"), place("yl")
    keep_s, send_s = project(core.reshape(1), struct_feats, struct_proj, False, "project_struct")
    got_s = shifted(send_s, "core", 1)
    keep_q, send_q = project(core.reshape(1), seq_feats.T, seq_proj, True, "project_seq")
    got_q = shifted(send_q, "core", 1)

    keep2_s, send2_s = merge(yl.reshape(1), keep_s, got_s, "merge_struct")
    got2_s = shifted(send2_s, "yl", 1)
    keep2_q, send2_q = merge(yl.reshape(1), keep_q, got_q, "merge_seq")
    got2_q = shifted(send2_q, "yl", 1)
    cluster_ids, hard_owner, hard_local, hard_valid, send2_s, send2_q = lax.optimization_barrier(
        (cluster_ids, hard_owner, hard_local, hard_valid, send2_s, send2_q)
    )
    own = lambda value: lax.dynamic_slice_in_dim(value, place(MP_AXES) * SHARE, SHARE, 0)
    labels = own(cluster_ids)
    owner = own(hard_owner[:, :, 0])
    local = own(hard_local)
    block = (owner >> 3) * 2 + ((local >> 7) & 1)
    chunk = (owner & 7) * 2 + (local >> 8)
    high = jnp.where(hard_valid > 0, block * 16 + chunk, -1).T
    low = (local & 127).T
    wide = lambda value: jnp.broadcast_to(value[None], (EXT, SHARE))
    seq_ext = jnp.concatenate([high, low, wide(labels >> 7), wide(labels & 127)], axis=1).astype(jnp.bfloat16)
    struct_ext = jnp.concatenate([wide(labels >> 7)[0:8], wide(labels & 127)[0:8]], axis=0).astype(jnp.bfloat16)

    struct_block, seq_block = finish(keep2_s, got2_s, keep2_q, got2_q, struct_ext, seq_ext)
    struct_blocks = lax.all_to_all(struct_block, COL_AXES, split_axis=0, concat_axis=0, tiled=True)
    seq_blocks = [each for held in over_z(seq_block) for each in (held, shifted(held, "core", 1))]

    rows, cols, self_dot = pair_sums(jnp.stack([place("z"), core, place(COL_AXES)]), seq_blocks, struct_blocks)
    rows = jnp.sum(lax.all_to_all(rows, "z", split_axis=0, concat_axis=0, tiled=True), axis=0)
    cols = lax.all_to_all(cols, COL_AXES, split_axis=0, concat_axis=0, tiled=True)
    rows = rows + shifted(rows, "core", 1)
    other_rows = shifted(rows, "yl", 1)
    seq_loss, struct_loss, hard_loss = losses(jnp.stack([yl, core]), rows, other_rows, cols, self_dot)
    return (seq_loss.reshape(4 * SHARE), struct_loss.reshape(SHARE), hard_loss.reshape(SHARE))


def solution(mesh):
    fine = Mesh(mesh.devices.reshape(8, 2, 4, 2, 2), ("z", "yh", "x", "yl", "core"))
    blk = ("z", "yh", "x")
    both = blk + MP_AXES
    placed = (
        P(blk, MP_AXES),
        P(blk, MP_AXES),
        P(MP_AXES, None),
        P(MP_AXES, None),
        P(blk),
        P(blk, None, None),
        P(blk, None),
        P(both, None),
    )
    return jax.shard_map(
        per_device,
        mesh=fine,
        in_specs=placed,
        out_specs=(P(blk), P(both), P(both)),
        check_vma=False,
    )
```
